256 devices in a mesh: dp: 64 (over y, z, core), mix: 4 (over x).
Axes of the slice: x: 4, y: 4, z: 8, core: 2. Of those that a mesh axis runs over, the one named last changes fastest.
Arguments:
- images: bfloat16 [512, 196, 768], P('dp', 'mix'), may hold values from -6 to 6
- cotangent: bfloat16 [512, 196, 768], P('dp', 'mix'), may hold values from -6 to 6
- image_counts: int32 [64], P('dp'), may hold values from 2 to 8, as said below
- w_tok_in: float32 [196, 384], P(None, 'dp'), may hold values from -0.4375 to 0.4375
- w_tok_out: float32 [384, 196], P('dp'), may hold values from -0.3125 to 0.3125
- w_up: float32 [768, 3072], P(None, ('dp', 'mix')), may hold values from -0.21875 to 0.21875
- w_down: float32 [3072, 768], P(('dp', 'mix')), may hold values from -0.109375 to 0.109375
- norm_params: float32 [4, 768], replicated
- biases: float32 [4420], replicated, may hold values from -3 to 3
- left_tok_in: float32 [196, 196], replicated
- right_tok_in: float32 [384, 384], replicated
- left_tok_out: float32 [384, 384], replicated
- right_tok_out: float32 [196, 196], replicated
- left_up: float32 [768, 768], P('dp', 'mix')
- right_up: float32 [3072, 3072], P(None, ('dp', 'mix'))
- left_down: float32 [3072, 3072], P(('dp', 'mix'))
- right_down: float32 [768, 768], P('dp', 'mix')
- root_left_tok_in: float32 [196, 196], replicated
- root_right_tok_in: float32 [384, 384], replicated
- root_left_tok_out: float32 [384, 384], replicated
- root_right_tok_out: float32 [196, 196], replicated
- root_left_up: float32 [768, 768], replicated
- root_right_up: float32 [3072, 3072], P(None, ('dp', 'mix'))
- root_left_down: float32 [3072, 3072], P(('dp', 'mix'))
- root_right_down: float32 [768, 768], replicated
- norm_second: float32 [4, 768], replicated
- bias_second: float32 [4420], replicated
Outputs:
- layer_output: bfloat16 [512, 196, 768], P('dp', 'mix')
- grad_images: float32 [512, 196, 768], P('dp', 'mix')
- grad_tok_in: float32 [196, 384], P(None, 'dp')
- grad_tok_out: float32 [384, 196], P('dp')
- grad_up: float32 [768, 3072], P(None, ('dp', 'mix'))
- grad_down: float32 [3072, 768], P(('dp', 'mix'))
- new_tok_in: float32 [196, 384], P(None, 'dp')
- new_tok_out: float32 [384, 196], P('dp')
- new_up: float32 [768, 3072], P(None, ('dp', 'mix'))
- new_down: float32 [3072, 768], P(('dp', 'mix'))
- new_left_tok_in: float32 [196, 196], replicated
- new_right_tok_in: float32 [384, 384], replicated
- new_left_tok_out: float32 [384, 384], replicated
- new_right_tok_out: float32 [196, 196], replicated
- new_left_up: float32 [768, 768], P('dp', 'mix')
- new_right_up: float32 [3072, 3072], P(None, ('dp', 'mix'))
- new_left_down: float32 [3072, 3072], P(('dp', 'mix'))
- new_right_down: float32 [768, 768], P('dp', 'mix')
- norm_grad: float32 [4, 768], replicated
- norm_second_new: float32 [4, 768], replicated
- norm_new: float32 [4, 768], replicated
- bias_grad: float32 [4420], replicated
- bias_second_new: float32 [4420], replicated
- bias_new: float32 [4420], replicated
The draws below stay inside these ranges and needn't reach their ends.
Inputs may be any that keep to these rules, and one draw needn't show every extreme that they name: Each index of dp holds 8 image slots; the first image_counts of them hold images and the others are padding. Some index is full in every draw.
All inputs are finite; a program needn't handle non-finite values.
Results may differ from the reference program's by a relative error of at most 0.011.
Values may be sent and summed in bfloat16 or wider, within the bound.
A program may use at most 192 MiB of HBM per device.

```python
import math
import jax
import jax.numpy as jnp
from jax import lax

D = 768
DC = 3072
DS = 384
S = 196
IMG_DEV = 8
IMAGES = 512
NB = 4420
N_DP = 64


def channel_factor():
    return math.sqrt(0.6 * S / IMAGES)


def mixing_factor():
    return math.sqrt(0.6 * D / IMAGES)


def size_tok_in():
    return 0.73 * math.sqrt(S / DS) * mixing_factor()


def size_tok_out():
    return 0.72 * mixing_factor()


def size_up():
    return 0.66 * math.sqrt(D / DC) * channel_factor()


def size_down():
    return 0.65 * channel_factor()


def statistics(key, rows_count, inner, grad_size, power, spread):
    first_key, second_key = jax.random.split(key)
    uniform_part = jax.random.uniform(first_key, (rows_count,), jnp.float32)
    factor = 4.0 ** uniform_part ** power
    diag_size = inner * grad_size * grad_size
    off_diag = jax.random.normal(second_key, (rows_count, rows_count), jnp.float32) * (spread * math.sqrt(inner) * grad_size * grad_size)
    off_diag = (off_diag + off_diag.T) * 0.5
    identity = jnp.eye(rows_count, dtype=jnp.float32)
    return off_diag * (1.0 - identity) + identity * (diag_size * factor)[:, None]


def root_matrix(key, rows_count, inner, grad_size, power, spread):
    first_key, second_key = jax.random.split(key)
    uniform_part = jax.random.uniform(first_key, (rows_count,), jnp.float32)
    factor = 2.0 ** (2.0 * uniform_part ** power - 1.0)
    diag_size = (inner * grad_size * grad_size) ** (-0.25)
    off_diag = jax.random.normal(second_key, (rows_count, rows_count), jnp.float32) * (spread * diag_size / math.sqrt(rows_count))
    off_diag = (off_diag + off_diag.T) * 0.5
    identity = jnp.eye(rows_count, dtype=jnp.float32)
    return off_diag * (1.0 - identity) + identity * (diag_size * factor)[:, None]


def draw_image_counts(key, part):
    key = jax.random.fold_in(key, 1)
    first_key, second_key = jax.random.split(key)
    counts = jax.random.randint(first_key, (N_DP,), max(1, IMG_DEV // 4), IMG_DEV + 1)
    full_index = jax.random.randint(second_key, (), 0, N_DP)
    return jnp.where(jnp.arange(N_DP) == full_index, IMG_DEV, counts).astype(jnp.int32)


def draw_norm_params(key, part):
    key = jax.random.fold_in(key, 2)
    first_key, second_key = jax.random.split(key)
    gain_rows = jnp.exp(jax.random.uniform(first_key, (2, D), jnp.float32, math.log(0.7), math.log(1.5)))
    shifts = jax.random.normal(second_key, (2, D), jnp.float32) * 0.3
    return jnp.stack([gain_rows[0], shifts[0], gain_rows[1], shifts[1]])


def draw_left_tok_in(key, part):
    key = jax.random.fold_in(key, 11)
    return statistics(key, S, DS, size_tok_in(), 1.0, 2.0)


def draw_right_tok_in(key, part):
    key = jax.random.fold_in(key, 12)
    return statistics(key, DS, S, size_tok_in(), 1.0, 2.0)


def draw_left_tok_out(key, part):
    key = jax.random.fold_in(key, 13)
    return statistics(key, DS, S, size_tok_out(), 1.0, 2.0)


def draw_right_tok_out(key, part):
    key = jax.random.fold_in(key, 14)
    return statistics(key, S, DS, size_tok_out(), 1.0, 2.0)


def draw_left_up(key, part):
    key = jax.random.fold_in(key, 15)
    return statistics(key, D, DC, size_up(), 1.0, 2.0)


def draw_right_up(key, part):
    key = jax.random.fold_in(key, 16)
    return statistics(key, DC, D, size_up(), 1.0, 2.0)


def draw_left_down(key, part):
    key = jax.random.fold_in(key, 17)
    return statistics(key, DC, D, size_down(), 1.0, 2.0)


def draw_right_down(key, part):
    key = jax.random.fold_in(key, 18)
    return statistics(key, D, DC, size_down(), 1.0, 2.0)


def draw_root_left_tok_in(key, part):
    key = jax.random.fold_in(key, 21)
    return root_matrix(key, S, DS, size_tok_in(), 1.0, 0.45)


def draw_root_right_tok_in(key, part):
    key = jax.random.fold_in(key, 22)
    return root_matrix(key, DS, S, size_tok_in(), 1.0, 0.45)


def draw_root_left_tok_out(key, part):
    key = jax.random.fold_in(key, 23)
    return root_matrix(key, DS, S, size_tok_out(), 1.0, 0.45)


def draw_root_right_tok_out(key, part):
    key = jax.random.fold_in(key, 24)
    return root_matrix(key, S, DS, size_tok_out(), 1.0, 0.45)


def draw_root_left_up(key, part):
    key = jax.random.fold_in(key, 25)
    return root_matrix(key, D, DC, size_up(), 1.0, 0.45)


def draw_root_right_up(key, part):
    key = jax.random.fold_in(key, 26)
    return root_matrix(key, DC, D, size_up(), 1.0, 0.45)


def draw_root_left_down(key, part):
    key = jax.random.fold_in(key, 27)
    return root_matrix(key, DC, D, size_down(), 1.0, 0.45)


def draw_root_right_down(key, part):
    key = jax.random.fold_in(key, 28)
    return root_matrix(key, D, DC, size_down(), 1.0, 0.45)


def second_moments(key, row_size, power):
    uniform_part = jax.random.uniform(key, row_size.shape, jnp.float32)
    return 4.0 ** uniform_part ** power * row_size * row_size


def draw_norm_second(key, part):
    key = jax.random.fold_in(key, 31)
    sizes_row = jnp.array([0.66, 0.66, 0.6, 0.6], jnp.float32) * channel_factor()
    row_size = jnp.broadcast_to(sizes_row[:, None], (4, D))
    return second_moments(key, row_size, 1.0)


def draw_bias_second(key, part):
    key = jax.random.fold_in(key, 32)
    row_size = jnp.concatenate([jnp.full((DS,), 0.66 * math.sqrt(S / DS) * mixing_factor(), jnp.float32), jnp.full((S,), 1.1 * mixing_factor(), jnp.float32), jnp.full((DC,), 0.6 * math.sqrt(D / DC) * channel_factor(), jnp.float32), jnp.full((D,), channel_factor(), jnp.float32)])
    return second_moments(key, row_size, 1.0)


def shard_levels(stream_key, extent, pieces, smallest, largest):
    def one(axis_at, parts):
        steps = jax.random.uniform(jax.random.fold_in(jax.random.fold_in(stream_key, 6), axis_at), (parts,), jnp.float32, smallest / len(pieces), largest / len(pieces))
        return jnp.repeat(jnp.exp(steps), extent[axis_at] // parts).reshape((-1,) + (1,) * (len(extent) - axis_at - 1))

    level = one(*pieces[0])
    for cut in pieces[1:]:
        level = level * one(*cut)
    return level


def scatter_about(rng, dims, scale, most, cuts=(), held_as=jnp.bfloat16):
    values = jax.random.normal(rng, dims, jnp.float32) * scale
    if len(cuts) > 0:
        values = shard_levels(rng, dims, cuts, -0.22, 0.18) * values
    return jnp.clip(values, min=-most, max=most).astype(held_as)


def setup_inputs(seed: int = 0) -> dict:
    keys = jax.random.split(jax.random.key(seed), 28)
    images = scatter_about(keys[0], (IMAGES, S, D), 1.0, 6.0, ((0, 64), (1, 4)))
    cotangent = scatter_about(keys[1], (IMAGES, S, D), 1.0, 6.0, ((0, 64), (1, 4)))
    image_counts = draw_image_counts(jax.random.fold_in(keys[27], 71), 0)
    w_tok_in = scatter_about(keys[3], (S, DS), S ** -0.5, 0.4375, ((1, 64),), jnp.float32)
    w_tok_out = scatter_about(keys[4], (DS, S), DS ** -0.5, 0.3125, ((0, 64),), jnp.float32)
    w_up = scatter_about(keys[5], (D, DC), D ** -0.5, 0.21875, ((1, 256),), jnp.float32)
    w_down = scatter_about(keys[6], (DC, D), DC ** -0.5, 0.109375, ((0, 256),), jnp.float32)
    norm_params = draw_norm_params(jax.random.fold_in(keys[27], 71), 0)
    biases = scatter_about(keys[8], (NB,), 0.3, 3.0, (), jnp.float32)
    left_tok_in = draw_left_tok_in(jax.random.fold_in(keys[27], 71), 0)
    right_tok_in = draw_right_tok_in(jax.random.fold_in(keys[27], 71), 0)
    left_tok_out = draw_left_tok_out(jax.random.fold_in(keys[27], 71), 0)
    right_tok_out = draw_right_tok_out(jax.random.fold_in(keys[27], 71), 0)
    left_up = draw_left_up(jax.random.fold_in(keys[27], 71), 0)
    right_up = draw_right_up(jax.random.fold_in(keys[27], 71), 0)
    left_down = draw_left_down(jax.random.fold_in(keys[27], 71), 0)
    right_down = draw_right_down(jax.random.fold_in(keys[27], 71), 0)
    root_left_tok_in = draw_root_left_tok_in(jax.random.fold_in(keys[27], 71), 0)
    root_right_tok_in = draw_root_right_tok_in(jax.random.fold_in(keys[27], 71), 0)
    root_left_tok_out = draw_root_left_tok_out(jax.random.fold_in(keys[27], 71), 0)
    root_right_tok_out = draw_root_right_tok_out(jax.random.fold_in(keys[27], 71), 0)
    root_left_up = draw_root_left_up(jax.random.fold_in(keys[27], 71), 0)
    root_right_up = draw_root_right_up(jax.random.fold_in(keys[27], 71), 0)
    root_left_down = draw_root_left_down(jax.random.fold_in(keys[27], 71), 0)
    root_right_down = draw_root_right_down(jax.random.fold_in(keys[27], 71), 0)
    norm_second = draw_norm_second(jax.random.fold_in(keys[27], 71), 0)
    bias_second = draw_bias_second(jax.random.fold_in(keys[27], 71), 0)
    return dict(images=images, cotangent=cotangent, image_counts=image_counts, w_tok_in=w_tok_in, w_tok_out=w_tok_out, w_up=w_up, w_down=w_down, norm_params=norm_params, biases=biases, left_tok_in=left_tok_in, right_tok_in=right_tok_in, left_tok_out=left_tok_out, right_tok_out=right_tok_out, left_up=left_up, right_up=right_up, left_down=left_down, right_down=right_down, root_left_tok_in=root_left_tok_in, root_right_tok_in=root_right_tok_in, root_left_tok_out=root_left_tok_out, root_right_tok_out=root_right_tok_out, root_left_up=root_left_up, root_right_up=root_right_up, root_left_down=root_left_down, root_right_down=root_right_down, norm_second=norm_second, bias_second=bias_second)


@jax.custom_vjp
def low(v):
    return lax.optimization_barrier(v.astype(jnp.bfloat16)).astype(jnp.float32)

@jax.custom_vjp
def low_back(v):
    return v

def low_keep(v):
    return (low(v), None)

def low_pass(kept, grad):
    return (grad,)

def back_keep(v):
    return (v, None)

def back_low(kept, grad):
    return (low(grad),)
low.defvjp(low_keep, low_pass)
low_back.defvjp(back_keep, back_low)
HIGH = lax.Precision.HIGHEST
NORM_EPS = 1e-06
DECAY = 0.5
RATE = 0.5
VECTOR_RATE = 0.5
VECTOR_EPS = 1e-08

def layer_norm(values, scale_row, shift_row):
    centre = values - lax.optimization_barrier(jnp.mean(values, axis=-1, keepdims=True))
    spread = lax.optimization_barrier(jnp.mean(centre * centre, axis=-1, keepdims=True))
    return centre * lax.rsqrt(spread + NORM_EPS) * scale_row + shift_row

def gelu_exact(values):
    return jax.nn.gelu(values, approximate=False)

def forward(parameters, pixels, keep_rows):
    w_tok_in, w_tok_out, w_up, w_down, norm_params, biases = parameters
    bias_tok_in = biases[:DS]
    bias_tok_out = biases[DS:DS + S]
    bias_up = biases[DS + S:DS + S + DC]
    bias_down = biases[DS + S + DC:]
    normed = low_back(low(layer_norm(pixels, norm_params[0], norm_params[1])))
    pre_tok = jnp.einsum('bsc,sk->bck', normed, low(w_tok_in), precision=HIGH) + bias_tok_in
    act_tok = low(gelu_exact(low_back(pre_tok)))
    mixed = jnp.einsum('bck,ks->bsc', act_tok, low(w_tok_out), precision=HIGH) + bias_tok_out[None, :, None]
    middle = pixels + low_back(low(mixed))
    normed_two = low(layer_norm(middle, norm_params[2], norm_params[3]))
    pre_chan = jnp.einsum('bsc,cf->bsf', normed_two, low(w_up), precision=HIGH) + bias_up
    act_chan = low(gelu_exact(low_back(pre_chan)))
    branch = jnp.einsum('bsf,fc->bsc', act_chan, low(w_down), precision=HIGH) + bias_down
    return keep_rows[:, None, None] * (middle + branch)

def product(left_matrix, right_matrix):
    return jnp.dot(left_matrix, right_matrix, precision=HIGH, preferred_element_type=jnp.float32)

def shampoo(weight, gradient, left_state, right_state, root_left, root_right):
    new_left = DECAY * left_state + (1.0 - DECAY) * product(gradient, gradient.T)
    new_right = DECAY * right_state + (1.0 - DECAY) * product(gradient.T, gradient)
    new_weight = weight - RATE * product(product(root_left, gradient), root_right)
    return (new_weight, new_left, new_right)

def diagonal_step(current, gradient, second):
    new_second = DECAY * second + (1.0 - DECAY) * gradient * gradient
    return (current - VECTOR_RATE * gradient * lax.rsqrt(new_second + VECTOR_EPS), new_second)

def reference(images, cotangent, image_counts, w_tok_in, w_tok_out, w_up, w_down, norm_params, biases, left_tok_in, right_tok_in, left_tok_out, right_tok_out, left_up, right_up, left_down, right_down, root_left_tok_in, root_right_tok_in, root_left_tok_out, root_right_tok_out, root_left_up, root_right_up, root_left_down, root_right_down, norm_second, bias_second):
    slots = jnp.arange(IMAGES, dtype=jnp.int32)
    owners = (slots // IMG_DEV).astype(jnp.int32)
    keep_image = (slots % IMG_DEV < image_counts[owners]).astype(jnp.float32)
    group_size = math.gcd(IMAGES, 16)
    group_count = IMAGES // group_size
    parameters = (w_tok_in, w_tok_out, w_up, w_down, norm_params, biases)

    def accumulate(totals, group_data):
        pixels, upstream, kept = group_data
        result, pull = jax.vjp(lambda params_in, inputs_in: forward(params_in, inputs_in, kept), parameters, pixels)
        param_grads, input_grad = pull(upstream)
        totals = jax.tree.map(lambda running, addend: running + addend, totals, param_grads)
        return (totals, (result.astype(jnp.bfloat16), input_grad))
    zeros_init = jax.tree.map(jnp.zeros_like, parameters)
    grouped = (images.astype(jnp.float32).reshape(group_count, group_size, S, D), cotangent.astype(jnp.float32).reshape(group_count, group_size, S, D), keep_image.reshape(group_count, group_size))
    totals, (outputs, input_grads) = lax.scan(accumulate, zeros_init, grouped)
    layer_output = outputs.reshape(IMAGES, S, D)
    grad_images = input_grads.reshape(IMAGES, S, D)
    per_image = 1.0 / IMAGES
    grad_tok_in, grad_tok_out, grad_up, grad_down, norm_grad, bias_grad = [term * per_image for term in totals]
    new_tok_in, new_left_tok_in, new_right_tok_in = shampoo(w_tok_in, grad_tok_in, left_tok_in, right_tok_in, root_left_tok_in, root_right_tok_in)
    new_tok_out, new_left_tok_out, new_right_tok_out = shampoo(w_tok_out, grad_tok_out, left_tok_out, right_tok_out, root_left_tok_out, root_right_tok_out)
    new_up, new_left_up, new_right_up = shampoo(w_up, grad_up, left_up, right_up, root_left_up, root_right_up)
    new_down, new_left_down, new_right_down = shampoo(w_down, grad_down, left_down, right_down, root_left_down, root_right_down)
    norm_new, norm_second_new = diagonal_step(norm_params, norm_grad, norm_second)
    bias_new, bias_second_new = diagonal_step(biases, bias_grad, bias_second)
    return (layer_output, grad_images, grad_tok_in, grad_tok_out, grad_up, grad_down, new_tok_in, new_tok_out, new_up, new_down, new_left_tok_in, new_right_tok_in, new_left_tok_out, new_right_tok_out, new_left_up, new_right_up, new_left_down, new_right_down, norm_grad, norm_second_new, norm_new, bias_grad, bias_second_new, bias_new)
```

```python
import jax
import jax.numpy as jnp
from jax import lax
from jax.experimental import pallas as pl
from jax.experimental.pallas import tpu as pltpu
from jax.sharding import PartitionSpec as P

MESH = pl.DeviceIdType.MESH
BF = jnp.bfloat16
F32 = jnp.float32
HIGH = lax.Precision.HIGHEST

D = 768
DC = 3072
DS = 384
S = 196
NX, NY, NZ = 4, 4, 8
EPS = 1e-06
PER_IMAGE = 1.0 / 512.0
PATCHES = 49
PAIR = 112
IMG = 256
ROW = 208
HALF = D // 2
LANES = (slice(0, HALF), slice(HALF, D))


def dot(left, right, left_dim=1, right_dim=0, precision=None):
    return lax.dot_general(
        left,
        right,
        (((left_dim,), (right_dim,)), ((), ())),
        preferred_element_type=F32,
        precision=precision,
    )


def pick(rows, cols, rule):
    row = lax.broadcasted_iota(jnp.int32, (rows, cols), 0)
    col = lax.broadcasted_iota(jnp.int32, (rows, cols), 1)
    return jnp.where(rule(row, col), 1.0, 0.0).astype(BF)


def ge(values, bound):
    return (values >= bound).astype(jnp.int32)


def gelu_and_slope(v):
    t = pl.reciprocal(1.0 + 0.23164188 * jnp.abs(v))
    e = jnp.exp(-0.5 * v * v)
    q = 0.5 * t * (
        0.254829592 + t * (-0.284496736 + t * (1.421413741 + t * (-1.453152027 + t * 1.061405429)))
    ) * e
    cdf = jnp.where(v >= 0, 1.0 - q, q)
    return v * cdf, cdf + v * e * 0.3989422804014327


def normalise(v):
    mean = jnp.mean(v, axis=-1, keepdims=True)
    centre = v - mean
    r = lax.rsqrt(jnp.mean(centre * centre, axis=-1, keepdims=True) + EPS)
    return centre * r, r


def normalise_back(xhat, r, dh, gain):
    dxh = dh * gain
    m1 = jnp.mean(dxh, axis=-1, keepdims=True)
    m2 = jnp.mean(dxh * xhat, axis=-1, keepdims=True)
    dv = r * (dxh - m1 - xhat * m2)
    return dv, jnp.sum(dh * xhat, axis=0, keepdims=True), jnp.sum(dh, axis=0, keepdims=True)


def fused(
    count, img, cot, tin, tout, wup, wdn, norm, btin, btout, bup, bdn,
    q_up, p_dn, p_up, q_dn, old_r_up, old_l_dn, old_l_up, old_r_dn,
    pl_ti, pr_ti, pl_to, pr_to, ol_ti, or_ti, ol_to, or_to,
    o_layer, o_gimg, o_gup, o_gdn, o_nup, o_ndn, o_rup, o_ldn, o_lup, o_rdn,
    o_small, o_gti, o_gto, o_nti, o_nto, o_lti, o_rti, o_lto, o_rto,
    ssem, rsem, lsem, stage, wst, tst, simg, scot, rimg, rcot, rlay, rgrad,
    xw, W, tk, tokin, tokout, ximg, normed, mid, slope, act, n2, mb, br, dn,
    upc, dnc, actb, dpb, xbi, G, RAr, RAl, XA, XB, RBr, RBl, PY,
    UJ, UJP, H, qst, Qx, XEo, XEi, SM, SB, SRr, SRl, SX, SY, SC, SF,
):
    dp = lax.axis_index("dp")
    x = lax.axis_index("mix")
    c = lax.rem(dp, 2)
    y = dp // (2 * NZ)
    z = lax.rem(dp // 2, NZ)

    def X(i):
        return lax.rem(x + i + NX, NX)

    def Y(i):
        return lax.rem(y + i + NY, NY)

    def Z(i):
        return lax.rem(z + i + NZ, NZ)

    def dev(xx, yy, zz, cc):
        return ((yy * NZ + zz) * 2 + cc, xx)

    to_x = [None] + [dev(X(i), y, z, c) for i in range(1, NX)]
    to_y = [None] + [dev(x, Y(i), z, c) for i in range(1, NY)]
    to_z = [None] + [dev(x, y, Z(i), c) for i in range(1, NZ)]
    sibling = dev(x, y, z, 1 - c)
    started = []
    used = [0]

    def put(src, dst, device):
        k = used[0]
        used[0] += 1
        copy = pltpu.make_async_remote_copy(
            src_ref=src, dst_ref=dst, send_sem=ssem.at[k], recv_sem=rsem.at[k],
            device_id=device, device_id_type=MESH,
        )
        copy.start()
        started.append(copy)
        return copy

    def arrived(copies):
        for copy in copies:
            copy.wait_recv()

    def total(*parts):
        value = parts[0].astype(F32)
        for part in parts[1:]:
            value = value + part.astype(F32)
        return value

    stage[...] = jnp.zeros_like(stage)
    stage[0:12, 0:D] = wup[...]
    stage[16:28, 0:D] = wdn[...]
    stage[0:6, D : D + S] = tin[...]
    stage[8:14, D : D + S] = tout[...]
    wst[...] = stage[:, 0:D].astype(BF)
    tst[...] = stage[0:16, D : D + 256].astype(BF)
    xw[x] = wst[...]
    tk[y, z, c] = tst[...]
    stage[0:12, :] = q_up[...]
    stage[12:16, :] = jnp.zeros((4, DC), F32)
    stage[16:28, :] = p_dn[...]
    qst[0] = stage[0:16, :].astype(BF)
    qst[1] = stage[16:32, :].astype(BF)
    Qx[:, x] = qst[:, :, pl.ds(pl.multiple_of(x * D, D), D)]
    for m in range(NX):
        def of_pair(row, col, m=m):
            second = ge(row, PATCHES)
            return (col == (row - PATCHES * second) * 8 + 2 * m + second) & (row < 2 * PATCHES)

        chooser = pick(PAIR, 8 * PATCHES, of_pair)
        simg[m] = dot(chooser, img[...]).astype(BF)
        scot[m] = dot(chooser, cot[...]).astype(BF)
    rimg[x] = simg[x]
    rcot[x] = scot[x]

    barrier = pltpu.get_barrier_semaphore()
    peers = to_x[1:] + to_y[1:] + to_z[1:] + [sibling]
    for peer in peers:
        pl.semaphore_signal(barrier, inc=1, device_id=peer, device_id_type=MESH)
    pl.semaphore_wait(barrier, len(peers))

    c_xw = [put(wst, xw.at[x], to_x[i]) for i in range(1, NX)]
    c_ty = [put(tk.at[y, z, c], tk.at[y, z, c], to_y[i]) for i in range(1, NY)]
    c_img = [put(simg.at[X(i)], rimg.at[x], to_x[i]) for i in range(1, NX)]

    arrived(c_xw)

    def of_shards(row, col):
        m, j = col >> 5, col & 31
        up = (j < 12) & (row == 12 * m + j)
        down = (j >= 16) & (j < 28) & (row == 32 + 12 * m + j)
        return up | down

    W[y, z] = dot(pick(96, 128, of_shards), xw[...].reshape(128, D)).astype(BF)

    LA, LB = LANES
    a_right, a_left, b_right, b_left, b_y = {}, {}, {}, {}, {}

    def a_send(step, d, right):
        if right:
            ref = W.at[Y(-d), Z(1 - step), :, LA]
            a_right[step, d] = put(ref, ref, to_z[1])
        else:
            ref = W.at[Y(-d), Z(step - 1), :, LA]
            a_left[step, d] = put(ref, ref, to_z[7])

    def b_send(step, right):
        if right:
            ref = W.at[y, Z(1 - step), :, LB]
            b_right[step] = put(ref, ref, to_z[1])
        else:
            ref = W.at[y, Z(step - 1), :, LB]
            b_left[step] = put(ref, ref, to_z[7])

    def b_spread(offset):
        ref = W.at[y, Z(offset), :, LB]
        b_y[offset] = [put(ref, ref, to_y[i]) for i in range(1, NY)]

    b_send(1, True)
    b_send(1, False)
    own_a = W.at[y, z, :, LA]
    c_ay = [None] + [put(own_a, own_a, to_y[i]) for i in range(1, NY)]
    a_send(1, 0, True)
    a_send(1, 0, False)
    b_spread(0)
    arrived(c_ty)
    c_tz = [put(tk.at[:, z, c], tk.at[:, z, c], to_z[i]) for i in range(1, NZ)]
    c_cot = [put(scot.at[X(i)], rcot.at[x], to_x[i]) for i in range(1, NX)]
    c_q = [
        put(qst.at[:, :, pl.ds(pl.multiple_of(X(i) * D, D), D)], Qx.at[:, x], to_x[i])
        for i in range(1, NX)
    ]
    for d in (1, 3, 2):
        c_ay[d].wait_recv()
        a_send(1, d, True)
        a_send(1, d, False)

    def gather_step(step):
        b_right[step].wait_recv()
        if step < 4:
            b_send(step + 1, True)
        b_spread(-step)
        if step < 4:
            b_left[step].wait_recv()
            if step < 3:
                b_send(step + 1, False)
            b_spread(step)
        for d in (0, 1, 3, 2):
            a_right[step, d].wait_recv()
            if step < 4:
                a_send(step + 1, d, True)
                a_left[step, d].wait_recv()
                if step < 3:
                    a_send(step + 1, d, False)

    arrived(c_tz)
    c_tc = put(tk.at[:, :, c], tk.at[:, :, c], sibling)
    gather_step(1)
    c_tc.wait_recv()

    def of_group(row, col):
        group, i = col >> 4, col & 15
        first = (i < 6) & (row == 6 * group + i)
        second = (i >= 8) & (i < 14) & (row == 40 + 6 * group + i)
        return first | second

    chooser = pick(96, 128, of_group)
    for g in range(8):
        part = tk[g // 2, 4 * (g % 2) : 4 * (g % 2) + 4].reshape(128, 256)
        part = dot(chooser, part).astype(BF)
        tokin[48 * g : 48 * g + 48, :] = part[0:48]
        tokout[48 * g : 48 * g + 48, :] = part[48:96]

    arrived(c_img)
    arrived(c_cot)
    keep = [jnp.where(2 * x + b < count[0], 1.0, 0.0).astype(F32) for b in range(2)]
    own = c * (2 * ROW)

    def own_rows(b):
        return pl.ds(pl.multiple_of(own + b * ROW, 16), ROW)

    both = pl.ds(pl.multiple_of(own, 16), 2 * ROW)
    for b in range(2):
        def of_image(row, col, b=b):
            part = ge(row, 49) + ge(row, 98) + ge(row, 147)
            return (col == 63 * part + 49 * b + row) & (row < S)

        chooser = pick(IMG, NX * PAIR, of_image)
        pixels = dot(chooser, rimg[...].reshape(NX * PAIR, D))
        ximg[b] = pixels
        back = dot(chooser[0:ROW], rcot[...].reshape(NX * PAIR, D)) * keep[b]
        mb[own_rows(b), :] = back.astype(BF)
        xhat, _ = normalise(pixels)
        normed[b] = (xhat * norm[0:1, :] + norm[1:2, :]).astype(BF)
    c_mb = put(mb.at[both], mb.at[both], sibling)
    gather_step(2)

    @pl.loop(0, 2)
    def _(b):
        pre = dot(tokin[...], normed[b]) + btin[...]
        value, grad = gelu_and_slope(pre)
        slope[b] = grad
        act[b] = value.astype(BF)
        mixed = dot(tokout[...], act[b], 0, 0) + btout[...]
        middle = ximg[b] + mixed.astype(BF).astype(F32)
        mid[b] = middle
        xhat, _ = normalise(middle[0:ROW])
        n2[own_rows(b), :] = (xhat * norm[2:3, :] + norm[3:4, :]).astype(BF)

    c_n2 = put(n2.at[both], n2.at[both], sibling)
    gather_step(3)
    gather_step(4)
    for offset in (0, -1, 1, -2, 2, -3, 3, -4):
        arrived(b_y[offset])
    c_mb.wait_recv()
    c_n2.wait_recv()

    SM[...] = jnp.zeros_like(SM)
    br[...] = jnp.zeros_like(br)
    dn[...] = jnp.zeros_like(dn)

    @pl.loop(0, 2)
    def _(half):
        for j in range(4):
            zz = Z(4 * half + j)
            upc[192 * j : 192 * j + 192, :] = W[:, zz, 0:48, :].reshape(192, D)
            dnc[192 * j : 192 * j + 192, :] = W[:, zz, 48:96, :].reshape(192, D)
        bias = jnp.concatenate([bup[2 * Z(4 * half + j) + c] for j in range(4)], axis=1)

        @pl.loop(0, 4)
        def _(r):
            rows = pl.ds(pl.multiple_of(r * ROW, 16), ROW)
            pre = dot(n2[rows, :], upc[...], 1, 1) + bias
            value, grad = gelu_and_slope(pre)
            low = value.astype(BF)
            actb[rows, :] = low
            br[rows, :] += dot(low, dnc[...])
            low = (grad * dot(mb[rows, :], dnc[...], 1, 1)).astype(BF)
            dpb[rows, :] = low
            dn[rows, :] += dot(low, upc[...])

        sums = dot(jnp.ones((8, 4 * ROW), BF), dpb[...])[0:1]
        for h in range(2):
            lanes = slice(384 * h, 384 * h + 384)
            for u, (left, right) in enumerate(((dpb, n2), (actb, mb))):
                grad = dot(left[:, lanes], right[...], 0, 0).astype(BF)
                for j in range(2):
                    part = grad[192 * j : 192 * j + 192].reshape(4, 48, D)
                    G[:, Z(4 * half + 2 * h + j), 48 * u : 48 * u + 48, :] = part
        for j in range(4):
            SM[pl.ds(464 + 8 * c + Z(4 * half + j), 1), 0:192] = sums[:, 192 * j : 192 * j + 192]

    other = pl.ds(pl.multiple_of((1 - c) * (2 * ROW), 16), 2 * ROW)
    upc[0 : 2 * ROW, :] = dn[other, :].astype(BF)
    c_dn = put(upc.at[0 : 2 * ROW], xbi.at[1], sibling)
    dnc[0 : 2 * ROW, :] = br[other, :].astype(BF)
    c_br = put(dnc.at[0 : 2 * ROW], xbi.at[0], sibling)

    ra, la, rb, lb, xb = {}, {}, {}, {}, {}

    def a_reduce(step):
        for w in range(NX):
            ref = G.at[X(w), Z(5 - step), :, LA]
            if step > 1:
                ra[step - 1, w].wait_recv()
                ref[...] = total(ref[...], RAr[step - 2, w]).astype(BF)
            ra[step, w] = put(ref, RAr.at[step - 1, w], to_z[1])
            if step < 4:
                ref = G.at[X(w), Z(step - 4), :, LA]
                if step > 1:
                    la[step - 1, w].wait_recv()
                    ref[...] = total(ref[...], RAl[step - 2, w]).astype(BF)
                la[step, w] = put(ref, RAl.at[step - 1, w], to_z[7])

    def b_sum(k, extra):
        arrived([xb[k % 8, i] for i in range(1, NX)])
        ref = G.at[x, Z(k), :, LB]
        parts = [XB[i, Z(k)] for i in range(NX - 1)]
        ref[...] = total(ref[...], *parts, *extra).astype(BF)
        return ref

    def b_reduce(step):
        extra = []
        if step > 1:
            rb[step - 1].wait_recv()
            extra = [RBr[step - 2]]
        rb[step] = put(b_sum(5 - step, extra), RBr.at[step - 1], to_z[1])
        if step < 4:
            extra = []
            if step > 1:
                lb[step - 1].wait_recv()
                extra = [RBl[step - 2]]
            lb[step] = put(b_sum(step - 4, extra), RBl.at[step - 1], to_z[7])

    a_reduce(1)
    for k in (4, 5, 3, 6, 2, 7, 1, 0):
        for i in range(1, NX):
            xb[k, i] = put(G.at[X(i), Z(k), :, LB], XB.at[i - 1, Z(k)], to_x[i])

    c_dn.wait_recv()
    c_br.wait_recv()
    lob, dmx = actb, dpb
    lob[0 : 2 * IMG, :] = jnp.zeros((2 * IMG, D), BF)
    dmx[0 : 2 * IMG, :] = jnp.zeros((2 * IMG, D), BF)
    gain_two = jnp.zeros((1, D), F32)
    shift_two = jnp.zeros((1, D), F32)
    for b in range(2):
        here = slice(b * ROW, b * ROW + ROW)
        branch = br[own_rows(b), :] + xbi[0, here, :].astype(F32) + bdn[...]
        lob[b * IMG : b * IMG + ROW, :] = (keep[b] * (mid[b, 0:ROW] + branch)).astype(BF)
        dh = dn[own_rows(b), :] + xbi[1, here, :].astype(F32)
        xhat, r = normalise(mid[b, 0:ROW])
        dv, gain, shift = normalise_back(xhat, r, dh, norm[2:3, :])
        gain_two = gain_two + gain
        shift_two = shift_two + shift
        back = mb[own_rows(b), :].astype(F32) + dv
        mid[b, 0:ROW] = back
        dmx[b * IMG : b * IMG + ROW, :] = back.astype(BF)

    def out_rows(m):
        def of_out(row, col):
            second = ge(row, PATCHES)
            place = (IMG - PATCHES) * second + PATCHES * m + row
            return (col == place) & (row < 2 * PATCHES)

        return pick(PAIR, 2 * IMG, of_out)

    a_reduce(2)
    for copy in c_img:
        copy.wait_send()
    for m in range(NX):
        simg[m] = dot(out_rows(m), lob[0 : 2 * IMG, :]).astype(BF)
    rlay[x] = simg[x]
    c_lay = [put(simg.at[X(i)], rlay.at[x], to_x[i]) for i in range(1, NX)]

    roots = [
        pltpu.make_async_copy(p_up, br.at[0:D], lsem.at[0]),
        pltpu.make_async_copy(q_dn, dn.at[0:D], lsem.at[1]),
    ]
    for copy in roots:
        copy.start()
    gti = jnp.zeros((IMG, DS), F32)
    gto = jnp.zeros((IMG, DS), F32)
    bti = jnp.zeros((8, DS), F32)
    bto = jnp.zeros((8, IMG), F32)
    gain_one = jnp.zeros((1, D), F32)
    shift_one = jnp.zeros((1, D), F32)
    ones = jnp.ones((8, D), BF)
    for b in range(2):
        dmixed = dmx[b * IMG : b * IMG + IMG, :]
        dpre = (slope[b] * dot(tokout[...], dmixed)).astype(BF)
        gti = gti + dot(normed[b], dpre, 1, 1)
        gto = gto + dot(dmixed, act[b], 1, 1)
        bti = bti + dot(ones, dpre, 1, 1)
        bto = bto + dot(ones, dmixed, 1, 1)
        dnormed = dot(tokin[...], dpre, 0, 0).astype(BF).astype(F32)
        xhat, r = normalise(ximg[b, 0:ROW])
        dv, gain, shift = normalise_back(xhat, r, dnormed[0:ROW], norm[0:1, :])
        gain_one = gain_one + gain
        shift_one = shift_one + shift
        lob[b * IMG : b * IMG + ROW, :] = (mid[b, 0:ROW] + dv).astype(BF)
        a_reduce(3 + b)

    SM[0:IMG, :] = gti
    SM[IMG : IMG + ROW, :] = gto[0:ROW]
    for j, row in enumerate((gain_one, shift_one, gain_two, shift_two)):
        SM[208 + 2 * j : 209 + 2 * j, :] = row[:, 0:HALF]
        SM[209 + 2 * j : 210 + 2 * j, :] = row[:, HALF:D]
    SM[216:224, :] = bti
    SM[224:232, 0:IMG] = bto
    SM[224:232, IMG:DS] = jnp.zeros((8, DS - IMG), F32)
    sums = dot(jnp.ones((8, 2 * ROW), BF), mb[both, :])
    SM[232:240, :] = sums[:, 0:HALF]
    SM[240:248, :] = sums[:, HALF:D]
    SB[...] = SM[...].reshape(NY, NZ, 16, DS).astype(BF)

    sr, sl = {}, {}

    def s_reduce(step):
        ref = SB.at[:, Z(5 - step)]
        if step > 1:
            sr[step - 1].wait_recv()
            ref[...] = total(ref[...], SRr[step - 2]).astype(BF)
        sr[step] = put(ref, SRr.at[step - 1], to_z[1])
        if step < 4:
            ref = SB.at[:, Z(step - 4)]
            if step > 1:
                sl[step - 1].wait_recv()
                ref[...] = total(ref[...], SRl[step - 2]).astype(BF)
            sl[step] = put(ref, SRl.at[step - 1], to_z[7])

    s_reduce(1)
    for copy in c_cot:
        copy.wait_send()
    for m in range(NX):
        scot[m] = dot(out_rows(m), lob[0 : 2 * IMG, :]).astype(BF)
    rgrad[x] = scot[x]

    c_xa = []
    for w in (1, 3, 2, 0):
        ra[4, w].wait_recv()
        la[3, w].wait_recv()
        ref = G.at[X(w), z, :, LA]
        ref[...] = total(ref[...], RAr[3, w], RAl[2, w]).astype(BF)
        if w > 0:
            c_xa.append(put(ref, XA.at[w - 1], to_x[w]))
    s_reduce(2)
    b_reduce(1)
    b_reduce(2)
    s_reduce(3)
    arrived(c_xa)
    ref = G.at[x, z, :, LA]
    PY[y, :, LA] = total(ref[...], XA[0], XA[1], XA[2]).astype(BF)
    c_py = [put(PY.at[y, :, LA], PY.at[y, :, LA], to_y[i]) for i in range(1, NY)]
    b_reduce(3)
    s_reduce(4)
    b_reduce(4)
    c_grad = [put(scot.at[X(i)], rgrad.at[x], to_x[i]) for i in range(1, NX)]

    sr[4].wait_recv()
    sl[3].wait_recv()
    ref = SB.at[:, z]
    ref[...] = total(ref[...], SRr[3], SRl[2]).astype(BF)
    c_sx = [put(SB.at[X(i), z], SX.at[i - 1], to_x[i]) for i in range(1, NX)]
    rb[4].wait_recv()
    lb[3].wait_recv()
    PY[y, :, LB] = b_sum(0, [RBr[3], RBl[2]])[...]
    c_py = c_py + [put(PY.at[y, :, LB], PY.at[y, :, LB], to_y[i]) for i in range(1, NY)]
    arrived(c_sx)
    SY[y] = total(SB[x, z], SX[0], SX[1], SX[2]).astype(BF)
    c_sy = [put(SY.at[y], SY.at[y], to_y[i]) for i in range(1, NY)]

    arrived(c_py)
    mean = total(PY[0], PY[1], PY[2], PY[3]) * PER_IMAGE
    H[z, c] = mean.astype(BF)
    hr, hl, hs = {}, {}, {}

    def h_send(step, u, right):
        ref = H.at[Z(1 - step) if right else Z(step - 1), c, 48 * u : 48 * u + 48]
        (hr if right else hl)[step, u] = put(ref, ref, to_z[1] if right else to_z[7])

    def h_share(offset):
        ref = H.at[Z(offset), c]
        hs[offset] = put(ref, ref, sibling)

    for u in range(2):
        h_send(1, u, True)
        h_send(1, u, False)
    h_share(0)

    first_j = used[0]
    used[0] += 3

    def j_copy(i):
        return pltpu.make_async_remote_copy(
            src_ref=H.at[z, c], dst_ref=UJ, send_sem=ssem.at[first_j + i - 1],
            recv_sem=rsem.at[first_j], device_id=to_x[i], device_id_type=MESH,
        )

    @pl.when(x == y)
    def _():
        for i in range(1, NX):
            j_copy(i).start()
        UJ[...] = H[z, c]

    arrived(c_sy)
    SC[c] = total(SY[0], SY[1], SY[2], SY[3]).astype(BF)
    c_sc = put(SC.at[c], SC.at[c], sibling)

    def h_step(step):
        for u in range(2):
            hr[step, u].wait_recv()
            if step < 4:
                h_send(step + 1, u, True)
                hl[step, u].wait_recv()
                if step < 3:
                    h_send(step + 1, u, False)
        h_share(-step)
        if step < 4:
            h_share(step)

    h_step(1)
    c_sc.wait_recv()
    SF[x, z] = (total(SC[0], SC[1]) * PER_IMAGE).astype(BF)
    c_fz = [put(SF.at[x, z], SF.at[x, z], to_z[i]) for i in range(1, NZ)]
    arrived(c_q)
    h_step(2)

    arrived(c_lay)
    arrived(c_grad)

    def of_patch(row, col):
        image = row & 7
        pair, second = image >> 1, image & 1
        return col == PAIR * pair + PATCHES * second + (row >> 3)

    chooser = pick(8 * PATCHES, NX * PAIR, of_patch)
    o_layer[...] = dot(chooser, rlay[...].reshape(NX * PAIR, D)).astype(BF)
    o_gimg[...] = dot(chooser, rgrad[...].reshape(NX * PAIR, D))
    h_step(3)
    arrived(c_fz)
    c_fx = [put(SF.at[x], SF.at[x], to_x[i]) for i in range(1, NX)]

    @pl.when(x != y)
    def _():
        j_copy(1).wait_recv()

    def of_rows(row, col):
        m, i = row >> 4, row & 15
        return (col == 12 * m + i) & (i < 12)

    spread = pick(64, 48, of_rows)
    channels = pick(16, D, lambda row, col: (col == 12 * dp + row) & (row < 12))
    for u, out in enumerate((o_gup, o_gdn)):
        UJP[u, 0:64] = dot(spread, UJ[48 * u : 48 * u + 48, :]).astype(BF)
        UJP[u, 64:80] = channels
        out[...] = UJP[u, pl.ds(pl.multiple_of(16 * x, 16), 16), :][0:12].astype(F32)
    h_step(4)

    arrived([hs[offset] for offset in (0, -1, 1, -2, 2, -3, 3, -4)])
    for u in range(2):
        quarter = H[:, :, 48 * u : 48 * u + 48, :].reshape(D, D)
        right = dot(UJP[u], quarter, 1, 1)
        left = jnp.concatenate([Qx[u].reshape(64, D), right[64:80].astype(BF)], axis=0)
        left = dot(left, quarter)
        for m in range(NX):
            XEo[m, u, :, 0:D] = right[16 * m : 16 * m + 16].astype(BF)
            XEo[m, u, :, D : 2 * D] = left[16 * m : 16 * m + 16].astype(BF)
            XEo[m, u, :, 2 * D : 2 * D + 192] = left[64:80, 192 * m : 192 * m + 192].astype(BF)
            XEo[m, u, :, 2 * D + 192 : 2 * D + 256] = jnp.zeros((16, 64), BF)
    XEi[x] = XEo[x]
    c_xe = [put(XEo.at[X(i)], XEi.at[x], to_x[i]) for i in range(1, NX)]

    arrived(c_fx)
    small = SF[...].reshape(512, DS)
    o_small[0:48, :] = small[208:256].astype(F32)
    o_small[48:64, :] = small[464:480].astype(F32)
    real = lax.broadcasted_iota(jnp.int32, (IMG, DS), 0) < S
    g_in = jnp.where(real, small[0:IMG].astype(F32), 0.0).astype(BF)
    g_out = jnp.where(real, small[IMG : 2 * IMG].astype(F32), 0.0).astype(BF)
    o_lti[...] = 0.5 * ol_ti[...] + 0.5 * dot(g_in, g_in, 1, 1)[0:S, 0:S]
    o_rti[...] = 0.5 * or_ti[...] + 0.5 * dot(g_in, g_in, 0, 0)
    o_lto[...] = 0.5 * ol_to[...] + 0.5 * dot(g_out, g_out, 0, 0)
    o_rto[...] = 0.5 * or_to[...] + 0.5 * dot(g_out, g_out, 1, 1)[0:S, 0:S]
    mine = pick(16, DS, lambda row, col: (col == 6 * dp + row) & (row < 6))
    o_gti[...] = dot(mine, g_in, 1, 1)[0:6, 0:S]
    o_gto[...] = dot(mine, g_out, 1, 1)[0:6, 0:S]
    mine = mine.astype(F32)
    step = dot(mine, pr_ti[...], 1, 1, HIGH)
    step = dot(step, g_in.astype(F32), 1, 1, HIGH)[:, 0:S]
    step = dot(step, pl_ti[...], 1, 1, HIGH)
    o_nti[...] = tin[...] - 0.5 * step[0:6]
    step = dot(mine, pl_to[...], 1, 0, HIGH)
    step = dot(step, g_out.astype(F32), 1, 1, HIGH)[:, 0:S]
    step = dot(step, pr_to[...], 1, 0, HIGH)
    o_nto[...] = tout[...] - 0.5 * step[0:6]

    arrived(c_xe)
    for copy in roots:
        copy.wait()
    for u, (o_stat, old_stat, o_side, old_side, o_new, weight, root, dim) in enumerate((
        (o_rup, old_r_up, o_lup, old_l_up, o_nup, wup, br, 1),
        (o_ldn, old_l_dn, o_rdn, old_r_dn, o_ndn, wdn, dn, 0),
    )):
        for m in range(NX):
            lanes = slice(D * m, D * m + D)
            fresh = XEi[m, u, :, 0:D][0:12].astype(F32)
            o_stat[:, lanes] = 0.5 * old_stat[:, lanes] + 0.5 * fresh
        side = total(*[XEi[m, u, :, 2 * D : 2 * D + 192] for m in range(NX)])
        o_side[...] = 0.5 * old_side[...] + 0.5 * side[0:12]
        step = total(*[XEi[m, u, :, D : 2 * D] for m in range(NX)])
        step = dot(step, root[0:D, :], 1, dim, HIGH)
        o_new[...] = weight[...] - 0.5 * step[0:12]

    for copy in started:
        if not any(copy is other for other in c_img + c_cot):
            copy.wait_send()

    @pl.when(x == y)
    def _():
        for i in range(1, NX):
            j_copy(i).wait_send()


def on_device(
    images, cotangent, image_counts, w_tok_in, w_tok_out, w_up, w_down, norm_params, biases,
    left_tok_in, right_tok_in, left_tok_out, right_tok_out, left_up, right_up, left_down, right_down,
    root_left_tok_in, root_right_tok_in, root_left_tok_out, root_right_tok_out,
    root_left_up, root_right_up, root_left_down, root_right_down, norm_second, bias_second,
):
    patch_rows = 8 * PATCHES

    def by_patch(v):
        return v.transpose(1, 0, 2).reshape(patch_rows, D)

    def by_image(v):
        return v.reshape(PATCHES, 8, D).transpose(1, 0, 2)

    args = (
        image_counts, by_patch(images), by_patch(cotangent), w_tok_in.T, w_tok_out, w_up.T, w_down,
        norm_params, biases[:DS].reshape(DS, 1),
        jnp.pad(biases[DS : DS + S], (0, IMG - S)).reshape(IMG, 1),
        biases[DS + S : DS + S + DC].reshape(NY, NZ, 2, 48).transpose(1, 2, 0, 3).reshape(16, 1, 192),
        biases[DS + S + DC :].reshape(1, D),
        root_right_up.T, root_left_down, root_left_up, root_right_down,
        right_up.T, left_down, left_up, right_down,
        root_left_tok_in, root_right_tok_in, root_left_tok_out, root_right_tok_out,
        left_tok_in, right_tok_in, left_tok_out, right_tok_out,
    )
    outs = [
        ((patch_rows, D), BF), ((patch_rows, D), F32), ((12, D), F32), ((12, D), F32), ((12, D), F32),
        ((12, D), F32), ((12, DC), F32), ((12, DC), F32), ((12, 192), F32), ((12, 192), F32),
        ((64, DS), F32), ((6, S), F32), ((6, S), F32), ((6, S), F32), ((6, S), F32),
        ((S, S), F32), ((DS, DS), F32), ((DS, DS), F32), ((S, S), F32),
    ]

    def vm(dtype, *shape):
        return pltpu.VMEM(shape, dtype)

    scratch = [
        pltpu.SemaphoreType.DMA((256,)), pltpu.SemaphoreType.DMA((256,)), pltpu.SemaphoreType.DMA((2,)),
        vm(F32, 32, DC), vm(BF, 32, D), vm(BF, 16, 256),
        *[vm(BF, NX, PAIR, D) for _ in range(6)],
        vm(BF, NX, 32, D), vm(BF, NY, NZ, 96, D), vm(BF, NY, NZ, 2, 16, 256),
        vm(BF, DS, 256), vm(BF, DS, 256),
        vm(F32, 2, IMG, D), vm(BF, 2, IMG, D), vm(F32, 2, IMG, D), vm(F32, 2, DS, D), vm(BF, 2, DS, D),
        vm(BF, 4 * ROW, D), vm(BF, 4 * ROW, D), vm(F32, 4 * ROW, D), vm(F32, 4 * ROW, D),
        vm(BF, D, D), vm(BF, D, D), vm(BF, 4 * ROW, D), vm(BF, 4 * ROW, D),
        vm(BF, 2, 2 * ROW, D),
        vm(BF, NY, NZ, 96, D),
        vm(BF, 4, NX, 96, HALF), vm(BF, 3, NX, 96, HALF), vm(BF, 3, 96, HALF), vm(BF, 3, NZ, 96, HALF),
        vm(BF, 4, 96, HALF), vm(BF, 3, 96, HALF), vm(BF, NY, 96, D),
        vm(BF, 96, D), vm(BF, 2, 80, D), vm(BF, NZ, 2, 96, D),
        vm(BF, 2, 16, DC), vm(BF, 2, NX, 16, D),
        vm(BF, NX, 2, 16, 1792), vm(BF, NX, 2, 16, 1792),
        vm(F32, 512, DS), vm(BF, NY, NZ, 16, DS), vm(BF, 4, NY, 16, DS), vm(BF, 3, NY, 16, DS),
        vm(BF, 3, 16, DS), vm(BF, NY, 16, DS), vm(BF, 2, 16, DS), vm(BF, NY, NZ, 16, DS),
    ]
    in_vmem = pl.BlockSpec(memory_space=pltpu.VMEM)
    (
        layer, gimg, gup, gdn, nup, ndn, rup, ldn, lup, rdn,
        small, gti, gto, nti, nto, lti, rti, lto, rto,
    ) = pl.pallas_call(
        fused,
        out_shape=[jax.ShapeDtypeStruct(shape, dtype) for shape, dtype in outs],
        in_specs=[pl.BlockSpec(memory_space=pltpu.SMEM)]
        + [pl.BlockSpec(memory_space=pl.ANY) if i in (14, 15) else in_vmem for i in range(1, len(args))],
        out_specs=[in_vmem] * len(outs),
        scratch_shapes=scratch,
        compiler_params=pltpu.CompilerParams(
            collective_id=0, has_side_effects=True, vmem_limit_bytes=64 * 2**20
        ),
        name="fused",
    )(*args)

    norm_grad = small[0:8].reshape(4, D)
    bias_grad = jnp.concatenate([
        small[8], small[16, :S],
        small[48:64, :192].reshape(2, NZ, NY, 48).transpose(2, 1, 0, 3).reshape(DC),
        small[24], small[32],
    ])

    def diagonal_step(current, gradient, second):
        fresh = 0.5 * second + 0.5 * gradient * gradient
        return current - 0.5 * gradient * lax.rsqrt(fresh + 1e-08), fresh

    norm_new, norm_second_new = diagonal_step(norm_params, norm_grad, norm_second)
    bias_new, bias_second_new = diagonal_step(biases, bias_grad, bias_second)
    return (
        by_image(layer), by_image(gimg), gti.T, gto, gup.T, gdn, nti.T, nto, nup.T, ndn,
        lti, rti, lto, rto, lup, rup.T, ldn, rdn,
        norm_grad, norm_second_new, norm_new, bias_grad, bias_second_new, bias_new,
    )


def solution(mesh):
    both, dp, rest = ("dp", "mix"), "dp", P()
    in_specs = (
        P(dp, "mix", None), P(dp, "mix", None), P(dp), P(None, dp), P(dp, None), P(None, both), P(both, None),
        rest, rest, rest, rest, rest, rest,
        P(dp, "mix"), P(None, both), P(both, None), P(dp, "mix"),
        rest, rest, rest, rest, rest, P(None, both), P(both, None), rest, rest, rest,
    )
    out_specs = (
        P(dp, "mix", None), P(dp, "mix", None), P(None, dp), P(dp, None), P(None, both), P(both, None),
        P(None, dp), P(dp, None), P(None, both), P(both, None),
        rest, rest, rest, rest, P(dp, "mix"), P(None, both), P(both, None), P(dp, "mix"),
        rest, rest, rest, rest, rest, rest,
    )
    return jax.shard_map(on_device, mesh=mesh, in_specs=in_specs, out_specs=out_specs, check_vma=False)
```

```python
import jax
import jax.numpy as jnp
from jax import lax
from jax.experimental import pallas as pl
from jax.experimental.pallas import tpu as pltpu
from jax.sharding import PartitionSpec as P

MESH = pl.DeviceIdType.MESH
BF = jnp.bfloat16
F32 = jnp.float32
HIGH = lax.Precision.HIGHEST

D = 768
DC = 3072
DS = 384
S = 196
NX, NY, NZ = 4, 4, 8
EPS = 1e-06
PER_IMAGE = 1.0 / 512.0
PATCHES = 49
PAIR = 112
IMG = 256
ROW = 208
HALF = D // 2
NB = 4420
NB_ROW = 5120
TILE = 128
P0, P1, P2 = slice(0, 256), slice(256, 512), slice(512, 768)
FAR_FIRST = (4, 5, 3, 6, 2, 7, 1, 0)


def dot(left, right, left_dim=1, right_dim=0, precision=None):
    return lax.dot_general(
        left,
        right,
        (((left_dim,), (right_dim,)), ((), ())),
        preferred_element_type=F32,
        precision=precision,
    )


def pick(rows, cols, rule):
    row = lax.broadcasted_iota(jnp.int32, (rows, cols), 0)
    col = lax.broadcasted_iota(jnp.int32, (rows, cols), 1)
    return jnp.where(rule(row, col), 1.0, 0.0).astype(BF)


def ge(values, bound):
    return (values >= bound).astype(jnp.int32)


def gelu_and_slope(v):
    t = pl.reciprocal(1.0 + 0.23164188 * jnp.abs(v))
    e = jnp.exp(-0.5 * v * v)
    q = 0.5 * t * (
        0.254829592 + t * (-0.284496736 + t * (1.421413741 + t * (-1.453152027 + t * 1.061405429)))
    ) * e
    cdf = jnp.where(v >= 0, 1.0 - q, q)
    return v * cdf, cdf + v * e * 0.3989422804014327


def normalise(v):
    mean = jnp.mean(v, axis=-1, keepdims=True)
    centre = v - mean
    r = lax.rsqrt(jnp.mean(centre * centre, axis=-1, keepdims=True) + EPS)
    return centre * r, r


def normalise_back(xhat, r, dh, gain):
    dxh = dh * gain
    m1 = jnp.mean(dxh, axis=-1, keepdims=True)
    m2 = jnp.mean(dxh * xhat, axis=-1, keepdims=True)
    dv = r * (dxh - m1 - xhat * m2)
    return dv, jnp.sum(dh * xhat, axis=0, keepdims=True), jnp.sum(dh, axis=0, keepdims=True)


def fused(
    count, img, cot, tin, tout, wup, wdn, norm, bias,
    q_up, p_dn, p_up, q_dn, old_r_up, old_l_dn, old_l_up, old_r_dn,
    pl_ti, pr_ti, pl_to, pr_to, ol_ti, or_ti, ol_to, or_to,
    rlay, rgrad, o_gup, o_gdn, o_nup, o_ndn, o_rup, o_ldn, o_lup, o_rdn,
    o_norm, o_bias, o_gti, o_gto, o_nti, o_nto, o_lti, o_rti, o_lto, o_rto,
    ssem, rsem, lsem, stage, wst, tst, simg, scot, rimg, rcot,
    xw, W, tk, tokin, tokout, bti, bto, bup, ximg, normed, mid, slope, act, n2, mb, br, dn,
    upc, dnc, actb, dpb, xbi, G, RAr, RAl, XA, YA, XB, YB, YC, XD, PZ, RZ,
    HQ, UJQ, UJP, qst, Qx, XEo, XEi, SM, SB, SX, SZ, SY, SC, SF,
):
    dp = lax.axis_index("dp")
    x = lax.axis_index("mix")
    c = lax.rem(dp, 2)
    y = dp // (2 * NZ)
    z = lax.rem(dp // 2, NZ)

    def X(i):
        return lax.rem(x + i + NX, NX)

    def Y(i):
        return lax.rem(y + i + NY, NY)

    def Z(i):
        return lax.rem(z + i + NZ, NZ)

    def dev(xx, yy, zz, cc):
        return ((yy * NZ + zz) * 2 + cc, xx)

    to_x = [None] + [dev(X(i), y, z, c) for i in range(1, NX)]
    to_y = [None] + [dev(x, Y(i), z, c) for i in range(1, NY)]
    to_z = [None] + [dev(x, y, Z(i), c) for i in range(1, NZ)]
    sibling = dev(x, y, z, 1 - c)
    started = []
    used = [0]

    def put(src, dst, device):
        k = used[0]
        used[0] += 1
        copy = pltpu.make_async_remote_copy(
            src_ref=src, dst_ref=dst, send_sem=ssem.at[k], recv_sem=rsem.at[k],
            device_id=device, device_id_type=MESH,
        )
        copy.start()
        started.append(copy)
        return copy

    def arrived(copies):
        for copy in copies:
            copy.wait_recv()

    def settle(copies):
        for copy in copies:
            copy.wait_send()
        started[:] = [item for item in started if not any(item is copy for copy in copies)]

    def total(*parts):
        value = parts[0].astype(F32)
        for part in parts[1:]:
            value = value + part.astype(F32)
        return value

    barrier = pltpu.get_barrier_semaphore()
    peers = to_x[1:] + to_y[1:] + to_z[1:] + [sibling]
    for peer in peers:
        pl.semaphore_signal(barrier, inc=1, device_id=peer, device_id_type=MESH)

    stage[:, 0 : 2 * D] = jnp.zeros((32, 2 * D), F32)
    stage[0:12, 0:D] = wup[...]
    stage[16:28, 0:D] = wdn[...]
    stage[0:6, D : D + S] = tin[...]
    stage[8:14, D : D + S] = tout[...]
    wst[...] = stage[:, 0:D].astype(BF)
    tst[...] = stage[0:16, D : D + 256].astype(BF)
    xw[x] = wst[...]
    tk[y, z, c] = tst[...]

    pl.semaphore_wait(barrier, len(peers))
    c_xw = [put(wst, xw.at[x], to_x[i]) for i in range(1, NX)]
    c_ty = [put(tk.at[y, z, c], tk.at[y, z, c], to_y[i]) for i in range(1, NY)]

    def of_pairs(row, col):
        m = ge(row, PAIR) + ge(row, 2 * PAIR) + ge(row, 3 * PAIR)
        i = row - PAIR * m
        second = ge(i, PATCHES)
        return (col == (i - PATCHES * second) * 8 + 2 * m + second) & (i < 2 * PATCHES)

    chooser = pick(NX * PAIR, 8 * PATCHES, of_pairs)
    simg[...] = dot(chooser, img[...]).astype(BF).reshape(NX, PAIR, D)
    c_img = [put(simg.at[X(i)], rimg.at[x], to_x[i]) for i in range(1, NX)]

    arrived(c_xw)

    def of_shards(row, col):
        m, j = col >> 5, col & 31
        up = (j < 12) & (row == 12 * m + j)
        down = (j >= 16) & (j < 28) & (row == 32 + 12 * m + j)
        return up | down

    upc[0:96, :] = dot(pick(96, 128, of_shards), xw[...].reshape(128, D)).astype(BF)
    W[y, z, :, 0:512] = upc[0:96, 0:512]

    def rows_of(q):
        return pl.ds(pl.multiple_of(48 * (q // 2), 16), 48)

    def lanes_of(q, part):
        return pl.ds(pl.multiple_of(256 * part + TILE * lax.rem(q, 2), TILE), TILE)

    a_right, a_left, b_right, b_left, b_y = {}, {}, {}, {}, {}

    def a_send(step, d, right):
        if right:
            ref = W.at[Y(-d), Z(1 - step), :, P0]
            a_right[step, d] = put(ref, ref, to_z[1])
        else:
            ref = W.at[Y(-d), Z(step - 1), :, P0]
            a_left[step, d] = put(ref, ref, to_z[7])

    def b_send(step, right):
        if right:
            ref = W.at[y, Z(1 - step), :, P1]
            b_right[step] = put(ref, ref, to_z[1])
        else:
            ref = W.at[y, Z(step - 1), :, P1]
            b_left[step] = put(ref, ref, to_z[7])

    def b_spread(offset):
        ref = W.at[y, Z(offset), :, P1]
        b_y[offset] = [put(ref, ref, to_y[i]) for i in range(1, NY)]

    def c_ref(yy, zz):
        return W.at[yy, zz, rows_of(x), lanes_of(x, 2)]

    def c_spread(d):
        ref = c_ref(Y(-d), slice(None))
        return [put(ref, ref, to_x[i]) for i in range(1, NX)]

    W[y, z, rows_of(x), lanes_of(x, 2)] = upc[rows_of(x), lanes_of(x, 2)]
    own_a = W.at[y, z, :, P0]
    b_send(1, True)
    b_send(1, False)
    c_ay = [None] + [put(own_a, own_a, to_y[i]) for i in range(1, NY)]
    c_cz = [put(c_ref(y, z), c_ref(y, z), to_z[i]) for i in range(1, NZ)]
    arrived(c_ty)
    c_tz = [put(tk.at[:, z, c], tk.at[:, z, c], to_z[i]) for i in range(1, NZ)]
    a_send(1, 0, True)
    a_send(1, 0, False)
    b_spread(0)
    for d in (1, 3, 2):
        c_ay[d].wait_recv()
        a_send(1, d, True)
        a_send(1, d, False)

    scot[...] = dot(chooser, cot[...]).astype(BF).reshape(NX, PAIR, D)
    c_cot = [put(scot.at[X(i)], rcot.at[x], to_x[i]) for i in range(1, NX)]
    rimg[x] = simg[x]
    rcot[x] = scot[x]
    stage[0:12, :] = q_up[...]
    stage[12:16, :] = jnp.zeros((4, DC), F32)
    stage[16:28, :] = p_dn[...]
    stage[28:32, :] = jnp.zeros((4, DC), F32)
    qst[0] = stage[0:16, :].astype(BF)
    qst[1] = stage[16:32, :].astype(BF)
    diagonal = pick(TILE, TILE, lambda row, col: row == col).astype(F32)

    def column(first):
        spread = jnp.broadcast_to(bias[:, first : first + TILE], (TILE, TILE))
        return jnp.sum(spread * diagonal, axis=1, keepdims=True)

    for j in range(3):
        bti[TILE * j : TILE * j + TILE, :] = column(TILE * j)
    for j in range(2):
        bto[TILE * j : TILE * j + TILE, :] = column(DS + TILE * j)
    for zz in range(NZ):
        for cc in range(2):
            first = [DS + S + 48 * ((yy * NZ + zz) * 2 + cc) for yy in range(NY)]
            bup[2 * zz + cc] = jnp.concatenate([bias[:, f : f + 48] for f in first], axis=1)
    bias_down = bias[:, DS + S + DC : NB]

    arrived(c_cz)
    c_cy = [None] + [put(c_ref(y, slice(None)), c_ref(y, slice(None)), to_y[i]) for i in range(1, NY)]
    c_cx = c_spread(0)

    def gather_step(step):
        b_right[step].wait_recv()
        if step < 4:
            b_send(step + 1, True)
        b_spread(-step)
        if step < 4:
            b_left[step].wait_recv()
            if step < 3:
                b_send(step + 1, False)
            b_spread(step)
        for d in (0, 1, 3, 2):
            a_right[step, d].wait_recv()
            if step < 4:
                a_send(step + 1, d, True)
                a_left[step, d].wait_recv()
                if step < 3:
                    a_send(step + 1, d, False)

    arrived(c_tz)
    c_tc = put(tk.at[:, :, c], tk.at[:, :, c], sibling)
    gather_step(1)
    for d in (1, 3, 2):
        c_cy[d].wait_recv()
        c_cx = c_cx + c_spread(d)
    c_tc.wait_recv()

    def of_group(row, col):
        group, i = col >> 4, col & 15
        first = (i < 6) & (row == 6 * group + i)
        second = (i >= 8) & (i < 14) & (row == 40 + 6 * group + i)
        return first | second

    chooser = pick(96, 128, of_group)
    for g in range(8):
        part = tk[g // 2, 4 * (g % 2) : 4 * (g % 2) + 4].reshape(128, 256)
        part = dot(chooser, part).astype(BF)
        tokin[48 * g : 48 * g + 48, :] = part[0:48]
        tokout[48 * g : 48 * g + 48, :] = part[48:96]

    arrived(c_img)
    arrived(c_cot)
    keep = [jnp.where(2 * x + b < count[0], 1.0, 0.0).astype(F32) for b in range(2)]
    own = c * (2 * ROW)

    def own_rows(b):
        return pl.ds(pl.multiple_of(own + b * ROW, 16), ROW)

    both = pl.ds(pl.multiple_of(own, 16), 2 * ROW)

    def of_images(row, col):
        b = ge(row, IMG)
        i = row - IMG * b
        part = ge(i, 49) + ge(i, 98) + ge(i, 147)
        return (col == 63 * part + 49 * b + i) & (i < S)

    chooser = pick(2 * IMG, NX * PAIR, of_images)
    ximg[...] = dot(chooser, rimg[...].reshape(NX * PAIR, D)).reshape(2, IMG, D)
    back = dot(chooser, rcot[...].reshape(NX * PAIR, D))
    for b in range(2):
        mb[own_rows(b), :] = (back[b * IMG : b * IMG + ROW] * keep[b]).astype(BF)
        xhat, _ = normalise(ximg[b])
        normed[b] = (xhat * norm[0:1, :] + norm[1:2, :]).astype(BF)
    c_mb = put(mb.at[both], mb.at[both], sibling)
    gather_step(2)

    @pl.loop(0, 2)
    def _(b):
        pre = dot(tokin[...], normed[b]) + bti[...]
        value, grad = gelu_and_slope(pre)
        slope[b] = grad
        act[b] = value.astype(BF)
        mixed = dot(tokout[...], act[b], 0, 0) + bto[...]
        middle = ximg[b] + mixed.astype(BF).astype(F32)
        mid[b] = middle
        xhat, _ = normalise(middle[0:ROW])
        n2[own_rows(b), :] = (xhat * norm[2:3, :] + norm[3:4, :]).astype(BF)

    c_n2 = put(n2.at[both], n2.at[both], sibling)
    gather_step(3)
    gather_step(4)
    for offset in (0, -1, 1, -2, 2, -3, 3, -4):
        arrived(b_y[offset])
    arrived(c_cx)
    c_mb.wait_recv()
    c_n2.wait_recv()

    br[...] = jnp.zeros_like(br)
    dn[...] = jnp.zeros_like(dn)
    for half in range(2):
        offsets = FAR_FIRST[4 * half : 4 * half + 4]
        for j, k in enumerate(offsets):
            upc[192 * j : 192 * j + 192, :] = W[:, Z(k), 0:48, :].reshape(192, D)
            dnc[192 * j : 192 * j + 192, :] = W[:, Z(k), 48:96, :].reshape(192, D)
        row = jnp.concatenate([bup[2 * Z(k) + c] for k in offsets], axis=1)
        lanes = slice(half * D, half * D + D)

        @pl.loop(0, 4)
        def _(r, row=row, lanes=lanes):
            rows = pl.ds(pl.multiple_of(r * ROW, 16), ROW)
            pre = dot(n2[rows, :], upc[...], 1, 1) + row
            value, grad = gelu_and_slope(pre)
            low = value.astype(BF)
            actb[rows, lanes] = low
            br[rows, :] += dot(low, dnc[...])
            low = (grad * dot(mb[rows, :], dnc[...], 1, 1)).astype(BF)
            dpb[rows, lanes] = low
            dn[rows, :] += dot(low, upc[...])

    other = pl.ds(pl.multiple_of((1 - c) * (2 * ROW), 16), 2 * ROW)
    upc[0 : 2 * ROW, :] = dn[other, :].astype(BF)
    c_dn = put(upc.at[0 : 2 * ROW], xbi.at[1], sibling)
    dnc[0 : 2 * ROW, :] = br[other, :].astype(BF)
    c_br = put(dnc.at[0 : 2 * ROW], xbi.at[0], sibling)

    ra, la, xb, yb, yc, xd, rz = {}, {}, {}, {}, {}, {}, {}

    def gradients(pair):
        lanes = slice(2 * 192 * pair, 2 * 192 * pair + 384)
        offsets = FAR_FIRST[2 * pair : 2 * pair + 2]
        for u, (left, right) in enumerate(((dpb, n2), (actb, mb))):
            grad = dot(left[:, lanes], right[...], 0, 0).astype(BF)
            for j, k in enumerate(offsets):
                part = grad[192 * j : 192 * j + 192].reshape(4, 48, D)
                G[:, Z(k), 48 * u : 48 * u + 48, :] = part
        for k in offsets:
            for i in range(1, NX):
                xb[k, i] = put(G.at[X(i), Z(k), :, P1], XB.at[i - 1, Z(k)], to_x[i])
                ref = G.at[:, Z(k), rows_of(Y(i)), lanes_of(Y(i), 2)]
                yb[k, i] = put(ref, YB.at[i - 1, Z(k)], to_y[i])

    def a_reduce(step):
        for w in range(NX):
            ref = G.at[X(w), Z(5 - step), :, P0]
            if step > 1:
                ra[step - 1, w].wait_recv()
                ref[...] = total(ref[...], RAr[step - 2, w]).astype(BF)
            ra[step, w] = put(ref, RAr.at[step - 1, w], to_z[1])
            if step < 4:
                ref = G.at[X(w), Z(step - 4), :, P0]
                if step > 1:
                    la[step - 1, w].wait_recv()
                    ref[...] = total(ref[...], RAl[step - 2, w]).astype(BF)
                la[step, w] = put(ref, RAl.at[step - 1, w], to_z[7])

    def second(k):
        arrived([xb[k, i] for i in range(1, NX)])
        ref = G.at[x, Z(k), :, P1]
        ref[...] = total(ref[...], *[XB[i, Z(k)] for i in range(NX - 1)]).astype(BF)
        for i in range(1, NY):
            ref = G.at[x, Z(k), rows_of(Y(i)), lanes_of(Y(i), 1)]
            yc[k, i] = put(ref, YC.at[i - 1, Z(k)], to_y[i])
        arrived([yb[k, i] for i in range(1, NY)])
        ref = G.at[:, Z(k), rows_of(y), lanes_of(y, 2)]
        ref[...] = total(ref[...], *[YB[i, Z(k)] for i in range(NY - 1)]).astype(BF)
        for i in range(1, NX):
            ref = G.at[X(i), Z(k), rows_of(y), lanes_of(y, 2)]
            xd[k, i] = put(ref, XD.at[i - 1, Z(k)], to_x[i])

    def third(k):
        arrived([yc[k, i] for i in range(1, NY)])
        value = G[x, Z(k), rows_of(y), lanes_of(y, 1)]
        PZ[Z(k), :, 0:TILE] = total(value, *[YC[i, Z(k)] for i in range(NY - 1)]).astype(BF)
        arrived([xd[k, i] for i in range(1, NX)])
        value = G[x, Z(k), rows_of(y), lanes_of(y, 2)]
        PZ[Z(k), :, TILE : 2 * TILE] = total(value, *[XD[i, Z(k)] for i in range(NX - 1)]).astype(BF)
        if k > 0:
            rz[k] = put(PZ.at[Z(k)], RZ.at[k - 1], to_z[k])

    gradients(0)
    a_reduce(1)
    gradients(1)
    gradients(2)
    a_reduce(2)
    gradients(3)

    c_dn.wait_recv()
    c_br.wait_recv()
    ones = jnp.ones((8, 4 * ROW), BF)
    up_sums = dot(ones, dpb[...])[0:1]
    down_sums = dot(ones[:, 0 : 2 * ROW], mb[both, :])
    lob, dmx = actb, dpb
    lob[0 : 2 * IMG, 0:D] = jnp.zeros((2 * IMG, D), BF)
    dmx[0 : 2 * IMG, 0:D] = jnp.zeros((2 * IMG, D), BF)
    gain_two = jnp.zeros((1, D), F32)
    shift_two = jnp.zeros((1, D), F32)
    for b in range(2):
        here = slice(b * ROW, b * ROW + ROW)
        branch = br[own_rows(b), :] + xbi[0, here, :].astype(F32) + bias_down
        lob[b * IMG : b * IMG + ROW, 0:D] = (keep[b] * (mid[b, 0:ROW] + branch)).astype(BF)
        dh = dn[own_rows(b), :] + xbi[1, here, :].astype(F32)
        xhat, r = normalise(mid[b, 0:ROW])
        dv, gain, shift = normalise_back(xhat, r, dh, norm[2:3, :])
        gain_two = gain_two + gain
        shift_two = shift_two + shift
        back = mb[own_rows(b), :].astype(F32) + dv
        mid[b, 0:ROW] = back
        dmx[b * IMG : b * IMG + ROW, 0:D] = back.astype(BF)

    def of_out(row, col):
        m = ge(row, PAIR) + ge(row, 2 * PAIR) + ge(row, 3 * PAIR)
        i = row - PAIR * m
        second_one = ge(i, PATCHES)
        place = (IMG - PATCHES) * second_one + PATCHES * m + i
        return (col == place) & (i < 2 * PATCHES)

    out_chooser = pick(NX * PAIR, 2 * IMG, of_out)

    def to_patches(buffer, sent):
        settle(sent)
        buffer[...] = dot(out_chooser, lob[0 : 2 * IMG, 0:D]).astype(BF).reshape(NX, PAIR, D)

    second(4)
    second(5)
    a_reduce(3)
    to_patches(simg, c_img)
    own_out = [pltpu.make_async_copy(simg.at[x], rlay.at[x], lsem.at[2])]
    own_out[0].start()
    c_lay = [put(simg.at[X(i)], rlay.at[x], to_x[i]) for i in range(1, NX)]
    second(3)
    second(6)

    roots = [
        pltpu.make_async_copy(p_up, br.at[0:D], lsem.at[0]),
        pltpu.make_async_copy(q_dn, dn.at[0:D], lsem.at[1]),
    ]
    for copy in roots:
        copy.start()
    gti = jnp.zeros((IMG, DS), F32)
    gto = jnp.zeros((IMG, DS), F32)
    sum_ti = jnp.zeros((8, DS), F32)
    sum_to = jnp.zeros((8, IMG), F32)
    gain_one = jnp.zeros((1, D), F32)
    shift_one = jnp.zeros((1, D), F32)
    ones = jnp.ones((8, D), BF)
    for b in range(2):
        dmixed = dmx[b * IMG : b * IMG + IMG, 0:D]
        dpre = (slope[b] * dot(tokout[...], dmixed)).astype(BF)
        gti = gti + dot(normed[b], dpre, 1, 1)
        gto = gto + dot(dmixed, act[b], 1, 1)
        sum_ti = sum_ti + dot(ones, dpre, 1, 1)
        sum_to = sum_to + dot(ones, dmixed, 1, 1)
        dnormed = dot(tokin[...], dpre, 0, 0).astype(BF).astype(F32)
        xhat, r = normalise(ximg[b, 0:ROW])
        dv, gain, shift = normalise_back(xhat, r, dnormed[0:ROW], norm[0:1, :])
        gain_one = gain_one + gain
        shift_one = shift_one + shift
        lob[b * IMG : b * IMG + ROW, 0:D] = (mid[b, 0:ROW] + dv).astype(BF)
        if b == 0:
            a_reduce(4)
            second(2)
            second(7)
            third(4)
            third(5)
        else:
            second(1)
            second(0)
            third(3)
            third(6)

    SM[0:IMG, :] = gti
    SM[IMG : IMG + ROW, :] = gto[0:ROW]
    SM[IMG + ROW :, :] = jnp.zeros((IMG - ROW, DS), F32)
    for j, row in enumerate((gain_one, shift_one, gain_two, shift_two)):
        SM[208 + 2 * j : 209 + 2 * j, :] = row[:, 0:HALF]
        SM[209 + 2 * j : 210 + 2 * j, :] = row[:, HALF:D]
    SM[216:224, :] = sum_ti
    SM[224:232, 0:IMG] = sum_to
    SM[224:232, IMG:DS] = jnp.zeros((8, DS - IMG), F32)
    SM[232:240, :] = down_sums[:, 0:HALF]
    SM[240:248, :] = down_sums[:, HALF:D]
    for j, k in enumerate(FAR_FIRST):
        SM[pl.ds(464 + 8 * c + Z(k), 1), 0:192] = up_sums[:, 192 * j : 192 * j + 192]
    SB[...] = SM[...].reshape(NY, NZ, 16, DS).astype(BF)
    c_sx = [put(SB.at[X(i)], SX.at[i - 1], to_x[i]) for i in range(1, NX)]

    c_xa = []
    for w in (1, 3, 2, 0):
        ra[4, w].wait_recv()
        la[3, w].wait_recv()
        ref = G.at[X(w), z, :, P0]
        ref[...] = total(ref[...], RAr[3, w], RAl[2, w]).astype(BF)
        if w > 0:
            c_xa.append(put(ref, XA.at[w - 1], to_x[w]))
    for k in (2, 7, 1, 0):
        third(k)
    arrived(c_xa)
    ref = G.at[x, z, :, P0]
    ref[...] = total(ref[...], XA[0], XA[1], XA[2]).astype(BF)
    c_ya = [
        put(G.at[x, z, rows_of(Y(i)), lanes_of(Y(i), 0)], YA.at[i - 1], to_y[i])
        for i in range(1, NY)
    ]
    arrived(c_sx)
    SB[x] = total(SB[x], SX[0], SX[1], SX[2]).astype(BF)
    c_sz = [put(SB.at[x, Z(i)], SZ.at[i - 1], to_z[i]) for i in range(1, NZ)]

    arrived(rz.values())
    mean = total(PZ[z], *[RZ[i] for i in range(NZ - 1)]) * PER_IMAGE
    HQ[c, y, z, :, TILE:] = mean.astype(BF)
    arrived(c_ya)
    mean = total(G[x, z, rows_of(y), lanes_of(y, 0)], YA[0], YA[1], YA[2]) * PER_IMAGE
    HQ[c, y, z, :, 0:TILE] = mean.astype(BF)
    hz, hy, hs = {}, {}, {}
    for i in (4, 3, 5, 2, 6, 1, 7):
        hz[i] = put(HQ.at[c, y, z], HQ.at[c, y, z], to_z[i])

    def h_spread(offset):
        ref = HQ.at[c, y, Z(offset)]
        hy[offset] = [put(ref, ref, to_y[i]) for i in range(1, NY)]

    def h_share(offset):
        arrived(hy[offset])
        ref = HQ.at[c, :, Z(offset)]
        hs[offset] = put(ref, ref, sibling)

    h_spread(0)
    to_patches(scot, c_cot)
    own_out.append(pltpu.make_async_copy(scot.at[x], rgrad.at[x], lsem.at[3]))
    own_out[1].start()
    c_grad = [put(scot.at[X(i)], rgrad.at[x], to_x[i]) for i in range(1, NX)]
    arrived(c_sz)
    SY[y] = total(SB[x, z], *[SZ[i] for i in range(NZ - 1)]).astype(BF)
    c_sy = [put(SY.at[y], SY.at[y], to_y[i]) for i in range(1, NY)]
    for i in (1, 7, 2, 6):
        hz[i].wait_recv()
        h_spread(-i)
    h_share(0)

    first_j = used[0]
    used[0] += 3

    def j_copy(i):
        return pltpu.make_async_remote_copy(
            src_ref=HQ.at[c, :, z], dst_ref=UJQ, send_sem=ssem.at[first_j + i - 1],
            recv_sem=rsem.at[first_j], device_id=to_x[i], device_id_type=MESH,
        )

    @pl.when(x == y)
    def _():
        for i in range(1, NX):
            j_copy(i).start()
        UJQ[...] = HQ[c, :, z]

    arrived(c_sy)
    SC[c] = total(SY[0], SY[1], SY[2], SY[3]).astype(BF)
    c_sc = put(SC.at[c], SC.at[c], sibling)
    for i in (3, 5, 4):
        hz[i].wait_recv()
        h_spread(-i)
    c_sc.wait_recv()
    SF[x, z] = (total(SC[0], SC[1]) * PER_IMAGE).astype(BF)
    c_fz = [put(SF.at[x, z], SF.at[x, z], to_z[i]) for i in range(1, NZ)]
    for i in (1, 7, 2, 6):
        h_share(-i)
    Qx[:, x] = qst[:, :, pl.ds(pl.multiple_of(x * D, D), D)]
    c_q = [
        put(qst.at[:, :, pl.ds(pl.multiple_of(X(i) * D, D), D)], Qx.at[:, x], to_x[i])
        for i in range(1, NX)
    ]

    @pl.when(x != y)
    def _():
        j_copy(1).wait_recv()

    def of_rows(row, col):
        m, i = row >> 4, row & 15
        return (col == 12 * m + i) & (i < 12)

    spread = pick(64, 48, of_rows)
    channels = pick(16, D, lambda row, col: (col == 12 * dp + row) & (row < 12))

    def unfold(dst, read, u):
        for t in range(2):
            value = read(2 * u + t)
            for part in range(3):
                lanes = slice(256 * part + TILE * t, 256 * part + TILE * t + TILE)
                dst[:, lanes] = value[..., TILE * part : TILE * part + TILE].reshape(-1, TILE)

    settle([c_dn, c_mb, c_n2])
    for u, out in enumerate((o_gup, o_gdn)):
        unfold(upc.at[0:48], lambda q: UJQ[q], u)
        UJP[u, 0:64] = dot(spread, upc[0:48, :]).astype(BF)
        UJP[u, 64:80] = channels
        out[...] = UJP[u, pl.ds(pl.multiple_of(16 * x, 16), 16), :][0:12].astype(F32)
    arrived(c_fz)
    c_fx = [put(SF.at[x], SF.at[x], to_x[i]) for i in range(1, NX)]
    for i in (3, 5, 4):
        h_share(-i)

    arrived([hs[offset] for offset in (0, -1, -7, -2, -6, -3, -5, -4)])
    arrived(c_q)
    for u in range(2):
        store = (n2, mb)[u]
        for zz in range(NZ):
            for cc in range(2):
                first = (2 * zz + cc) * 48
                unfold(store.at[first : first + 48], lambda q: HQ[cc, q, zz], u)
        quarter = store[0:D, :]
        right = dot(UJP[u], quarter, 1, 1)
        left = jnp.concatenate([Qx[u].reshape(64, D), right[64:80].astype(BF)], axis=0)
        left = dot(left, quarter)
        for m in range(NX):
            XEo[m, u, :, 0:D] = right[16 * m : 16 * m + 16].astype(BF)
            XEo[m, u, :, D : 2 * D] = left[16 * m : 16 * m + 16].astype(BF)
            XEo[m, u, :, 2 * D : 2 * D + 192] = left[64:80, 192 * m : 192 * m + 192].astype(BF)
            XEo[m, u, :, 2 * D + 192 : 2 * D + 256] = jnp.zeros((16, 64), BF)
    XEi[x] = XEo[x]
    c_xe = [put(XEo.at[X(i)], XEi.at[x], to_x[i]) for i in range(1, NX)]

    arrived(c_fx)
    small = SF[...].reshape(512, DS)
    o_norm[...] = small[208:216].astype(F32)
    vector = small[208:256].astype(F32)
    ups = small[464:480].astype(F32)
    pieces = [vector[8:9], vector[16:17, 0:S]]
    for yy in range(NY):
        for zz in range(NZ):
            for cc in range(2):
                pieces.append(ups[8 * cc + zz : 8 * cc + zz + 1, 48 * yy : 48 * yy + 48])
    pieces += [vector[24:25], vector[32:33], jnp.zeros((1, NB_ROW - NB), F32)]
    o_bias[...] = jnp.concatenate(pieces, axis=1)
    real = lax.broadcasted_iota(jnp.int32, (IMG, DS), 0) < S
    g_in = jnp.where(real, small[0:IMG].astype(F32), 0.0).astype(BF)
    g_out = jnp.where(real, small[IMG : 2 * IMG].astype(F32), 0.0).astype(BF)
    o_lti[...] = 0.5 * ol_ti[...] + 0.5 * dot(g_in, g_in, 1, 1)[0:S, 0:S]
    o_rti[...] = 0.5 * or_ti[...] + 0.5 * dot(g_in, g_in, 0, 0)
    o_lto[...] = 0.5 * ol_to[...] + 0.5 * dot(g_out, g_out, 0, 0)
    o_rto[...] = 0.5 * or_to[...] + 0.5 * dot(g_out, g_out, 1, 1)[0:S, 0:S]
    mine = pick(16, DS, lambda row, col: (col == 6 * dp + row) & (row < 6))
    o_gti[...] = dot(mine, g_in, 1, 1)[0:6, 0:S]
    o_gto[...] = dot(mine, g_out, 1, 1)[0:6, 0:S]
    mine = mine.astype(F32)
    step = dot(mine, pr_ti[...], 1, 1, HIGH)
    step = dot(step, g_in.astype(F32), 1, 1, HIGH)[:, 0:S]
    step = dot(step, pl_ti[...], 1, 1, HIGH)
    o_nti[...] = tin[...] - 0.5 * step[0:6]
    step = dot(mine, pl_to[...], 1, 0, HIGH)
    step = dot(step, g_out.astype(F32), 1, 1, HIGH)[:, 0:S]
    step = dot(step, pr_to[...], 1, 0, HIGH)
    o_nto[...] = tout[...] - 0.5 * step[0:6]

    arrived(c_xe)
    for copy in roots:
        copy.wait()
    for u, (o_stat, old_stat, o_side, old_side, o_new, weight, root, dim) in enumerate((
        (o_rup, old_r_up, o_lup, old_l_up, o_nup, wup, br, 1),
        (o_ldn, old_l_dn, o_rdn, old_r_dn, o_ndn, wdn, dn, 0),
    )):
        for m in range(NX):
            lanes = slice(D * m, D * m + D)
            fresh = XEi[m, u, :, 0:D][0:12].astype(F32)
            o_stat[:, lanes] = 0.5 * old_stat[:, lanes] + 0.5 * fresh
        side = total(*[XEi[m, u, :, 2 * D : 2 * D + 192] for m in range(NX)])
        o_side[...] = 0.5 * old_side[...] + 0.5 * side[0:12]
        step = total(*[XEi[m, u, :, D : 2 * D] for m in range(NX)])
        step = dot(step, root[0:D, :], 1, dim, HIGH)
        o_new[...] = weight[...] - 0.5 * step[0:12]

    arrived(c_lay)
    arrived(c_grad)
    for copy in own_out:
        copy.wait()
    settle(list(started))

    @pl.when(x == y)
    def _():
        for i in range(1, NX):
            j_copy(i).wait_send()


def finish(
    rlay, rgrad, grads, norm, second, *refs
):
    handed = (len(refs) - 5) // 2
    sources, outs = refs[:handed], refs[handed:]
    o_layer, o_gimg, o_grad, o_second, o_norm = outs[handed:]
    for src, dst in zip(sources, outs):
        dst[...] = src[...]

    def of_patch(row, col):
        image = row & 7
        pair, second_one = image >> 1, image & 1
        return col == PAIR * pair + PATCHES * second_one + (row >> 3)

    chooser = pick(8 * PATCHES, NX * PAIR, of_patch)
    o_layer[...] = dot(chooser, rlay[...].reshape(NX * PAIR, D)).astype(BF)
    o_gimg[...] = dot(chooser, rgrad[...].reshape(NX * PAIR, D))
    for j in range(4):
        row = slice(j, j + 1)
        grad = jnp.concatenate([grads[2 * j : 2 * j + 1, :], grads[2 * j + 1 : 2 * j + 2, :]], axis=1)
        fresh = 0.5 * second[row, :] + 0.5 * grad * grad
        o_grad[row, :] = grad
        o_second[row, :] = fresh
        o_norm[row, :] = norm[row, :] - 0.5 * grad * lax.rsqrt(fresh + 1e-08)


def on_device(
    images, cotangent, image_counts, w_tok_in, w_tok_out, w_up, w_down, norm_params, biases,
    left_tok_in, right_tok_in, left_tok_out, right_tok_out, left_up, right_up, left_down, right_down,
    root_left_tok_in, root_right_tok_in, root_left_tok_out, root_right_tok_out,
    root_left_up, root_right_up, root_left_down, root_right_down, norm_second, bias_second,
):
    patch_rows = 8 * PATCHES

    def by_patch(v):
        return v.transpose(1, 0, 2).reshape(patch_rows, D)

    def by_image(v):
        return v.reshape(PATCHES, 8, D).transpose(1, 0, 2)

    args = (
        image_counts, by_patch(images), by_patch(cotangent), w_tok_in.T, w_tok_out, w_up.T, w_down,
        norm_params, jnp.pad(biases, (0, NB_ROW - NB)).reshape(1, NB_ROW),
        root_right_up.T, root_left_down, root_left_up, root_right_down,
        right_up.T, left_down, left_up, right_down,
        root_left_tok_in, root_right_tok_in, root_left_tok_out, root_right_tok_out,
        left_tok_in, right_tok_in, left_tok_out, right_tok_out,
    )
    outs = [
        ((NX, PAIR, D), BF), ((NX, PAIR, D), BF), ((12, D), F32), ((12, D), F32), ((12, D), F32),
        ((12, D), F32), ((12, DC), F32), ((12, DC), F32), ((12, 192), F32), ((12, 192), F32),
        ((8, DS), F32), ((1, NB_ROW), F32), ((6, S), F32), ((6, S), F32), ((6, S), F32), ((6, S), F32),
        ((S, S), F32), ((DS, DS), F32), ((DS, DS), F32), ((S, S), F32),
    ]

    def shapes(items):
        return [jax.ShapeDtypeStruct(shape, dtype) for shape, dtype in items]

    def vm(dtype, *shape):
        return pltpu.VMEM(shape, dtype)

    copies = 400
    scratch = [
        pltpu.SemaphoreType.DMA((copies,)), pltpu.SemaphoreType.DMA((copies,)), pltpu.SemaphoreType.DMA((4,)),
        vm(F32, 32, DC), vm(BF, 32, D), vm(BF, 16, 256),
        *[vm(BF, NX, PAIR, D) for _ in range(4)],
        vm(BF, NX, 32, D), vm(BF, NY, NZ, 96, D), vm(BF, NY, NZ, 2, 16, 256),
        vm(BF, DS, 256), vm(BF, DS, 256), vm(F32, DS, 1), vm(F32, IMG, 1), vm(F32, 16, 1, 192),
        vm(F32, 2, IMG, D), vm(BF, 2, IMG, D), vm(F32, 2, IMG, D), vm(F32, 2, DS, D), vm(BF, 2, DS, D),
        vm(BF, 4 * ROW, D), vm(BF, 4 * ROW, D), vm(F32, 4 * ROW, D), vm(F32, 4 * ROW, D),
        vm(BF, D, D), vm(BF, D, D), vm(BF, 4 * ROW, 2 * D), vm(BF, 4 * ROW, 2 * D),
        vm(BF, 2, 2 * ROW, D),
        vm(BF, NY, NZ, 96, D),
        vm(BF, 4, NX, 96, 256), vm(BF, 3, NX, 96, 256), vm(BF, 3, 96, 256), vm(BF, 3, 48, TILE),
        vm(BF, 3, NZ, 96, 256), vm(BF, 3, NZ, NY, 48, TILE), vm(BF, 3, NZ, 48, TILE), vm(BF, 3, NZ, 48, TILE),
        vm(BF, NZ, 48, 256), vm(BF, 7, 48, 256),
        vm(BF, 2, NY, NZ, 48, DS), vm(BF, NY, 48, DS), vm(BF, 2, 80, D),
        vm(BF, 2, 16, DC), vm(BF, 2, NX, 16, D),
        vm(BF, NX, 2, 16, 1792), vm(BF, NX, 2, 16, 1792),
        vm(F32, 512, DS), vm(BF, NY, NZ, 16, DS), vm(BF, 3, NZ, 16, DS), vm(BF, 7, 16, DS),
        vm(BF, NY, 16, DS), vm(BF, 2, 16, DS), vm(BF, NY, NZ, 16, DS),
    ]
    in_vmem = pl.BlockSpec(memory_space=pltpu.VMEM)
    anywhere = pl.BlockSpec(memory_space=pl.ANY)
    rlay, rgrad, *rest = pl.pallas_call(
        fused,
        out_shape=shapes(outs),
        in_specs=[pl.BlockSpec(memory_space=pltpu.SMEM)]
        + [anywhere if i in (11, 12) else in_vmem for i in range(1, len(args))],
        out_specs=[anywhere, anywhere] + [in_vmem] * (len(outs) - 2),
        scratch_shapes=scratch,
        compiler_params=pltpu.CompilerParams(
            collective_id=0, has_side_effects=True, vmem_limit_bytes=64 * 2**20
        ),
        name="fused",
    )(*args)
    handed = rest[:8] + rest[10:]
    handed_outs = outs[2:10] + outs[12:]
    own_outs = [((patch_rows, D), BF), ((patch_rows, D), F32)] + [((4, D), F32)] * 3
    (
        gup, gdn, nup, ndn, rup, ldn, lup, rdn, gti, gto, nti, nto, lti, rti, lto, rto,
        layer, gimg, norm_grad, norm_second_new, norm_new,
    ) = pl.pallas_call(
        finish,
        out_shape=shapes(handed_outs + own_outs),
        in_specs=[in_vmem] * (5 + len(handed)),
        out_specs=[in_vmem] * (5 + len(handed)),
        compiler_params=pltpu.CompilerParams(vmem_limit_bytes=64 * 2**20),
        name="finish",
    )(rlay, rgrad, rest[8], norm_params, norm_second, *handed)

    bias_grad = rest[9].reshape(NB_ROW)[:NB]
    bias_second_new = 0.5 * bias_second + 0.5 * bias_grad * bias_grad
    bias_new = biases - 0.5 * bias_grad * lax.rsqrt(bias_second_new + 1e-08)
    return (
        by_image(layer), by_image(gimg), gti.T, gto, gup.T, gdn, nti.T, nto, nup.T, ndn,
        lti, rti, lto, rto, lup, rup.T, ldn, rdn,
        norm_grad, norm_second_new, norm_new, bias_grad, bias_second_new, bias_new,
    )


def solution(mesh):
    both, dp, rest = ("dp", "mix"), "dp", P()
    in_specs = (
        P(dp, "mix", None), P(dp, "mix", None), P(dp), P(None, dp), P(dp, None), P(None, both), P(both, None),
        rest, rest, rest, rest, rest, rest,
        P(dp, "mix"), P(None, both), P(both, None), P(dp, "mix"),
        rest, rest, rest, rest, rest, P(None, both), P(both, None), rest, rest, rest,
    )
    out_specs = (
        P(dp, "mix", None), P(dp, "mix", None), P(None, dp), P(dp, None), P(None, both), P(both, None),
        P(None, dp), P(dp, None), P(None, both), P(both, None),
        rest, rest, rest, rest, P(dp, "mix"), P(None, both), P(both, None), P(dp, "mix"),
        rest, rest, rest, rest, rest, rest,
    )
    return jax.shard_map(on_device, mesh=mesh, in_specs=in_specs, out_specs=out_specs, check_vma=False)
```

```python
import jax
import jax.numpy as jnp
from jax import lax
from jax.experimental import pallas as pl
from jax.experimental.pallas import tpu as pltpu
from jax.sharding import PartitionSpec as P

MESH = pl.DeviceIdType.MESH
BF = jnp.bfloat16
F32 = jnp.float32
HIGH = lax.Precision.HIGHEST

D = 768
DC = 3072
DS = 384
S = 196
NX, NY, NZ = 4, 4, 8
EPS = 1e-06
PER_IMAGE = 1.0 / 512.0
PATCHES = 49
NUM_LATE = 16
PAIR = 112
IMG = 256
ROW = 208
HALF = D // 2
NB = 4420
TILE = 128
P0, P1, P2 = slice(0, 256), slice(256, 512), slice(512, 768)
FAR_FIRST = (4, 5, 3, 6, 2, 7, 1, 0)
NEAR, FAR = (0, 7, 1, 2), (6, 3, 5, 4)


def dot(left, right, left_dim=1, right_dim=0, precision=None):
    return lax.dot_general(
        left,
        right,
        (((left_dim,), (right_dim,)), ((), ())),
        preferred_element_type=F32,
        precision=precision,
    )


def pick(rows, cols, rule):
    row = lax.broadcasted_iota(jnp.int32, (rows, cols), 0)
    col = lax.broadcasted_iota(jnp.int32, (rows, cols), 1)
    return jnp.where(rule(row, col), 1.0, 0.0).astype(BF)


def ge(values, bound):
    return (values >= bound).astype(jnp.int32)


def gelu_and_slope(v):
    t = pl.reciprocal(1.0 + 0.23164188 * jnp.abs(v))
    e = jnp.exp(-0.5 * v * v)
    q = 0.5 * t * (
        0.254829592 + t * (-0.284496736 + t * (1.421413741 + t * (-1.453152027 + t * 1.061405429)))
    ) * e
    cdf = jnp.where(v >= 0, 1.0 - q, q)
    return v * cdf, cdf + v * e * 0.3989422804014327


def normalise(v):
    mean = jnp.mean(v, axis=-1, keepdims=True)
    centre = v - mean
    r = lax.rsqrt(jnp.mean(centre * centre, axis=-1, keepdims=True) + EPS)
    return centre * r, r


def normalise_back(xhat, r, dh, gain):
    dxh = dh * gain
    m1 = jnp.mean(dxh, axis=-1, keepdims=True)
    m2 = jnp.mean(dxh * xhat, axis=-1, keepdims=True)
    dv = r * (dxh - m1 - xhat * m2)
    return dv, jnp.sum(dh * xhat, axis=0, keepdims=True), jnp.sum(dh, axis=0, keepdims=True)


def fused(
    count, img, cot_far, tin, tout, wup, wdn, norm, bias, *refs
):
    late = refs[:NUM_LATE]
    (
        rlay, rgrad, o_gup, o_gdn, o_nup, o_ndn, o_rup, o_ldn, o_lup, o_rdn,
        o_norm, o_bias, o_gti, o_gto, o_nti, o_nto, o_lti, o_rti, o_lto, o_rto,
        ssem, rsem, lsem, stage, wst, tst, simg, scot, rimg, rcot,
        xw, W, tk, tokin, tokout, bti, bto, bup, brow, ximg, normed, mid, slope, act, n2, mb, br, dn,
        upc, dnc, actb, dpb, xbi, G, RAr, RAl, XA, YA, XB, YB, YC, XD, PZ, RZ,
        HQ, UJQ, UJP, qst, Qx, XEo, XEi, SM, SB, SX, SZ, SY, SC, SF,
        cot, q_up, p_dn, old_r_up, old_l_dn, old_l_up, old_r_dn,
        pl_ti, pr_ti, pl_to, pr_to, ol_ti, or_ti, ol_to, or_to,
    ) = refs[NUM_LATE:]
    loaded = (
        q_up, p_dn, None, None, old_r_up, old_l_dn, old_l_up, old_r_dn,
        pl_ti, pr_ti, pl_to, pr_to, ol_ti, or_ti, ol_to, or_to,
    )
    dp = lax.axis_index("dp")
    x = lax.axis_index("mix")
    c = lax.rem(dp, 2)
    y = dp // (2 * NZ)
    z = lax.rem(dp // 2, NZ)

    def X(i):
        return lax.rem(x + i + NX, NX)

    def Y(i):
        return lax.rem(y + i + NY, NY)

    def Z(i):
        return lax.rem(z + i + NZ, NZ)

    def dev(xx, yy, zz, cc):
        return ((yy * NZ + zz) * 2 + cc, xx)

    to_x = [None] + [dev(X(i), y, z, c) for i in range(1, NX)]
    to_y = [None] + [dev(x, Y(i), z, c) for i in range(1, NY)]
    to_z = [None] + [dev(x, y, Z(i), c) for i in range(1, NZ)]
    sibling = dev(x, y, z, 1 - c)
    started = []
    used = [0]

    def put(src, dst, device):
        k = used[0]
        used[0] += 1
        copy = pltpu.make_async_remote_copy(
            src_ref=src, dst_ref=dst, send_sem=ssem.at[k], recv_sem=rsem.at[k],
            device_id=device, device_id_type=MESH,
        )
        copy.start()
        started.append(copy)
        return copy

    def arrived(copies):
        for copy in copies:
            copy.wait_recv()

    def settle(copies):
        for copy in copies:
            copy.wait_send()
        started[:] = [item for item in started if not any(item is copy for copy in copies)]

    def total(*parts):
        value = parts[0].astype(F32)
        for part in parts[1:]:
            value = value + part.astype(F32)
        return value

    barrier = pltpu.get_barrier_semaphore()
    peers = to_x[1:] + to_y[1:] + to_z[1:] + [sibling]
    for peer in peers:
        pl.semaphore_signal(barrier, inc=1, device_id=peer, device_id_type=MESH)

    get_cot = pltpu.make_async_copy(cot_far, cot, lsem.at[0])
    get_cot.start()
    loads = [None] * NUM_LATE
    for k in (0, 1, *range(4, NUM_LATE)):
        loads[k] = pltpu.make_async_copy(late[k], loaded[k], lsem.at[4 + k])
        loads[k].start()

    stage[:, 0 : 2 * D] = jnp.zeros((32, 2 * D), F32)
    stage[0:12, 0:D] = wup[...]
    stage[16:28, 0:D] = wdn[...]
    stage[0:6, D : D + S] = tin[...]
    stage[8:14, D : D + S] = tout[...]
    wst[...] = stage[:, 0:D].astype(BF)
    tst[...] = stage[0:16, D : D + 256].astype(BF)
    xw[x] = wst[...]
    tk[y, z, c] = tst[...]

    pl.semaphore_wait(barrier, len(peers))
    c_xw = [put(wst, xw.at[x], to_x[i]) for i in range(1, NX)]
    c_tz = [put(tk.at[y, z, c], tk.at[y, z, c], to_z[i]) for i in range(1, NZ)]

    def of_pairs(row, col):
        m = ge(row, PAIR) + ge(row, 2 * PAIR) + ge(row, 3 * PAIR)
        i = row - PAIR * m
        second = ge(i, PATCHES)
        return (col == (i - PATCHES * second) * 8 + 2 * m + second) & (i < 2 * PATCHES)

    chooser = pick(NX * PAIR, 8 * PATCHES, of_pairs)
    simg[...] = dot(chooser, img[...]).astype(BF).reshape(NX, PAIR, D)
    c_img = [put(simg.at[X(i)], rimg.at[x], to_x[i]) for i in range(1, NX)]
    get_cot.wait()
    scot[...] = dot(chooser, cot[...]).astype(BF).reshape(NX, PAIR, D)
    c_cot = [put(scot.at[X(i)], rcot.at[x], to_x[i]) for i in range(1, NX)]

    arrived(c_xw)

    def of_shards(row, col):
        m, j = col >> 5, col & 31
        up = (j < 12) & (row == 12 * m + j)
        down = (j >= 16) & (j < 28) & (row == 32 + 12 * m + j)
        return up | down

    upc[0:96, :] = dot(pick(96, 128, of_shards), xw[...].reshape(128, D)).astype(BF)
    W[y, z, :, 0:512] = upc[0:96, 0:512]

    def rows_of(q):
        return pl.ds(pl.multiple_of(48 * (q // 2), 16), 48)

    def lanes_of(q, part):
        return pl.ds(pl.multiple_of(256 * part + TILE * lax.rem(q, 2), TILE), TILE)

    a_right, a_left, b_right, b_left, b_y = {}, {}, {}, {}, {}

    def a_send(step, d, right):
        if right:
            ref = W.at[Y(-d), Z(1 - step), :, P0]
            a_right[step, d] = put(ref, ref, to_z[1])
        else:
            ref = W.at[Y(-d), Z(step - 1), :, P0]
            a_left[step, d] = put(ref, ref, to_z[7])

    def b_send(step, right):
        if right:
            ref = W.at[y, Z(1 - step), :, P1]
            b_right[step] = put(ref, ref, to_z[1])
        else:
            ref = W.at[y, Z(step - 1), :, P1]
            b_left[step] = put(ref, ref, to_z[7])

    def b_spread(offset):
        ref = W.at[y, Z(offset), :, P1]
        b_y[offset] = [put(ref, ref, to_y[i]) for i in range(1, NY)]

    def c_ref(yy, zz):
        return W.at[yy, zz, rows_of(x), lanes_of(x, 2)]

    def c_part(k, i):
        return W.at[:, Z(k), rows_of(X(i)), lanes_of(X(i), 2)]

    W[y, z, rows_of(x), lanes_of(x, 2)] = upc[rows_of(x), lanes_of(x, 2)]
    own_a = W.at[y, z, :, P0]
    def c_send_y(k):
        ref = c_ref(y, Z(k))
        c_y[k] = [put(ref, ref, to_y[i]) for i in range(1, NY)]

    c_z, c_y = {}, {}
    for i in (1, 7, 6, 2, 5, 3, 4):
        c_z[i] = put(c_ref(y, z), c_ref(y, z), to_z[i])
    b_send(1, True)
    b_send(1, False)
    c_ay = [None] + [put(own_a, own_a, to_y[i]) for i in range(1, NY)]
    c_send_y(0)
    a_send(1, 0, True)
    a_send(1, 0, False)
    b_spread(0)

    rimg[x] = simg[x]
    rcot[x] = scot[x]
    diagonal = pick(TILE, TILE, lambda row, col: row == col).astype(F32)
    brow[...] = bias[...].reshape(1, NB)

    def column(first):
        spread = jnp.broadcast_to(brow[:, first : first + TILE], (TILE, TILE))
        return jnp.sum(spread * diagonal, axis=1, keepdims=True)

    for j in range(3):
        bti[TILE * j : TILE * j + TILE, :] = column(TILE * j)
    for j in range(2):
        bto[TILE * j : TILE * j + TILE, :] = column(DS + TILE * j)
    for d in (1, 3, 2):
        c_ay[d].wait_recv()
        a_send(1, d, True)
        a_send(1, d, False)
    arrived(c_tz)
    c_ty = [put(tk.at[y, :, c], tk.at[y, :, c], to_y[i]) for i in range(1, NY)]
    x_right, x_left, x_on, x_far = {}, {}, {}, []
    for k in NEAR[1:]:
        c_z[NZ - k].wait_recv()
        c_send_y(k)

    def gather_step(step):
        b_right[step].wait_recv()
        if step < 4:
            b_send(step + 1, True)
        b_spread(-step)
        if step < 4:
            b_left[step].wait_recv()
            if step < 3:
                b_send(step + 1, False)
            b_spread(step)
        if step < 4:
            for d in (0, 1, 3, 2):
                a_right[step, d].wait_recv()
                if step < 3 or d < 2:
                    a_send(step + 1, d, True)
                a_left[step, d].wait_recv()
                if step < 3 or d > 1:
                    a_send(step + 1, d, False)

    gather_step(1)
    for k in FAR:
        c_z[NZ - k].wait_recv()
        c_send_y(k)
    arrived(c_ty)
    c_tc = put(tk.at[:, :, c], tk.at[:, :, c], sibling)
    for k in NEAR:
        arrived(c_y[k])
        x_right[k] = put(c_part(k, 0), c_part(k, 0), to_x[1])
        x_left[k] = put(c_part(k, 0), c_part(k, 0), to_x[3])
    for zz in range(NZ):
        for cc in range(2):
            first = [DS + S + 48 * ((yy * NZ + zz) * 2 + cc) for yy in range(NY)]
            bup[2 * zz + cc] = jnp.concatenate([brow[:, f : f + 48] for f in first], axis=1)
    bias_down = brow[:, DS + S + DC : NB]

    c_tc.wait_recv()

    def of_group(row, col):
        group, i = col >> 4, col & 15
        first = (i < 6) & (row == 6 * group + i)
        second = (i >= 8) & (i < 14) & (row == 40 + 6 * group + i)
        return first | second

    chooser = pick(96, 128, of_group)
    for g in range(8):
        part = tk[g // 2, 4 * (g % 2) : 4 * (g % 2) + 4].reshape(128, 256)
        part = dot(chooser, part).astype(BF)
        tokin[48 * g : 48 * g + 48, :] = part[0:48]
        tokout[48 * g : 48 * g + 48, :] = part[48:96]

    arrived(c_img)
    arrived(c_cot)
    keep = [jnp.where(2 * x + b < count[0], 1.0, 0.0).astype(F32) for b in range(2)]
    own = c * (2 * ROW)

    def own_rows(b):
        return pl.ds(pl.multiple_of(own + b * ROW, 16), ROW)

    both = pl.ds(pl.multiple_of(own, 16), 2 * ROW)

    def of_images(row, col):
        b = ge(row, IMG)
        i = row - IMG * b
        part = ge(i, 49) + ge(i, 98) + ge(i, 147)
        return (col == 63 * part + 49 * b + i) & (i < S)

    chooser = pick(2 * IMG, NX * PAIR, of_images)
    ximg[...] = dot(chooser, rimg[...].reshape(NX * PAIR, D)).reshape(2, IMG, D)
    back = dot(chooser, rcot[...].reshape(NX * PAIR, D))
    for b in range(2):
        mb[own_rows(b), :] = (back[b * IMG : b * IMG + ROW] * keep[b]).astype(BF)
        xhat, _ = normalise(ximg[b])
        normed[b] = (xhat * norm[0:1, :] + norm[1:2, :]).astype(BF)
    c_mb = put(mb.at[both], mb.at[both], sibling)
    for k in FAR:
        arrived(c_y[k])
        x_far += [put(c_part(k, 0), c_part(k, 0), to_x[i]) for i in range(1, NX)]
    gather_step(2)

    @pl.loop(0, 2)
    def _(b):
        pre = dot(tokin[...], normed[b]) + bti[...]
        value, grad = gelu_and_slope(pre)
        slope[b] = grad
        act[b] = value.astype(BF)
        mixed = dot(tokout[...], act[b], 0, 0) + bto[...]
        middle = ximg[b] + mixed.astype(BF).astype(F32)
        mid[b] = middle
        xhat, _ = normalise(middle[0:ROW])
        n2[own_rows(b), :] = (xhat * norm[2:3, :] + norm[3:4, :]).astype(BF)

    c_n2 = put(n2.at[both], n2.at[both], sibling)
    for k in NEAR:
        if k < 2:
            x_right[k].wait_recv()
            x_on[k] = put(c_part(k, 3), c_part(k, 3), to_x[1])
        else:
            x_left[k].wait_recv()
            x_on[k] = put(c_part(k, 1), c_part(k, 1), to_x[3])
    gather_step(3)
    gather_step(4)
    c_mb.wait_recv()
    c_n2.wait_recv()

    def channel_pass(half):
        offsets = FAR_FIRST[4 * half : 4 * half + 4]
        for j, k in enumerate(offsets):
            upc[192 * j : 192 * j + 192, :] = W[:, Z(k), 0:48, :].reshape(192, D)
            dnc[192 * j : 192 * j + 192, :] = W[:, Z(k), 48:96, :].reshape(192, D)
        row = jnp.concatenate([bup[2 * Z(k) + c] for k in offsets], axis=1)
        lanes = slice(half * D, half * D + D)

        @pl.loop(0, 2)
        def _(r):
            rows = pl.ds(pl.multiple_of(r * (2 * ROW), 16), 2 * ROW)
            pre = dot(n2[rows, :], upc[...], 1, 1) + row
            value, grad = gelu_and_slope(pre)
            low = value.astype(BF)
            actb[rows, lanes] = low
            part = dot(low, dnc[...])
            br[rows, :] = part if half == 1 else br[rows, :] + part
            low = (grad * dot(mb[rows, :], dnc[...], 1, 1)).astype(BF)
            dpb[rows, lanes] = low
            part = dot(low, upc[...])
            dn[rows, :] = part if half == 1 else dn[rows, :] + part

    ra, la, xb, yb, yc, xd, rz = {}, {}, {}, {}, {}, {}, {}

    def gradients(pair):
        lanes = slice(2 * 192 * pair, 2 * 192 * pair + 384)
        offsets = FAR_FIRST[2 * pair : 2 * pair + 2]
        for u, (left, right) in enumerate(((dpb, n2), (actb, mb))):
            grad = dot(left[:, lanes], right[...], 0, 0).astype(BF)
            for j, k in enumerate(offsets):
                part = grad[192 * j : 192 * j + 192].reshape(4, 48, D)
                G[:, Z(k), 48 * u : 48 * u + 48, :] = part
        for k in offsets:
            for i in range(1, NX):
                xb[k, i] = put(G.at[X(i), Z(k), :, P1], XB.at[i - 1, Z(k)], to_x[i])
                ref = G.at[:, Z(k), rows_of(Y(i)), lanes_of(Y(i), 2)]
                yb[k, i] = put(ref, YB.at[i - 1, Z(k)], to_y[i])

    def a_reduce(step, ws):
        for w in ws:
            first = 1 if w < 2 else 2
            if step >= first:
                ref = G.at[X(w), Z(5 - step), :, P0]
                if step > first:
                    ra[step - 1, w].wait_recv()
                    ref[...] = total(ref[...], RAr[step - 2, w]).astype(BF)
                ra[step, w] = put(ref, RAr.at[step - 1, w], to_z[1])
            first = 2 if w < 2 else 1
            if step >= first:
                ref = G.at[X(w), Z(step - 5), :, P0]
                if step > first:
                    la[step - 1, w].wait_recv()
                    ref[...] = total(ref[...], RAl[step - 2, w]).astype(BF)
                la[step, w] = put(ref, RAl.at[step - 1, w], to_z[7])

    def second(k):
        arrived([xb[k, i] for i in range(1, NX)])
        ref = G.at[x, Z(k), :, P1]
        ref[...] = total(ref[...], *[XB[i, Z(k)] for i in range(NX - 1)]).astype(BF)
        for i in range(1, NY):
            ref = G.at[x, Z(k), rows_of(Y(i)), lanes_of(Y(i), 1)]
            yc[k, i] = put(ref, YC.at[i - 1, Z(k)], to_y[i])
        arrived([yb[k, i] for i in range(1, NY)])
        ref = G.at[:, Z(k), rows_of(y), lanes_of(y, 2)]
        ref[...] = total(ref[...], *[YB[i, Z(k)] for i in range(NY - 1)]).astype(BF)
        for i in range(1, NX):
            ref = G.at[X(i), Z(k), rows_of(y), lanes_of(y, 2)]
            xd[k, i] = put(ref, XD.at[i - 1, Z(k)], to_x[i])

    def third(k):
        arrived([yc[k, i] for i in range(1, NY)])
        value = G[x, Z(k), rows_of(y), lanes_of(y, 1)]
        PZ[Z(k), :, 0:TILE] = total(value, *[YC[i, Z(k)] for i in range(NY - 1)]).astype(BF)
        arrived([xd[k, i] for i in range(1, NX)])
        value = G[x, Z(k), rows_of(y), lanes_of(y, 2)]
        PZ[Z(k), :, TILE : 2 * TILE] = total(value, *[XD[i, Z(k)] for i in range(NX - 1)]).astype(BF)
        if k > 0:
            rz[k] = put(PZ.at[Z(k)], RZ.at[k - 1], to_z[k])

    for offset in (0, -1, 1, 2):
        arrived(b_y[offset])
    for k in NEAR:
        arrived([x_left[k] if k < 2 else x_right[k], x_on[k]])
    loads[0].wait()
    loads[1].wait()
    stage[0:12, :] = q_up[...]
    stage[12:16, :] = jnp.zeros((4, DC), F32)
    stage[16:28, :] = p_dn[...]
    stage[28:32, :] = jnp.zeros((4, DC), F32)
    qst[0] = stage[0:16, :].astype(BF)
    qst[1] = stage[16:32, :].astype(BF)
    Qx[:, x] = qst[:, :, pl.ds(pl.multiple_of(x * D, D), D)]
    c_q = [
        put(qst.at[:, :, pl.ds(pl.multiple_of(X(i) * D, D), D)], Qx.at[:, x], to_x[i])
        for i in range(1, NX)
    ]
    channel_pass(1)
    gradients(2)
    gradients(3)
    for offset in (-2, 3, -3, -4):
        arrived(b_y[offset])
    arrived(x_far)
    for d in (0, 1, 3, 2):
        (a_right if d < 2 else a_left)[4, d].wait_recv()
    channel_pass(0)

    other = pl.ds(pl.multiple_of((1 - c) * (2 * ROW), 16), 2 * ROW)
    upc[0 : 2 * ROW, :] = dn[other, :].astype(BF)
    c_dn = put(upc.at[0 : 2 * ROW], xbi.at[1], sibling)
    dnc[0 : 2 * ROW, :] = br[other, :].astype(BF)
    c_br = put(dnc.at[0 : 2 * ROW], xbi.at[0], sibling)

    gradients(0)
    a_reduce(1, range(4))
    gradients(1)
    for k in NEAR:
        second(k)

    ones = jnp.ones((8, 4 * ROW), BF)
    up_sums = dot(ones, dpb[...])[0:1]
    down_sums = dot(ones[:, 0 : 2 * ROW], mb[both, :])
    lob, dmx = actb, dpb
    lob[0 : 2 * IMG, 0:D] = jnp.zeros((2 * IMG, D), BF)
    dmx[0 : 2 * IMG, 0:D] = jnp.zeros((2 * IMG, D), BF)
    c_dn.wait_recv()
    c_br.wait_recv()
    gain_two = jnp.zeros((1, D), F32)
    shift_two = jnp.zeros((1, D), F32)
    for b in range(2):
        here = slice(b * ROW, b * ROW + ROW)
        branch = br[own_rows(b), :] + xbi[0, here, :].astype(F32) + bias_down
        lob[b * IMG : b * IMG + ROW, 0:D] = (keep[b] * (mid[b, 0:ROW] + branch)).astype(BF)
        dh = dn[own_rows(b), :] + xbi[1, here, :].astype(F32)
        xhat, r = normalise(mid[b, 0:ROW])
        dv, gain, shift = normalise_back(xhat, r, dh, norm[2:3, :])
        gain_two = gain_two + gain
        shift_two = shift_two + shift
        back = mb[own_rows(b), :].astype(F32) + dv
        mid[b, 0:ROW] = back
        dmx[b * IMG : b * IMG + ROW, 0:D] = back.astype(BF)
        a_reduce(2, (2 * b, 2 * b + 1))

    def of_out(row, col):
        m = ge(row, PAIR) + ge(row, 2 * PAIR) + ge(row, 3 * PAIR)
        i = row - PAIR * m
        second_one = ge(i, PATCHES)
        place = (IMG - PATCHES) * second_one + PATCHES * m + i
        return (col == place) & (i < 2 * PATCHES)

    out_chooser = pick(NX * PAIR, 2 * IMG, of_out)

    def to_patches(buffer, sent):
        settle(sent)
        buffer[...] = dot(out_chooser, lob[0 : 2 * IMG, 0:D]).astype(BF).reshape(NX, PAIR, D)

    a_reduce(3, (0, 1))
    to_patches(simg, c_img)
    a_reduce(3, (2, 3))

    roots = [
        pltpu.make_async_copy(late[2], br.at[0:D], lsem.at[0]),
        pltpu.make_async_copy(late[3], dn.at[0:D], lsem.at[1]),
    ]
    for copy in roots:
        copy.start()
    gti = jnp.zeros((IMG, DS), F32)
    gto = jnp.zeros((IMG, DS), F32)
    sum_ti = jnp.zeros((8, DS), F32)
    sum_to = jnp.zeros((8, IMG), F32)
    gain_one = jnp.zeros((1, D), F32)
    shift_one = jnp.zeros((1, D), F32)
    ones = jnp.ones((8, D), BF)
    for b in range(2):
        dmixed = dmx[b * IMG : b * IMG + IMG, 0:D]
        dpre = (slope[b] * dot(tokout[...], dmixed)).astype(BF)
        gti = gti + dot(normed[b], dpre, 1, 1)
        gto = gto + dot(dmixed, act[b], 1, 1)
        sum_ti = sum_ti + dot(ones, dpre, 1, 1)
        sum_to = sum_to + dot(ones, dmixed, 1, 1)
        dnormed = dot(tokin[...], dpre, 0, 0).astype(BF).astype(F32)
        xhat, r = normalise(ximg[b, 0:ROW])
        dv, gain, shift = normalise_back(xhat, r, dnormed[0:ROW], norm[0:1, :])
        gain_one = gain_one + gain
        shift_one = shift_one + shift
        lob[b * IMG : b * IMG + ROW, 0:D] = (mid[b, 0:ROW] + dv).astype(BF)
        if b == 0:
            a_reduce(4, (0, 1))
            second(4)
            second(5)
            a_reduce(4, (2, 3))

    second(3)
    second(6)
    c_xa = []
    for w in (1, 3, 2, 0):
        ra[4, w].wait_recv()
        la[4, w].wait_recv()
        ref = G.at[X(w), z, :, P0]
        ref[...] = total(ref[...], RAr[3, w], RAl[3, w]).astype(BF)
        if w > 0:
            c_xa.append(put(ref, XA.at[w - 1], to_x[w]))
    for k in NEAR:
        third(k)

    SM[0:IMG, :] = gti
    SM[IMG : IMG + ROW, :] = gto[0:ROW]
    SM[IMG + ROW :, :] = jnp.zeros((IMG - ROW, DS), F32)
    for j, row in enumerate((gain_one, shift_one, gain_two, shift_two)):
        SM[208 + 2 * j : 209 + 2 * j, :] = row[:, 0:HALF]
        SM[209 + 2 * j : 210 + 2 * j, :] = row[:, HALF:D]
    SM[216:224, :] = sum_ti
    SM[224:232, 0:IMG] = sum_to
    SM[224:232, IMG:DS] = jnp.zeros((8, DS - IMG), F32)
    SM[232:240, :] = down_sums[:, 0:HALF]
    SM[240:248, :] = down_sums[:, HALF:D]
    for j, k in enumerate(FAR_FIRST):
        SM[pl.ds(464 + 8 * c + Z(k), 1), 0:192] = up_sums[:, 192 * j : 192 * j + 192]
    SB[...] = SM[...].reshape(NY, NZ, 16, DS).astype(BF)
    c_sx = [put(SB.at[X(i)], SX.at[i - 1], to_x[i]) for i in range(1, NX)]

    for k in (4, 5):
        third(k)
    arrived(c_xa)
    ref = G.at[x, z, :, P0]
    ref[...] = total(ref[...], XA[0], XA[1], XA[2]).astype(BF)
    c_ya = [
        put(G.at[x, z, rows_of(Y(i)), lanes_of(Y(i), 0)], YA.at[i - 1], to_y[i])
        for i in range(1, NY)
    ]
    for k in (3, 6):
        third(k)
    arrived(c_sx)
    SB[x] = total(SB[x], SX[0], SX[1], SX[2]).astype(BF)
    c_sz = [put(SB.at[x, Z(i)], SZ.at[i - 1], to_z[i]) for i in range(1, NZ)]


    hz, hy, hs = {}, {}, {}

    def h_send(lanes):
        ref = HQ.at[c, y, z, :, lanes]
        for i in (4, 3, 5, 2, 6, 1, 7):
            hz[i] = hz.get(i, []) + [put(ref, ref, to_z[i])]

    arrived(c_ya)
    mean = total(G[x, z, rows_of(y), lanes_of(y, 0)], YA[0], YA[1], YA[2]) * PER_IMAGE
    HQ[c, y, z, :, 0:TILE] = mean.astype(BF)
    h_send(slice(0, TILE))
    arrived(rz.values())
    mean = total(PZ[z], *[RZ[i] for i in range(NZ - 1)]) * PER_IMAGE
    HQ[c, y, z, :, TILE:] = mean.astype(BF)
    h_send(slice(TILE, DS))

    def h_spread(offset):
        ref = HQ.at[c, y, Z(offset)]
        hy[offset] = [put(ref, ref, to_y[i]) for i in range(1, NY)]

    def h_share(offset):
        arrived(hy[offset])
        ref = HQ.at[c, :, Z(offset)]
        hs[offset] = put(ref, ref, sibling)

    h_spread(0)
    own_out = [pltpu.make_async_copy(simg.at[x], rlay.at[x], lsem.at[2])]
    own_out[0].start()
    c_lay = [put(simg.at[X(i)], rlay.at[x], to_x[i]) for i in range(1, NX)]
    to_patches(scot, c_cot)
    own_out.append(pltpu.make_async_copy(scot.at[x], rgrad.at[x], lsem.at[3]))
    own_out[1].start()
    c_grad = [put(scot.at[X(i)], rgrad.at[x], to_x[i]) for i in range(1, NX)]
    arrived(c_sz)
    SY[y] = total(SB[x, z], *[SZ[i] for i in range(NZ - 1)]).astype(BF)
    c_sy = [put(SY.at[y], SY.at[y], to_y[i]) for i in range(1, NY)]
    for i in (1, 7, 2, 6):
        arrived(hz[i])
        h_spread(-i)
    h_share(0)

    first_j = used[0]
    used[0] += 3

    def j_copy(i):
        return pltpu.make_async_remote_copy(
            src_ref=HQ.at[c, :, z], dst_ref=UJQ, send_sem=ssem.at[first_j + i - 1],
            recv_sem=rsem.at[first_j], device_id=to_x[i], device_id_type=MESH,
        )

    @pl.when(x == y)
    def _():
        for i in range(1, NX):
            j_copy(i).start()
        UJQ[...] = HQ[c, :, z]

    arrived(c_sy)
    SC[c] = total(SY[0], SY[1], SY[2], SY[3]).astype(BF)
    c_sc = put(SC.at[c], SC.at[c], sibling)
    for i in (3, 5, 4):
        arrived(hz[i])
        h_spread(-i)
    c_sc.wait_recv()
    SF[x, z] = (total(SC[0], SC[1]) * PER_IMAGE).astype(BF)
    c_fz = [put(SF.at[x, z], SF.at[x, z], to_z[i]) for i in range(1, NZ)]
    for i in (1, 7, 2, 6):
        h_share(-i)
    @pl.when(x != y)
    def _():
        j_copy(1).wait_recv()

    def of_rows(row, col):
        m, i = row >> 4, row & 15
        return (col == 12 * m + i) & (i < 12)

    spread = pick(64, 48, of_rows)
    channels = pick(16, D, lambda row, col: (col == 12 * dp + row) & (row < 12))

    def unfold(dst, read, u):
        for t in range(2):
            value = read(2 * u + t)
            for part in range(3):
                lanes = slice(256 * part + TILE * t, 256 * part + TILE * t + TILE)
                dst[:, lanes] = value[..., TILE * part : TILE * part + TILE].reshape(-1, TILE)

    settle([c_dn, c_mb, c_n2])
    for u, out in enumerate((o_gup, o_gdn)):
        unfold(upc.at[0:48], lambda q: UJQ[q], u)
        UJP[u, 0:64] = dot(spread, upc[0:48, :]).astype(BF)
        UJP[u, 64:80] = channels
        out[...] = UJP[u, pl.ds(pl.multiple_of(16 * x, 16), 16), :][0:12].astype(F32)
    arrived(c_fz)
    c_fx = [put(SF.at[x], SF.at[x], to_x[i]) for i in range(1, NX)]
    for i in (3, 5, 4):
        h_share(-i)

    arrived([hs[offset] for offset in (0, -1, -7, -2, -6, -3, -5, -4)])
    arrived(c_q)
    c_xe = []
    for u in range(2):
        store = (n2, mb)[u]
        for zz in range(NZ):
            for cc in range(2):
                first = (2 * zz + cc) * 48
                unfold(store.at[first : first + 48], lambda q: HQ[cc, q, zz], u)
        quarter = store[0:D, :]
        right = dot(UJP[u], quarter, 1, 1)
        left = jnp.concatenate([Qx[u].reshape(64, D), right[64:80].astype(BF)], axis=0)
        left = dot(left, quarter)
        for m in range(NX):
            XEo[m, u, :, 0:D] = right[16 * m : 16 * m + 16].astype(BF)
            XEo[m, u, :, D : 2 * D] = left[16 * m : 16 * m + 16].astype(BF)
            XEo[m, u, :, 2 * D : 2 * D + 192] = left[64:80, 192 * m : 192 * m + 192].astype(BF)
            XEo[m, u, :, 2 * D + 192 : 2 * D + 256] = jnp.zeros((16, 64), BF)
        XEi[x, u] = XEo[x, u]
        c_xe.append([put(XEo.at[X(i), u], XEi.at[x, u], to_x[i]) for i in range(1, NX)])

    for copy in loads[4:]:
        copy.wait()

    arrived(c_fx)
    small = SF[...].reshape(512, DS)
    o_norm[...] = small[208:216].astype(F32)
    vector = small[208:256].astype(F32)
    ups = small[464:480].astype(F32)
    pieces = [vector[8:9], vector[16:17, 0:S]]
    for yy in range(NY):
        for zz in range(NZ):
            for cc in range(2):
                pieces.append(ups[8 * cc + zz : 8 * cc + zz + 1, 48 * yy : 48 * yy + 48])
    pieces += [vector[24:25], vector[32:33]]
    o_bias[...] = jnp.concatenate(pieces, axis=1)
    real = lax.broadcasted_iota(jnp.int32, (IMG, DS), 0) < S
    g_in = jnp.where(real, small[0:IMG].astype(F32), 0.0).astype(BF)
    g_out = jnp.where(real, small[IMG : 2 * IMG].astype(F32), 0.0).astype(BF)
    o_lti[...] = 0.5 * ol_ti[...] + 0.5 * dot(g_in, g_in, 1, 1)[0:S, 0:S]
    o_rti[...] = 0.5 * or_ti[...] + 0.5 * dot(g_in, g_in, 0, 0)
    o_lto[...] = 0.5 * ol_to[...] + 0.5 * dot(g_out, g_out, 0, 0)
    o_rto[...] = 0.5 * or_to[...] + 0.5 * dot(g_out, g_out, 1, 1)[0:S, 0:S]
    mine = pick(16, DS, lambda row, col: (col == 6 * dp + row) & (row < 6))
    o_gti[...] = dot(mine, g_in, 1, 1)[0:6, 0:S]
    o_gto[...] = dot(mine, g_out, 1, 1)[0:6, 0:S]
    mine = mine.astype(F32)
    step = dot(mine, pr_ti[...], 1, 1, HIGH)
    step = dot(step, g_in.astype(F32), 1, 1, HIGH)[:, 0:S]
    step = dot(step, pl_ti[...], 1, 1, HIGH)
    o_nti[...] = tin[...] - 0.5 * step[0:6]
    step = dot(mine, pl_to[...], 1, 0, HIGH)
    step = dot(step, g_out.astype(F32), 1, 1, HIGH)[:, 0:S]
    step = dot(step, pr_to[...], 1, 0, HIGH)
    o_nto[...] = tout[...] - 0.5 * step[0:6]

    for copy in roots:
        copy.wait()
    settle([c_br])
    upc[...] = br[0:D, :].astype(BF)
    dnc[...] = dn[0:D, :].astype(BF)
    for u, (o_stat, old_stat, o_side, old_side, o_new, weight, root, dim) in enumerate((
        (o_rup, old_r_up, o_lup, old_l_up, o_nup, wup, upc, 1),
        (o_ldn, old_l_dn, o_rdn, old_r_dn, o_ndn, wdn, dnc, 0),
    )):
        arrived(c_xe[u])
        for m in range(NX):
            lanes = slice(D * m, D * m + D)
            fresh = XEi[m, u, :, 0:D][0:12].astype(F32)
            o_stat[:, lanes] = 0.5 * old_stat[:, lanes] + 0.5 * fresh
        side = total(*[XEi[m, u, :, 2 * D : 2 * D + 192] for m in range(NX)])
        o_side[...] = 0.5 * old_side[...] + 0.5 * side[0:12]
        step = total(*[XEi[m, u, :, D : 2 * D] for m in range(NX)])
        high = step.astype(BF)
        step = jnp.concatenate([high, (step - high.astype(F32)).astype(BF)], axis=0)
        step = dot(step, root[...], 1, dim)
        o_new[...] = weight[...] - 0.5 * (step[0:12] + step[16:28])

    arrived(c_lay)
    arrived(c_grad)
    for copy in own_out:
        copy.wait()
    settle(list(started))

    @pl.when(x == y)
    def _():
        for i in range(1, NX):
            j_copy(i).wait_send()


def finish(
    rlay, rgrad, grads, bias_grad, norm, second, bias, bias_second, *refs
):
    handed = (len(refs) - 8) // 2
    sources, outs = refs[:handed], refs[handed:]
    o_layer, o_gimg, o_grad, o_second, o_norm, o_bias_grad, o_bias_second, o_bias = outs[handed:]
    for src, dst in zip(sources, outs):
        dst[...] = src[...]

    def of_patch(row, col):
        image = row & 7
        pair, second_one = image >> 1, image & 1
        return col == PAIR * pair + PATCHES * second_one + (row >> 3)

    chooser = pick(8 * PATCHES, NX * PAIR, of_patch)
    o_layer[...] = dot(chooser, rlay[...].reshape(NX * PAIR, D)).astype(BF)
    o_gimg[...] = dot(chooser, rgrad[...].reshape(NX * PAIR, D))
    for j in range(4):
        row = slice(j, j + 1)
        grad = jnp.concatenate([grads[2 * j : 2 * j + 1, :], grads[2 * j + 1 : 2 * j + 2, :]], axis=1)
        fresh = 0.5 * second[row, :] + 0.5 * grad * grad
        o_grad[row, :] = grad
        o_second[row, :] = fresh
        o_norm[row, :] = norm[row, :] - 0.5 * grad * lax.rsqrt(fresh + 1e-08)
    grad = bias_grad[...].reshape(NB)
    fresh = 0.5 * bias_second[...] + 0.5 * grad * grad
    o_bias_grad[...] = grad
    o_bias_second[...] = fresh
    o_bias[...] = bias[...] - 0.5 * grad * lax.rsqrt(fresh + 1e-08)


def on_device(
    images, cotangent, image_counts, w_tok_in, w_tok_out, w_up, w_down, norm_params, biases,
    left_tok_in, right_tok_in, left_tok_out, right_tok_out, left_up, right_up, left_down, right_down,
    root_left_tok_in, root_right_tok_in, root_left_tok_out, root_right_tok_out,
    root_left_up, root_right_up, root_left_down, root_right_down, norm_second, bias_second,
):
    patch_rows = 8 * PATCHES

    def by_patch(v):
        return v.transpose(1, 0, 2).reshape(patch_rows, D)

    def by_image(v):
        return v.reshape(PATCHES, 8, D).transpose(1, 0, 2)

    args = (
        image_counts, by_patch(images), by_patch(cotangent), w_tok_in.T, w_tok_out, w_up.T, w_down,
        norm_params, biases,
        root_right_up.T, root_left_down, root_left_up, root_right_down,
        right_up.T, left_down, left_up, right_down,
        root_left_tok_in, root_right_tok_in, root_left_tok_out, root_right_tok_out,
        left_tok_in, right_tok_in, left_tok_out, right_tok_out,
    )
    outs = [
        ((NX, PAIR, D), BF), ((NX, PAIR, D), BF), ((12, D), F32), ((12, D), F32), ((12, D), F32),
        ((12, D), F32), ((12, DC), F32), ((12, DC), F32), ((12, 192), F32), ((12, 192), F32),
        ((8, DS), F32), ((1, NB), F32), ((6, S), F32), ((6, S), F32), ((6, S), F32), ((6, S), F32),
        ((S, S), F32), ((DS, DS), F32), ((DS, DS), F32), ((S, S), F32),
    ]

    def shapes(items):
        return [jax.ShapeDtypeStruct(shape, dtype) for shape, dtype in items]

    def vm(dtype, *shape):
        return pltpu.VMEM(shape, dtype)

    copies = 400
    scratch = [
        pltpu.SemaphoreType.DMA((copies,)), pltpu.SemaphoreType.DMA((copies,)), pltpu.SemaphoreType.DMA((4 + NUM_LATE,)),
        vm(F32, 32, DC), vm(BF, 32, D), vm(BF, 16, 256),
        *[vm(BF, NX, PAIR, D) for _ in range(4)],
        vm(BF, NX, 32, D), vm(BF, NY, NZ, 96, D), vm(BF, NY, NZ, 2, 16, 256),
        vm(BF, DS, 256), vm(BF, DS, 256), vm(F32, DS, 1), vm(F32, IMG, 1), vm(F32, 16, 1, 192), vm(F32, 1, NB),
        vm(F32, 2, IMG, D), vm(BF, 2, IMG, D), vm(F32, 2, IMG, D), vm(F32, 2, DS, D), vm(BF, 2, DS, D),
        vm(BF, 4 * ROW, D), vm(BF, 4 * ROW, D), vm(F32, 4 * ROW, D), vm(F32, 4 * ROW, D),
        vm(BF, D, D), vm(BF, D, D), vm(BF, 4 * ROW, 2 * D), vm(BF, 4 * ROW, 2 * D),
        vm(BF, 2, 2 * ROW, D),
        vm(BF, NY, NZ, 96, D),
        vm(BF, 4, NX, 96, 256), vm(BF, 4, NX, 96, 256), vm(BF, 3, 96, 256), vm(BF, 3, 48, TILE),
        vm(BF, 3, NZ, 96, 256), vm(BF, 3, NZ, NY, 48, TILE), vm(BF, 3, NZ, 48, TILE), vm(BF, 3, NZ, 48, TILE),
        vm(BF, NZ, 48, 256), vm(BF, 7, 48, 256),
        vm(BF, 2, NY, NZ, 48, DS), vm(BF, NY, 48, DS), vm(BF, 2, 80, D),
        vm(BF, 2, 16, DC), vm(BF, 2, NX, 16, D),
        vm(BF, NX, 2, 16, 1792), vm(BF, NX, 2, 16, 1792),
        vm(F32, 512, DS), vm(BF, NY, NZ, 16, DS), vm(BF, 3, NZ, 16, DS), vm(BF, 7, 16, DS),
        vm(BF, NY, 16, DS), vm(BF, 2, 16, DS), vm(BF, NY, NZ, 16, DS),
        vm(BF, patch_rows, D), vm(F32, 12, DC), vm(F32, 12, DC), vm(F32, 12, DC), vm(F32, 12, DC),
        vm(F32, 12, 192), vm(F32, 12, 192),
        *[vm(F32, n, n) for n in (S, DS, DS, S, S, DS, DS, S)],
    ]
    in_vmem = pl.BlockSpec(memory_space=pltpu.VMEM)
    anywhere = pl.BlockSpec(memory_space=pl.ANY)
    rlay, rgrad, *rest = pl.pallas_call(
        fused,
        out_shape=shapes(outs),
        in_specs=[pl.BlockSpec(memory_space=pltpu.SMEM)]
        + [anywhere if i == 2 or i > 8 else in_vmem for i in range(1, len(args))],
        out_specs=[anywhere, anywhere] + [in_vmem] * (len(outs) - 2),
        scratch_shapes=scratch,
        compiler_params=pltpu.CompilerParams(
            collective_id=0, has_side_effects=True, vmem_limit_bytes=64 * 2**20
        ),
        name="fused",
    )(*args)
    handed = rest[:8] + rest[10:]
    handed_outs = outs[2:10] + outs[12:]
    own_outs = [((patch_rows, D), BF), ((patch_rows, D), F32)] + [((4, D), F32)] * 3 + [((NB,), F32)] * 3
    (
        gup, gdn, nup, ndn, rup, ldn, lup, rdn, gti, gto, nti, nto, lti, rti, lto, rto,
        layer, gimg, norm_grad, norm_second_new, norm_new, bias_grad, bias_second_new, bias_new,
    ) = pl.pallas_call(
        finish,
        out_shape=shapes(handed_outs + own_outs),
        in_specs=[in_vmem] * (8 + len(handed)),
        out_specs=[in_vmem] * (8 + len(handed)),
        compiler_params=pltpu.CompilerParams(vmem_limit_bytes=64 * 2**20),
        name="finish",
    )(rlay, rgrad, rest[8], rest[9], norm_params, norm_second, biases, bias_second, *handed)

    return (
        by_image(layer), by_image(gimg), gti.T, gto, gup.T, gdn, nti.T, nto, nup.T, ndn,
        lti, rti, lto, rto, lup, rup.T, ldn, rdn,
        norm_grad, norm_second_new, norm_new, bias_grad, bias_second_new, bias_new,
    )


def solution(mesh):
    both, dp, rest = ("dp", "mix"), "dp", P()
    in_specs = (
        P(dp, "mix", None), P(dp, "mix", None), P(dp), P(None, dp), P(dp, None), P(None, both), P(both, None),
        rest, rest, rest, rest, rest, rest,
        P(dp, "mix"), P(None, both), P(both, None), P(dp, "mix"),
        rest, rest, rest, rest, rest, P(None, both), P(both, None), rest, rest, rest,
    )
    out_specs = (
        P(dp, "mix", None), P(dp, "mix", None), P(None, dp), P(dp, None), P(None, both), P(both, None),
        P(None, dp), P(dp, None), P(None, both), P(both, None),
        rest, rest, rest, rest, P(dp, "mix"), P(None, both), P(both, None), P(dp, "mix"),
        rest, rest, rest, rest, rest, rest,
    )
    return jax.shard_map(on_device, mesh=mesh, in_specs=in_specs, out_specs=out_specs, check_vma=False)
```

```python
import jax
import jax.numpy as jnp
from jax import lax
from jax.experimental import pallas as pl
from jax.experimental.pallas import tpu as pltpu
from jax.sharding import PartitionSpec as P

MESH = pl.DeviceIdType.MESH
BF = jnp.bfloat16
F32 = jnp.float32
HIGH = lax.Precision.HIGHEST

D = 768
DC = 3072
DS = 384
S = 196
NX, NY, NZ = 4, 4, 8
EPS = 1e-06
PER_IMAGE = 1.0 / 512.0
PATCHES = 49
NUM_LATE = 16
PAIR = 112
IMG = 256
ROW = 208
HALF = D // 2
NB = 4420
TILE = 128
P0, P1, P2 = slice(0, 256), slice(256, 512), slice(512, 768)
FAR_FIRST = (4, 5, 3, 6, 2, 7, 1, 0)
NEAR, FAR = (0, 7, 1, 2), (6, 3, 5, 4)


def dot(left, right, left_dim=1, right_dim=0, precision=None):
    return lax.dot_general(
        left,
        right,
        (((left_dim,), (right_dim,)), ((), ())),
        preferred_element_type=F32,
        precision=precision,
    )


def pick(rows, cols, rule):
    row = lax.broadcasted_iota(jnp.int32, (rows, cols), 0)
    col = lax.broadcasted_iota(jnp.int32, (rows, cols), 1)
    return jnp.where(rule(row, col), 1.0, 0.0).astype(BF)


def ge(values, bound):
    return (values >= bound).astype(jnp.int32)


def gelu_and_slope(v):
    t = pl.reciprocal(1.0 + 0.23164188 * jnp.abs(v))
    e = jnp.exp(-0.5 * v * v)
    q = 0.5 * t * (
        0.254829592 + t * (-0.284496736 + t * (1.421413741 + t * (-1.453152027 + t * 1.061405429)))
    ) * e
    cdf = jnp.where(v >= 0, 1.0 - q, q)
    return v * cdf, cdf + v * e * 0.3989422804014327


def normalise(v):
    mean = jnp.mean(v, axis=-1, keepdims=True)
    centre = v - mean
    r = lax.rsqrt(jnp.mean(centre * centre, axis=-1, keepdims=True) + EPS)
    return centre * r, r


def normalise_back(xhat, r, dh, gain):
    dxh = dh * gain
    m1 = jnp.mean(dxh, axis=-1, keepdims=True)
    m2 = jnp.mean(dxh * xhat, axis=-1, keepdims=True)
    dv = r * (dxh - m1 - xhat * m2)
    return dv, jnp.sum(dh * xhat, axis=0, keepdims=True), jnp.sum(dh, axis=0, keepdims=True)


def fused(
    count, img, cot_far, tin, tout, wup, wdn, norm, bias, *refs
):
    late = refs[:NUM_LATE]
    (
        rlay, rgrad, o_gup, o_gdn, o_nup, o_ndn, o_rup, o_ldn, o_lup, o_rdn,
        o_norm, o_bias, o_gti, o_gto, o_nti, o_nto, o_lti, o_rti, o_lto, o_rto,
        ssem, rsem, lsem, stage, wst, tst, simg, scot, rimg, rcot,
        xw, W, tk, tokin, tokout, bti, bto, bup, brow, ximg, normed, mid, slope, act, n2, mb, br, dn,
        upc, dnc, actb, dpb, xbi, G, RAr, RAl, XA, YA, XB, YB, YC, XD, PZ, RZ,
        HQ, UJQ, UJP, qst, Qx, XEo, XEi, SM, SB, SX, SZ, S8, SF,
        cot, q_up, p_dn, old_r_up, old_l_dn, old_l_up, old_r_dn,
        pl_ti, pr_ti, pl_to, pr_to, ol_ti, or_ti, ol_to, or_to,
    ) = refs[NUM_LATE:]
    loaded = (
        q_up, p_dn, None, None, old_r_up, old_l_dn, old_l_up, old_r_dn,
        pl_ti, pr_ti, pl_to, pr_to, ol_ti, or_ti, ol_to, or_to,
    )
    dp = lax.axis_index("dp")
    x = lax.axis_index("mix")
    c = lax.rem(dp, 2)
    y = dp // (2 * NZ)
    z = lax.rem(dp // 2, NZ)

    def X(i):
        return lax.rem(x + i + NX, NX)

    def Y(i):
        return lax.rem(y + i + NY, NY)

    def Z(i):
        return lax.rem(z + i + NZ, NZ)

    def dev(xx, yy, zz, cc):
        return ((yy * NZ + zz) * 2 + cc, xx)

    to_x = [None] + [dev(X(i), y, z, c) for i in range(1, NX)]
    to_y = [None] + [dev(x, Y(i), z, c) for i in range(1, NY)]
    to_z = [None] + [dev(x, y, Z(i), c) for i in range(1, NZ)]
    sibling = dev(x, y, z, 1 - c)
    started = []
    used = [0]

    def put(src, dst, device):
        k = used[0]
        used[0] += 1
        copy = pltpu.make_async_remote_copy(
            src_ref=src, dst_ref=dst, send_sem=ssem.at[k], recv_sem=rsem.at[k],
            device_id=device, device_id_type=MESH,
        )
        copy.start()
        started.append(copy)
        return copy

    def arrived(copies):
        for copy in copies:
            copy.wait_recv()

    def settle(copies):
        for copy in copies:
            copy.wait_send()
        started[:] = [item for item in started if not any(item is copy for copy in copies)]

    def total(*parts):
        value = parts[0].astype(F32)
        for part in parts[1:]:
            value = value + part.astype(F32)
        return value

    barrier = pltpu.get_barrier_semaphore()
    to_same = [dev(x, Y(i), z, cc) for i in range(NY) for cc in (c, 1 - c)][1:]
    peers = to_x[1:] + to_z[1:] + to_same
    for peer in peers:
        pl.semaphore_signal(barrier, inc=1, device_id=peer, device_id_type=MESH)

    get_cot = pltpu.make_async_copy(cot_far, cot, lsem.at[0])
    get_cot.start()
    loads = [None] * NUM_LATE
    for k in (0, 1, *range(4, NUM_LATE)):
        loads[k] = pltpu.make_async_copy(late[k], loaded[k], lsem.at[4 + k])
        loads[k].start()

    stage[:, 0 : 2 * D] = jnp.zeros((32, 2 * D), F32)
    stage[0:12, 0:D] = wup[...]
    stage[16:28, 0:D] = wdn[...]
    stage[0:6, D : D + S] = tin[...]
    stage[8:14, D : D + S] = tout[...]
    wst[...] = stage[:, 0:D].astype(BF)
    tst[...] = stage[0:16, D : D + 256].astype(BF)
    xw[x] = wst[...]
    tk[y, z, c] = tst[...]

    pl.semaphore_wait(barrier, len(peers))
    c_xw = [put(wst, xw.at[x], to_x[i]) for i in range(1, NX)]
    c_tz = [put(tk.at[y, z, c], tk.at[y, z, c], to_z[i]) for i in range(1, NZ)]

    def of_pairs(row, col):
        m = ge(row, PAIR) + ge(row, 2 * PAIR) + ge(row, 3 * PAIR)
        i = row - PAIR * m
        second = ge(i, PATCHES)
        return (col == (i - PATCHES * second) * 8 + 2 * m + second) & (i < 2 * PATCHES)

    chooser = pick(NX * PAIR, 8 * PATCHES, of_pairs)
    simg[...] = dot(chooser, img[...]).astype(BF).reshape(NX, PAIR, D)
    c_img = [put(simg.at[X(i)], rimg.at[x], to_x[i]) for i in range(1, NX)]
    get_cot.wait()
    scot[...] = dot(chooser, cot[...]).astype(BF).reshape(NX, PAIR, D)
    c_cot = [put(scot.at[X(i)], rcot.at[x], to_x[i]) for i in range(1, NX)]

    arrived(c_xw)

    def of_shards(row, col):
        m, j = col >> 5, col & 31
        up = (j < 12) & (row == 12 * m + j)
        down = (j >= 16) & (j < 28) & (row == 32 + 12 * m + j)
        return up | down

    upc[0:96, :] = dot(pick(96, 128, of_shards), xw[...].reshape(128, D)).astype(BF)
    W[y, z, :, 0:512] = upc[0:96, 0:512]

    def rows_of(q):
        return pl.ds(pl.multiple_of(48 * (q // 2), 16), 48)

    def lanes_of(q, part):
        return pl.ds(pl.multiple_of(256 * part + TILE * lax.rem(q, 2), TILE), TILE)

    a_right, a_left, b_right, b_left, b_y = {}, {}, {}, {}, {}

    def a_send(step, d, right):
        if right:
            ref = W.at[Y(-d), Z(1 - step), :, P0]
            a_right[step, d] = put(ref, ref, to_z[1])
        else:
            ref = W.at[Y(-d), Z(step - 1), :, P0]
            a_left[step, d] = put(ref, ref, to_z[7])

    def b_send(step, right):
        if right:
            ref = W.at[y, Z(1 - step), :, P1]
            b_right[step] = put(ref, ref, to_z[1])
        else:
            ref = W.at[y, Z(step - 1), :, P1]
            b_left[step] = put(ref, ref, to_z[7])

    def b_spread(offset):
        ref = W.at[y, Z(offset), :, P1]
        b_y[offset] = [put(ref, ref, to_y[i]) for i in range(1, NY)]

    def c_ref(yy, zz):
        return W.at[yy, zz, rows_of(x), lanes_of(x, 2)]

    def c_part(k):
        return W.at[:, Z(k), rows_of(x), lanes_of(x, 2)]

    W[y, z, rows_of(x), lanes_of(x, 2)] = upc[rows_of(x), lanes_of(x, 2)]
    own_a = W.at[y, z, :, P0]
    def c_send_y(k):
        ref = c_ref(y, Z(k))
        c_y[k] = [put(ref, ref, to_y[i]) for i in range(1, NY)]

    c_z, c_y = {}, {}
    for i in (1, 7, 6, 2, 5, 3, 4):
        c_z[i] = put(c_ref(y, z), c_ref(y, z), to_z[i])
    b_send(1, True)
    b_send(1, False)
    c_ay = [None] + [put(own_a, own_a, to_y[i]) for i in range(1, NY)]
    c_send_y(0)
    a_send(1, 0, True)
    a_send(1, 0, False)
    b_spread(0)

    rimg[x] = simg[x]
    rcot[x] = scot[x]
    diagonal = pick(TILE, TILE, lambda row, col: row == col).astype(F32)
    brow[...] = bias[...].reshape(1, NB)

    def column(first):
        spread = jnp.broadcast_to(brow[:, first : first + TILE], (TILE, TILE))
        return jnp.sum(spread * diagonal, axis=1, keepdims=True)

    for j in range(3):
        bti[TILE * j : TILE * j + TILE, :] = column(TILE * j)
    for j in range(2):
        bto[TILE * j : TILE * j + TILE, :] = column(DS + TILE * j)
    for d in (1, 3, 2):
        c_ay[d].wait_recv()
        a_send(1, d, True)
        a_send(1, d, False)
    arrived(c_tz)
    c_ty = [put(tk.at[y, :, c], tk.at[y, :, c], to_y[i]) for i in range(1, NY)]
    c_x = {}

    def x_send(k):
        arrived(c_y[k])
        c_x[k] = [put(c_part(k), c_part(k), to_x[i]) for i in range(1, NX)]

    for k in NEAR[1:]:
        c_z[NZ - k].wait_recv()
        c_send_y(k)

    def gather_step(step):
        b_right[step].wait_recv()
        if step < 4:
            b_send(step + 1, True)
        b_spread(-step)
        if step < 4:
            b_left[step].wait_recv()
            if step < 3:
                b_send(step + 1, False)
            b_spread(step)
        if step < 4:
            for d in (0, 1, 3, 2):
                a_right[step, d].wait_recv()
                if step < 3 or d < 2:
                    a_send(step + 1, d, True)
                a_left[step, d].wait_recv()
                if step < 3 or d > 1:
                    a_send(step + 1, d, False)

    gather_step(1)
    for k in FAR:
        c_z[NZ - k].wait_recv()
        c_send_y(k)
    arrived(c_ty)
    c_tc = put(tk.at[:, :, c], tk.at[:, :, c], sibling)
    for k in NEAR:
        x_send(k)
    for zz in range(NZ):
        for cc in range(2):
            first = [DS + S + 48 * ((yy * NZ + zz) * 2 + cc) for yy in range(NY)]
            bup[2 * zz + cc] = jnp.concatenate([brow[:, f : f + 48] for f in first], axis=1)
    bias_down = brow[:, DS + S + DC : NB]

    c_tc.wait_recv()

    def of_group(row, col):
        group, i = col >> 4, col & 15
        first = (i < 6) & (row == 6 * group + i)
        second = (i >= 8) & (i < 14) & (row == 40 + 6 * group + i)
        return first | second

    chooser = pick(96, 128, of_group)
    for g in range(8):
        part = tk[g // 2, 4 * (g % 2) : 4 * (g % 2) + 4].reshape(128, 256)
        part = dot(chooser, part).astype(BF)
        tokin[48 * g : 48 * g + 48, :] = part[0:48]
        tokout[48 * g : 48 * g + 48, :] = part[48:96]

    arrived(c_img)
    arrived(c_cot)
    keep = [jnp.where(2 * x + b < count[0], 1.0, 0.0).astype(F32) for b in range(2)]
    own = c * (2 * ROW)

    def own_rows(b):
        return pl.ds(pl.multiple_of(own + b * ROW, 16), ROW)

    both = pl.ds(pl.multiple_of(own, 16), 2 * ROW)

    def of_images(row, col):
        b = ge(row, IMG)
        i = row - IMG * b
        part = ge(i, 49) + ge(i, 98) + ge(i, 147)
        return (col == 63 * part + 49 * b + i) & (i < S)

    chooser = pick(2 * IMG, NX * PAIR, of_images)
    ximg[...] = dot(chooser, rimg[...].reshape(NX * PAIR, D)).reshape(2, IMG, D)
    back = dot(chooser, rcot[...].reshape(NX * PAIR, D))
    for b in range(2):
        mb[own_rows(b), :] = (back[b * IMG : b * IMG + ROW] * keep[b]).astype(BF)
        xhat, _ = normalise(ximg[b])
        normed[b] = (xhat * norm[0:1, :] + norm[1:2, :]).astype(BF)
    c_mb = put(mb.at[both], mb.at[both], sibling)
    for k in FAR:
        x_send(k)
    gather_step(2)

    @pl.loop(0, 2)
    def _(b):
        pre = dot(tokin[...], normed[b]) + bti[...]
        value, grad = gelu_and_slope(pre)
        slope[b] = grad
        act[b] = value.astype(BF)
        mixed = dot(tokout[...], act[b], 0, 0) + bto[...]
        middle = ximg[b] + mixed.astype(BF).astype(F32)
        mid[b] = middle
        xhat, _ = normalise(middle[0:ROW])
        n2[own_rows(b), :] = (xhat * norm[2:3, :] + norm[3:4, :]).astype(BF)

    c_n2 = put(n2.at[both], n2.at[both], sibling)
    gather_step(3)
    gather_step(4)
    c_mb.wait_recv()
    c_n2.wait_recv()

    def channel_pass(half):
        offsets = FAR_FIRST[4 * half : 4 * half + 4]
        for j, k in enumerate(offsets):
            upc[192 * j : 192 * j + 192, :] = W[:, Z(k), 0:48, :].reshape(192, D)
            dnc[192 * j : 192 * j + 192, :] = W[:, Z(k), 48:96, :].reshape(192, D)
        row = jnp.concatenate([bup[2 * Z(k) + c] for k in offsets], axis=1)
        lanes = slice(half * D, half * D + D)

        @pl.loop(0, 2)
        def _(r):
            rows = pl.ds(pl.multiple_of(r * (2 * ROW), 16), 2 * ROW)
            pre = dot(n2[rows, :], upc[...], 1, 1) + row
            value, grad = gelu_and_slope(pre)
            low = value.astype(BF)
            actb[rows, lanes] = low
            part = dot(low, dnc[...])
            br[rows, :] = part if half == 1 else br[rows, :] + part
            low = (grad * dot(mb[rows, :], dnc[...], 1, 1)).astype(BF)
            dpb[rows, lanes] = low
            part = dot(low, upc[...])
            dn[rows, :] = part if half == 1 else dn[rows, :] + part

    ra, la, xb, yb, yc, xd, rz = {}, {}, {}, {}, {}, {}, {}

    def gradients(pair):
        lanes = slice(2 * 192 * pair, 2 * 192 * pair + 384)
        offsets = FAR_FIRST[2 * pair : 2 * pair + 2]
        for u, (left, right) in enumerate(((dpb, n2), (actb, mb))):
            grad = dot(left[:, lanes], right[...], 0, 0).astype(BF)
            for j, k in enumerate(offsets):
                part = grad[192 * j : 192 * j + 192].reshape(4, 48, D)
                G[:, Z(k), 48 * u : 48 * u + 48, :] = part
        for k in offsets:
            for i in range(1, NX):
                xb[k, i] = put(G.at[X(i), Z(k), :, P1], XB.at[i - 1, Z(k)], to_x[i])
                ref = G.at[:, Z(k), rows_of(Y(i)), lanes_of(Y(i), 2)]
                yb[k, i] = put(ref, YB.at[i - 1, Z(k)], to_y[i])

    def a_reduce(step, ws):
        for w in ws:
            first = 1 if w < 2 else 2
            if step >= first:
                ref = G.at[X(w), Z(5 - step), :, P0]
                if step > first:
                    ra[step - 1, w].wait_recv()
                    ref[...] = total(ref[...], RAr[step - 2, w]).astype(BF)
                ra[step, w] = put(ref, RAr.at[step - 1, w], to_z[1])
            first = 2 if w < 2 else 1
            if step >= first:
                ref = G.at[X(w), Z(step - 5), :, P0]
                if step > first:
                    la[step - 1, w].wait_recv()
                    ref[...] = total(ref[...], RAl[step - 2, w]).astype(BF)
                la[step, w] = put(ref, RAl.at[step - 1, w], to_z[7])

    def second(k):
        arrived([xb[k, i] for i in range(1, NX)])
        ref = G.at[x, Z(k), :, P1]
        ref[...] = total(ref[...], *[XB[i, Z(k)] for i in range(NX - 1)]).astype(BF)
        for i in range(1, NY):
            ref = G.at[x, Z(k), rows_of(Y(i)), lanes_of(Y(i), 1)]
            yc[k, i] = put(ref, YC.at[i - 1, Z(k)], to_y[i])
        arrived([yb[k, i] for i in range(1, NY)])
        ref = G.at[:, Z(k), rows_of(y), lanes_of(y, 2)]
        ref[...] = total(ref[...], *[YB[i, Z(k)] for i in range(NY - 1)]).astype(BF)
        for i in range(1, NX):
            ref = G.at[X(i), Z(k), rows_of(y), lanes_of(y, 2)]
            xd[k, i] = put(ref, XD.at[i - 1, Z(k)], to_x[i])

    def third(k):
        arrived([yc[k, i] for i in range(1, NY)])
        value = G[x, Z(k), rows_of(y), lanes_of(y, 1)]
        PZ[Z(k), :, 0:TILE] = total(value, *[YC[i, Z(k)] for i in range(NY - 1)]).astype(BF)
        arrived([xd[k, i] for i in range(1, NX)])
        value = G[x, Z(k), rows_of(y), lanes_of(y, 2)]
        PZ[Z(k), :, TILE : 2 * TILE] = total(value, *[XD[i, Z(k)] for i in range(NX - 1)]).astype(BF)
        if k > 0:
            rz[k] = put(PZ.at[Z(k)], RZ.at[k - 1], to_z[k])

    for offset in (0, -1, 1, 2):
        arrived(b_y[offset])
    for k in NEAR:
        arrived(c_x[k])
    loads[0].wait()
    loads[1].wait()
    stage[0:12, :] = q_up[...]
    stage[12:16, :] = jnp.zeros((4, DC), F32)
    stage[16:28, :] = p_dn[...]
    stage[28:32, :] = jnp.zeros((4, DC), F32)
    qst[0] = stage[0:16, :].astype(BF)
    qst[1] = stage[16:32, :].astype(BF)
    Qx[:, x] = qst[:, :, pl.ds(pl.multiple_of(x * D, D), D)]
    c_q = [
        put(qst.at[:, :, pl.ds(pl.multiple_of(X(i) * D, D), D)], Qx.at[:, x], to_x[i])
        for i in range(1, NX)
    ]
    channel_pass(1)
    gradients(2)
    gradients(3)
    for offset in (-2, 3, -3, -4):
        arrived(b_y[offset])
    for k in FAR:
        arrived(c_x[k])
    for d in (0, 1, 3, 2):
        (a_right if d < 2 else a_left)[4, d].wait_recv()
    channel_pass(0)

    other = pl.ds(pl.multiple_of((1 - c) * (2 * ROW), 16), 2 * ROW)
    upc[0 : 2 * ROW, :] = dn[other, :].astype(BF)
    c_dn = put(upc.at[0 : 2 * ROW], xbi.at[1], sibling)
    dnc[0 : 2 * ROW, :] = br[other, :].astype(BF)
    c_br = put(dnc.at[0 : 2 * ROW], xbi.at[0], sibling)

    gradients(0)
    a_reduce(1, range(4))
    gradients(1)
    for k in NEAR:
        second(k)

    ones = jnp.ones((8, 4 * ROW), BF)
    up_sums = dot(ones, dpb[...])[0:1]
    down_sums = dot(ones[:, 0 : 2 * ROW], mb[both, :])
    lob, dmx = actb, dpb
    lob[0 : 2 * IMG, 0:D] = jnp.zeros((2 * IMG, D), BF)
    dmx[0 : 2 * IMG, 0:D] = jnp.zeros((2 * IMG, D), BF)
    c_dn.wait_recv()
    c_br.wait_recv()
    gain_two = jnp.zeros((1, D), F32)
    shift_two = jnp.zeros((1, D), F32)
    for b in range(2):
        here = slice(b * ROW, b * ROW + ROW)
        branch = br[own_rows(b), :] + xbi[0, here, :].astype(F32) + bias_down
        lob[b * IMG : b * IMG + ROW, 0:D] = (keep[b] * (mid[b, 0:ROW] + branch)).astype(BF)
        dh = dn[own_rows(b), :] + xbi[1, here, :].astype(F32)
        xhat, r = normalise(mid[b, 0:ROW])
        dv, gain, shift = normalise_back(xhat, r, dh, norm[2:3, :])
        gain_two = gain_two + gain
        shift_two = shift_two + shift
        back = mb[own_rows(b), :].astype(F32) + dv
        mid[b, 0:ROW] = back
        dmx[b * IMG : b * IMG + ROW, 0:D] = back.astype(BF)
        a_reduce(2, (2 * b, 2 * b + 1))

    def of_out(row, col):
        m = ge(row, PAIR) + ge(row, 2 * PAIR) + ge(row, 3 * PAIR)
        i = row - PAIR * m
        second_one = ge(i, PATCHES)
        place = (IMG - PATCHES) * second_one + PATCHES * m + i
        return (col == place) & (i < 2 * PATCHES)

    out_chooser = pick(NX * PAIR, 2 * IMG, of_out)

    def to_patches(buffer, sent):
        settle(sent)
        buffer[...] = dot(out_chooser, lob[0 : 2 * IMG, 0:D]).astype(BF).reshape(NX, PAIR, D)

    a_reduce(3, (0, 1))
    to_patches(simg, c_img)
    a_reduce(3, (2, 3))

    roots = [
        pltpu.make_async_copy(late[2], br.at[0:D], lsem.at[0]),
        pltpu.make_async_copy(late[3], dn.at[0:D], lsem.at[1]),
    ]
    for copy in roots:
        copy.start()
    gti = jnp.zeros((IMG, DS), F32)
    gto = jnp.zeros((IMG, DS), F32)
    sum_ti = jnp.zeros((8, DS), F32)
    sum_to = jnp.zeros((8, IMG), F32)
    gain_one = jnp.zeros((1, D), F32)
    shift_one = jnp.zeros((1, D), F32)
    ones = jnp.ones((8, D), BF)
    for b in range(2):
        dmixed = dmx[b * IMG : b * IMG + IMG, 0:D]
        dpre = (slope[b] * dot(tokout[...], dmixed)).astype(BF)
        gti = gti + dot(normed[b], dpre, 1, 1)
        gto = gto + dot(dmixed, act[b], 1, 1)
        sum_ti = sum_ti + dot(ones, dpre, 1, 1)
        sum_to = sum_to + dot(ones, dmixed, 1, 1)
        dnormed = dot(tokin[...], dpre, 0, 0).astype(BF).astype(F32)
        xhat, r = normalise(ximg[b, 0:ROW])
        dv, gain, shift = normalise_back(xhat, r, dnormed[0:ROW], norm[0:1, :])
        gain_one = gain_one + gain
        shift_one = shift_one + shift
        lob[b * IMG : b * IMG + ROW, 0:D] = (mid[b, 0:ROW] + dv).astype(BF)
        if b == 0:
            a_reduce(4, (0, 1))
            second(4)
            second(5)
            a_reduce(4, (2, 3))

    second(3)
    second(6)
    c_xa = []
    for w in (1, 3, 2, 0):
        ra[4, w].wait_recv()
        la[4, w].wait_recv()
        ref = G.at[X(w), z, :, P0]
        ref[...] = total(ref[...], RAr[3, w], RAl[3, w]).astype(BF)
        if w > 0:
            c_xa.append(put(ref, XA.at[w - 1], to_x[w]))
    for k in NEAR:
        third(k)

    SM[0:IMG, :] = gti
    SM[IMG : IMG + ROW, :] = gto[0:ROW]
    SM[IMG + ROW :, :] = jnp.zeros((IMG - ROW, DS), F32)
    for j, row in enumerate((gain_one, shift_one, gain_two, shift_two)):
        SM[208 + 2 * j : 209 + 2 * j, :] = row[:, 0:HALF]
        SM[209 + 2 * j : 210 + 2 * j, :] = row[:, HALF:D]
    SM[216:224, :] = sum_ti
    SM[224:232, 0:IMG] = sum_to
    SM[224:232, IMG:DS] = jnp.zeros((8, DS - IMG), F32)
    SM[232:240, :] = down_sums[:, 0:HALF]
    SM[240:248, :] = down_sums[:, HALF:D]
    for j, k in enumerate(FAR_FIRST):
        SM[pl.ds(464 + 8 * c + Z(k), 1), 0:192] = up_sums[:, 192 * j : 192 * j + 192]
    SB[...] = SM[...].reshape(NY, NZ, 16, DS).astype(BF)
    c_sx = [put(SB.at[X(i)], SX.at[i - 1], to_x[i]) for i in range(1, NX)]

    for k in (4, 5):
        third(k)
    arrived(c_xa)
    ref = G.at[x, z, :, P0]
    ref[...] = total(ref[...], XA[0], XA[1], XA[2]).astype(BF)
    c_ya = [
        put(G.at[x, z, rows_of(Y(i)), lanes_of(Y(i), 0)], YA.at[i - 1], to_y[i])
        for i in range(1, NY)
    ]
    for k in (3, 6):
        third(k)
    arrived(c_sx)
    SB[x] = total(SB[x], SX[0], SX[1], SX[2]).astype(BF)
    c_sz = [put(SB.at[x, Z(i)], SZ.at[i - 1], to_z[i]) for i in range(1, NZ)]


    hz, hy, hs = {}, {}, {}

    def h_send(lanes):
        ref = HQ.at[c, y, z, :, lanes]
        for i in (4, 3, 5, 2, 6, 1, 7):
            hz[i] = hz.get(i, []) + [put(ref, ref, to_z[i])]

    arrived(c_ya)
    mean = total(G[x, z, rows_of(y), lanes_of(y, 0)], YA[0], YA[1], YA[2]) * PER_IMAGE
    HQ[c, y, z, :, 0:TILE] = mean.astype(BF)
    h_send(slice(0, TILE))
    arrived(rz.values())
    mean = total(PZ[z], *[RZ[i] for i in range(NZ - 1)]) * PER_IMAGE
    HQ[c, y, z, :, TILE:] = mean.astype(BF)
    h_send(slice(TILE, DS))

    def h_spread(offset):
        ref = HQ.at[c, y, Z(offset)]
        hy[offset] = [put(ref, ref, to_y[i]) for i in range(1, NY)]

    def h_share(offset):
        arrived(hy[offset])
        ref = HQ.at[c, :, Z(offset)]
        hs[offset] = put(ref, ref, sibling)

    h_spread(0)
    own_out = [pltpu.make_async_copy(simg.at[x], rlay.at[x], lsem.at[2])]
    own_out[0].start()
    c_lay = [put(simg.at[X(i)], rlay.at[x], to_x[i]) for i in range(1, NX)]
    to_patches(scot, c_cot)
    own_out.append(pltpu.make_async_copy(scot.at[x], rgrad.at[x], lsem.at[3]))
    own_out[1].start()
    c_grad = [put(scot.at[X(i)], rgrad.at[x], to_x[i]) for i in range(1, NX)]
    arrived(c_sz)
    S8[y, c] = total(SB[x, z], *[SZ[i] for i in range(NZ - 1)]).astype(BF)
    c_s8 = [put(S8.at[y, c], S8.at[y, c], device) for device in to_same]
    for i in (1, 7, 2, 6):
        arrived(hz[i])
        h_spread(-i)
    h_share(0)

    first_j = used[0]
    used[0] += 3

    def j_copy(i):
        return pltpu.make_async_remote_copy(
            src_ref=HQ.at[c, :, z], dst_ref=UJQ, send_sem=ssem.at[first_j + i - 1],
            recv_sem=rsem.at[first_j], device_id=to_x[i], device_id_type=MESH,
        )

    @pl.when(x == y)
    def _():
        for i in range(1, NX):
            j_copy(i).start()
        UJQ[...] = HQ[c, :, z]

    for i in (3, 5, 4):
        arrived(hz[i])
        h_spread(-i)
    arrived(c_s8)
    parts = [S8[yy, cc] for yy in range(NY) for cc in range(2)]
    SF[x, z] = (total(*parts) * PER_IMAGE).astype(BF)
    c_fz = [put(SF.at[x, z], SF.at[x, z], to_z[i]) for i in range(1, NZ)]
    for i in (1, 7, 2, 6):
        h_share(-i)
    @pl.when(x != y)
    def _():
        j_copy(1).wait_recv()

    def of_rows(row, col):
        m, i = row >> 4, row & 15
        return (col == 12 * m + i) & (i < 12)

    spread = pick(64, 48, of_rows)
    channels = pick(16, D, lambda row, col: (col == 12 * dp + row) & (row < 12))

    def unfold(dst, read, u):
        for t in range(2):
            value = read(2 * u + t)
            for part in range(3):
                lanes = slice(256 * part + TILE * t, 256 * part + TILE * t + TILE)
                dst[:, lanes] = value[..., TILE * part : TILE * part + TILE].reshape(-1, TILE)

    settle([c_dn, c_mb, c_n2])
    for u, out in enumerate((o_gup, o_gdn)):
        unfold(upc.at[0:48], lambda q: UJQ[q], u)
        UJP[u, 0:64] = dot(spread, upc[0:48, :]).astype(BF)
        UJP[u, 64:80] = channels
        out[...] = UJP[u, pl.ds(pl.multiple_of(16 * x, 16), 16), :][0:12].astype(F32)
    for i in (3, 5, 4):
        h_share(-i)
    arrived(c_fz)
    c_fx = [put(SF.at[x], SF.at[x], to_x[i]) for i in range(1, NX)]

    arrived([hs[offset] for offset in (0, -1, -7, -2, -6, -3, -5, -4)])
    arrived(c_q)
    c_xe = []
    for u in range(2):
        store = (n2, mb)[u]
        for zz in range(NZ):
            for cc in range(2):
                first = (2 * zz + cc) * 48
                unfold(store.at[first : first + 48], lambda q: HQ[cc, q, zz], u)
        quarter = store[0:D, :]
        right = dot(UJP[u], quarter, 1, 1)
        left = jnp.concatenate([Qx[u].reshape(64, D), right[64:80].astype(BF)], axis=0)
        left = dot(left, quarter)
        for m in range(NX):
            XEo[m, u, :, 0:D] = right[16 * m : 16 * m + 16].astype(BF)
            XEo[m, u, :, D : 2 * D] = left[16 * m : 16 * m + 16].astype(BF)
            XEo[m, u, :, 2 * D : 2 * D + 192] = left[64:80, 192 * m : 192 * m + 192].astype(BF)
            XEo[m, u, :, 2 * D + 192 : 2 * D + 256] = jnp.zeros((16, 64), BF)
        XEi[x, u] = XEo[x, u]
        c_xe.append([put(XEo.at[X(i), u], XEi.at[x, u], to_x[i]) for i in range(1, NX)])

    for copy in loads[4:]:
        copy.wait()

    arrived(c_fx)
    small = SF[...].reshape(512, DS)
    o_norm[...] = small[208:216].astype(F32)
    vector = small[208:256].astype(F32)
    ups = small[464:480].astype(F32)
    pieces = [vector[8:9], vector[16:17, 0:S]]
    for yy in range(NY):
        for zz in range(NZ):
            for cc in range(2):
                pieces.append(ups[8 * cc + zz : 8 * cc + zz + 1, 48 * yy : 48 * yy + 48])
    pieces += [vector[24:25], vector[32:33]]
    o_bias[...] = jnp.concatenate(pieces, axis=1)
    real = lax.broadcasted_iota(jnp.int32, (IMG, DS), 0) < S
    g_in = jnp.where(real, small[0:IMG].astype(F32), 0.0).astype(BF)
    g_out = jnp.where(real, small[IMG : 2 * IMG].astype(F32), 0.0).astype(BF)
    o_lti[...] = 0.5 * ol_ti[...] + 0.5 * dot(g_in, g_in, 1, 1)[0:S, 0:S]
    o_rti[...] = 0.5 * or_ti[...] + 0.5 * dot(g_in, g_in, 0, 0)
    o_lto[...] = 0.5 * ol_to[...] + 0.5 * dot(g_out, g_out, 0, 0)
    o_rto[...] = 0.5 * or_to[...] + 0.5 * dot(g_out, g_out, 1, 1)[0:S, 0:S]
    mine = pick(16, DS, lambda row, col: (col == 6 * dp + row) & (row < 6))
    o_gti[...] = dot(mine, g_in, 1, 1)[0:6, 0:S]
    o_gto[...] = dot(mine, g_out, 1, 1)[0:6, 0:S]
    mine = mine.astype(F32)
    step = dot(mine, pr_ti[...], 1, 1, HIGH)
    step = dot(step, g_in.astype(F32), 1, 1, HIGH)[:, 0:S]
    step = dot(step, pl_ti[...], 1, 1, HIGH)
    o_nti[...] = tin[...] - 0.5 * step[0:6]
    step = dot(mine, pl_to[...], 1, 0, HIGH)
    step = dot(step, g_out.astype(F32), 1, 1, HIGH)[:, 0:S]
    step = dot(step, pr_to[...], 1, 0, HIGH)
    o_nto[...] = tout[...] - 0.5 * step[0:6]

    for copy in roots:
        copy.wait()
    settle([c_br])
    upc[...] = br[0:D, :].astype(BF)
    dnc[...] = dn[0:D, :].astype(BF)
    for u, (o_stat, old_stat, o_side, old_side, o_new, weight, root, dim) in enumerate((
        (o_rup, old_r_up, o_lup, old_l_up, o_nup, wup, upc, 1),
        (o_ldn, old_l_dn, o_rdn, old_r_dn, o_ndn, wdn, dnc, 0),
    )):
        arrived(c_xe[u])
        for m in range(NX):
            lanes = slice(D * m, D * m + D)
            fresh = XEi[m, u, :, 0:D][0:12].astype(F32)
            o_stat[:, lanes] = 0.5 * old_stat[:, lanes] + 0.5 * fresh
        side = total(*[XEi[m, u, :, 2 * D : 2 * D + 192] for m in range(NX)])
        o_side[...] = 0.5 * old_side[...] + 0.5 * side[0:12]
        step = total(*[XEi[m, u, :, D : 2 * D] for m in range(NX)])
        high = step.astype(BF)
        step = jnp.concatenate([high, (step - high.astype(F32)).astype(BF)], axis=0)
        step = dot(step, root[...], 1, dim)
        o_new[...] = weight[...] - 0.5 * (step[0:12] + step[16:28])

    arrived(c_lay)
    arrived(c_grad)
    for copy in own_out:
        copy.wait()
    settle(list(started))

    @pl.when(x == y)
    def _():
        for i in range(1, NX):
            j_copy(i).wait_send()


def finish(
    rlay, rgrad, grads, bias_grad, norm, second, bias, bias_second, *refs
):
    handed = (len(refs) - 8) // 2
    sources, outs = refs[:handed], refs[handed:]
    o_layer, o_gimg, o_grad, o_second, o_norm, o_bias_grad, o_bias_second, o_bias = outs[handed:]
    for src, dst in zip(sources, outs):
        dst[...] = src[...]

    def of_patch(row, col):
        image = row & 7
        pair, second_one = image >> 1, image & 1
        return col == PAIR * pair + PATCHES * second_one + (row >> 3)

    chooser = pick(8 * PATCHES, NX * PAIR, of_patch)
    o_layer[...] = dot(chooser, rlay[...].reshape(NX * PAIR, D)).astype(BF)
    o_gimg[...] = dot(chooser, rgrad[...].reshape(NX * PAIR, D))
    for j in range(4):
        row = slice(j, j + 1)
        grad = jnp.concatenate([grads[2 * j : 2 * j + 1, :], grads[2 * j + 1 : 2 * j + 2, :]], axis=1)
        fresh = 0.5 * second[row, :] + 0.5 * grad * grad
        o_grad[row, :] = grad
        o_second[row, :] = fresh
        o_norm[row, :] = norm[row, :] - 0.5 * grad * lax.rsqrt(fresh + 1e-08)
    grad = bias_grad[...].reshape(NB)
    fresh = 0.5 * bias_second[...] + 0.5 * grad * grad
    o_bias_grad[...] = grad
    o_bias_second[...] = fresh
    o_bias[...] = bias[...] - 0.5 * grad * lax.rsqrt(fresh + 1e-08)


def on_device(
    images, cotangent, image_counts, w_tok_in, w_tok_out, w_up, w_down, norm_params, biases,
    left_tok_in, right_tok_in, left_tok_out, right_tok_out, left_up, right_up, left_down, right_down,
    root_left_tok_in, root_right_tok_in, root_left_tok_out, root_right_tok_out,
    root_left_up, root_right_up, root_left_down, root_right_down, norm_second, bias_second,
):
    patch_rows = 8 * PATCHES

    def by_patch(v):
        return v.transpose(1, 0, 2).reshape(patch_rows, D)

    def by_image(v):
        return v.reshape(PATCHES, 8, D).transpose(1, 0, 2)

    args = (
        image_counts, by_patch(images), by_patch(cotangent), w_tok_in.T, w_tok_out, w_up.T, w_down,
        norm_params, biases,
        root_right_up.T, root_left_down, root_left_up, root_right_down,
        right_up.T, left_down, left_up, right_down,
        root_left_tok_in, root_right_tok_in, root_left_tok_out, root_right_tok_out,
        left_tok_in, right_tok_in, left_tok_out, right_tok_out,
    )
    outs = [
        ((NX, PAIR, D), BF), ((NX, PAIR, D), BF), ((12, D), F32), ((12, D), F32), ((12, D), F32),
        ((12, D), F32), ((12, DC), F32), ((12, DC), F32), ((12, 192), F32), ((12, 192), F32),
        ((8, DS), F32), ((1, NB), F32), ((6, S), F32), ((6, S), F32), ((6, S), F32), ((6, S), F32),
        ((S, S), F32), ((DS, DS), F32), ((DS, DS), F32), ((S, S), F32),
    ]

    def shapes(items):
        return [jax.ShapeDtypeStruct(shape, dtype) for shape, dtype in items]

    def vm(dtype, *shape):
        return pltpu.VMEM(shape, dtype)

    copies = 400
    scratch = [
        pltpu.SemaphoreType.DMA((copies,)), pltpu.SemaphoreType.DMA((copies,)), pltpu.SemaphoreType.DMA((4 + NUM_LATE,)),
        vm(F32, 32, DC), vm(BF, 32, D), vm(BF, 16, 256),
        *[vm(BF, NX, PAIR, D) for _ in range(4)],
        vm(BF, NX, 32, D), vm(BF, NY, NZ, 96, D), vm(BF, NY, NZ, 2, 16, 256),
        vm(BF, DS, 256), vm(BF, DS, 256), vm(F32, DS, 1), vm(F32, IMG, 1), vm(F32, 16, 1, 192), vm(F32, 1, NB),
        vm(F32, 2, IMG, D), vm(BF, 2, IMG, D), vm(F32, 2, IMG, D), vm(F32, 2, DS, D), vm(BF, 2, DS, D),
        vm(BF, 4 * ROW, D), vm(BF, 4 * ROW, D), vm(F32, 4 * ROW, D), vm(F32, 4 * ROW, D),
        vm(BF, D, D), vm(BF, D, D), vm(BF, 4 * ROW, 2 * D), vm(BF, 4 * ROW, 2 * D),
        vm(BF, 2, 2 * ROW, D),
        vm(BF, NY, NZ, 96, D),
        vm(BF, 4, NX, 96, 256), vm(BF, 4, NX, 96, 256), vm(BF, 3, 96, 256), vm(BF, 3, 48, TILE),
        vm(BF, 3, NZ, 96, 256), vm(BF, 3, NZ, NY, 48, TILE), vm(BF, 3, NZ, 48, TILE), vm(BF, 3, NZ, 48, TILE),
        vm(BF, NZ, 48, 256), vm(BF, 7, 48, 256),
        vm(BF, 2, NY, NZ, 48, DS), vm(BF, NY, 48, DS), vm(BF, 2, 80, D),
        vm(BF, 2, 16, DC), vm(BF, 2, NX, 16, D),
        vm(BF, NX, 2, 16, 1792), vm(BF, NX, 2, 16, 1792),
        vm(F32, 512, DS), vm(BF, NY, NZ, 16, DS), vm(BF, 3, NZ, 16, DS), vm(BF, 7, 16, DS),
        vm(BF, NY, 2, 16, DS), vm(BF, NY, NZ, 16, DS),
        vm(BF, patch_rows, D), vm(F32, 12, DC), vm(F32, 12, DC), vm(F32, 12, DC), vm(F32, 12, DC),
        vm(F32, 12, 192), vm(F32, 12, 192),
        *[vm(F32, n, n) for n in (S, DS, DS, S, S, DS, DS, S)],
    ]
    in_vmem = pl.BlockSpec(memory_space=pltpu.VMEM)
    anywhere = pl.BlockSpec(memory_space=pl.ANY)
    rlay, rgrad, *rest = pl.pallas_call(
        fused,
        out_shape=shapes(outs),
        in_specs=[pl.BlockSpec(memory_space=pltpu.SMEM)]
        + [anywhere if i == 2 or i > 8 else in_vmem for i in range(1, len(args))],
        out_specs=[anywhere, anywhere] + [in_vmem] * (len(outs) - 2),
        scratch_shapes=scratch,
        compiler_params=pltpu.CompilerParams(
            collective_id=0, has_side_effects=True, vmem_limit_bytes=64 * 2**20
        ),
        name="fused",
    )(*args)
    handed = rest[:8] + rest[10:]
    handed_outs = outs[2:10] + outs[12:]
    own_outs = [((patch_rows, D), BF), ((patch_rows, D), F32)] + [((4, D), F32)] * 3 + [((NB,), F32)] * 3
    (
        gup, gdn, nup, ndn, rup, ldn, lup, rdn, gti, gto, nti, nto, lti, rti, lto, rto,
        layer, gimg, norm_grad, norm_second_new, norm_new, bias_grad, bias_second_new, bias_new,
    ) = pl.pallas_call(
        finish,
        out_shape=shapes(handed_outs + own_outs),
        in_specs=[in_vmem] * (8 + len(handed)),
        out_specs=[in_vmem] * (8 + len(handed)),
        compiler_params=pltpu.CompilerParams(vmem_limit_bytes=64 * 2**20),
        name="finish",
    )(rlay, rgrad, rest[8], rest[9], norm_params, norm_second, biases, bias_second, *handed)

    return (
        by_image(layer), by_image(gimg), gti.T, gto, gup.T, gdn, nti.T, nto, nup.T, ndn,
        lti, rti, lto, rto, lup, rup.T, ldn, rdn,
        norm_grad, norm_second_new, norm_new, bias_grad, bias_second_new, bias_new,
    )


def solution(mesh):
    both, dp, rest = ("dp", "mix"), "dp", P()
    in_specs = (
        P(dp, "mix", None), P(dp, "mix", None), P(dp), P(None, dp), P(dp, None), P(None, both), P(both, None),
        rest, rest, rest, rest, rest, rest,
        P(dp, "mix"), P(None, both), P(both, None), P(dp, "mix"),
        rest, rest, rest, rest, rest, P(None, both), P(both, None), rest, rest, rest,
    )
    out_specs = (
        P(dp, "mix", None), P(dp, "mix", None), P(None, dp), P(dp, None), P(None, both), P(both, None),
        P(None, dp), P(dp, None), P(None, both), P(both, None),
        rest, rest, rest, rest, P(dp, "mix"), P(None, both), P(both, None), P(dp, "mix"),
        rest, rest, rest, rest, rest, rest,
    )
    return jax.shard_map(on_device, mesh=mesh, in_specs=in_specs, out_specs=out_specs, check_vma=False)
```

```python
import jax
import jax.numpy as jnp
from jax import lax
from jax.experimental import pallas as pl
from jax.experimental.pallas import tpu as pltpu
from jax.sharding import PartitionSpec as P

MESH = pl.DeviceIdType.MESH
BF = jnp.bfloat16
F32 = jnp.float32
HIGH = lax.Precision.HIGHEST

D = 768
DC = 3072
DS = 384
S = 196
NX, NY, NZ = 4, 4, 8
EPS = 1e-06
PER_IMAGE = 1.0 / 512.0
PATCHES = 49
NUM_LATE = 16
PAIR = 112
IMG = 256
ROW = 208
HALF = D // 2
NB = 4420
TILE = 128
P0, P1, P2 = slice(0, 256), slice(256, 512), slice(512, 768)
FAR_FIRST = (4, 5, 3, 6, 2, 7, 1, 0)
NEAR, FAR = (0, 7, 1, 2), (6, 3, 5, 4)


def dot(left, right, left_dim=1, right_dim=0, precision=None):
    return lax.dot_general(
        left,
        right,
        (((left_dim,), (right_dim,)), ((), ())),
        preferred_element_type=F32,
        precision=precision,
    )


def pick(rows, cols, rule):
    row = lax.broadcasted_iota(jnp.int32, (rows, cols), 0)
    col = lax.broadcasted_iota(jnp.int32, (rows, cols), 1)
    return jnp.where(rule(row, col), 1.0, 0.0).astype(BF)


def ge(values, bound):
    return (values >= bound).astype(jnp.int32)


def gelu_and_slope(v):
    t = pl.reciprocal(1.0 + 0.23164188 * jnp.abs(v))
    e = jnp.exp(-0.5 * v * v)
    q = 0.5 * t * (
        0.254829592 + t * (-0.284496736 + t * (1.421413741 + t * (-1.453152027 + t * 1.061405429)))
    ) * e
    cdf = jnp.where(v >= 0, 1.0 - q, q)
    return v * cdf, cdf + v * e * 0.3989422804014327


def normalise(v):
    mean = jnp.mean(v, axis=-1, keepdims=True)
    centre = v - mean
    r = lax.rsqrt(jnp.mean(centre * centre, axis=-1, keepdims=True) + EPS)
    return centre * r, r


def normalise_back(xhat, r, dh, gain):
    dxh = dh * gain
    m1 = jnp.mean(dxh, axis=-1, keepdims=True)
    m2 = jnp.mean(dxh * xhat, axis=-1, keepdims=True)
    dv = r * (dxh - m1 - xhat * m2)
    return dv, jnp.sum(dh * xhat, axis=0, keepdims=True), jnp.sum(dh, axis=0, keepdims=True)


def fused(
    count, img_far, cot_far, tin, tout, wup, wdn, norm, bias, *refs
):
    late = refs[:NUM_LATE]
    (
        rlay, rgrad, o_gup, o_gdn, o_nup, o_ndn, o_rup, o_ldn, o_lup, o_rdn,
        o_norm, o_bias, o_gti, o_gto, o_nti, o_nto, o_lti, o_rti, o_lto, o_rto,
        ssem, rsem, lsem, stage, wst, tst, simg, scot, rimg, rcot,
        xw, W, tk, tokin, tokout, bti, bto, bup, brow, ximg, normed, mid, slope, act, n2, mb, br, dn,
        upc, dnc, actb, dpb, xbi, G, RAr, RAl, XA, YA, XB, YB, YC, XD, PZ, RZ,
        HQ, UJQ, UJP, qst, Qx, XEo, XEi, SM, SB, SY, SZ, S8, SF,
        img, cot, q_up, p_dn, old_r_up, old_l_dn, old_l_up, old_r_dn,
        pl_ti, pr_ti, pl_to, pr_to, ol_ti, or_ti, ol_to, or_to,
    ) = refs[NUM_LATE:]
    loaded = (
        q_up, p_dn, None, None, old_r_up, old_l_dn, old_l_up, old_r_dn,
        pl_ti, pr_ti, pl_to, pr_to, ol_ti, or_ti, ol_to, or_to,
    )
    dp = lax.axis_index("dp")
    x = lax.axis_index("mix")
    c = lax.rem(dp, 2)
    y = dp // (2 * NZ)
    z = lax.rem(dp // 2, NZ)

    def X(i):
        return lax.rem(x + i + NX, NX)

    def Y(i):
        return lax.rem(y + i + NY, NY)

    def Z(i):
        return lax.rem(z + i + NZ, NZ)

    def dev(xx, yy, zz, cc):
        return ((yy * NZ + zz) * 2 + cc, xx)

    to_x = [None] + [dev(X(i), y, z, c) for i in range(1, NX)]
    to_y = [None] + [dev(x, Y(i), z, c) for i in range(1, NY)]
    to_z = [None] + [dev(x, y, Z(i), c) for i in range(1, NZ)]
    sibling = dev(x, y, z, 1 - c)
    started = []
    used = [0]

    def put(src, dst, device):
        k = used[0]
        used[0] += 1
        copy = pltpu.make_async_remote_copy(
            src_ref=src, dst_ref=dst, send_sem=ssem.at[k], recv_sem=rsem.at[k],
            device_id=device, device_id_type=MESH,
        )
        copy.start()
        started.append(copy)
        return copy

    def arrived(copies):
        for copy in copies:
            copy.wait_recv()

    def settle(copies):
        for copy in copies:
            copy.wait_send()
        started[:] = [item for item in started if not any(item is copy for copy in copies)]

    def total(*parts):
        value = parts[0].astype(F32)
        for part in parts[1:]:
            value = value + part.astype(F32)
        return value

    barrier = pltpu.get_barrier_semaphore()
    to_same = [dev(X(i), y, z, cc) for i in range(NX) for cc in (c, 1 - c)][1:]
    peers = to_y[1:] + to_z[1:] + to_same
    for peer in peers:
        pl.semaphore_signal(barrier, inc=1, device_id=peer, device_id_type=MESH)

    get_img = pltpu.make_async_copy(img_far, img, lsem.at[1])
    get_img.start()
    get_cot = pltpu.make_async_copy(cot_far, cot, lsem.at[0])
    get_cot.start()
    loads = [None] * NUM_LATE
    for k in (0, 1, *range(4, NUM_LATE)):
        loads[k] = pltpu.make_async_copy(late[k], loaded[k], lsem.at[4 + k])
        loads[k].start()

    stage[:, 0 : 2 * D] = jnp.zeros((32, 2 * D), F32)
    stage[0:12, 0:D] = wup[...]
    stage[16:28, 0:D] = wdn[...]
    stage[0:6, D : D + S] = tin[...]
    stage[8:14, D : D + S] = tout[...]
    wst[...] = stage[:, 0:D].astype(BF)
    tst[...] = stage[0:16, D : D + 256].astype(BF)
    xw[x] = wst[...]
    tk[y, z, c] = tst[...]

    pl.semaphore_wait(barrier, len(peers))
    c_xw = [put(wst, xw.at[x], to_x[i]) for i in range(1, NX)]
    c_tz = [put(tk.at[y, z, c], tk.at[y, z, c], to_z[i]) for i in range(1, NZ)]

    def of_pairs(row, col):
        m = ge(row, PAIR) + ge(row, 2 * PAIR) + ge(row, 3 * PAIR)
        i = row - PAIR * m
        second = ge(i, PATCHES)
        return (col == (i - PATCHES * second) * 8 + 2 * m + second) & (i < 2 * PATCHES)

    chooser = pick(NX * PAIR, 8 * PATCHES, of_pairs)
    get_img.wait()
    simg[...] = dot(chooser, img[...]).astype(BF).reshape(NX, PAIR, D)
    c_img = [put(simg.at[X(i)], rimg.at[x], to_x[i]) for i in range(1, NX)]
    get_cot.wait()
    scot[...] = dot(chooser, cot[...]).astype(BF).reshape(NX, PAIR, D)
    c_cot = [put(scot.at[X(i)], rcot.at[x], to_x[i]) for i in range(1, NX)]

    arrived(c_xw)

    def of_shards(row, col):
        m, j = col >> 5, col & 31
        up = (j < 12) & (row == 12 * m + j)
        down = (j >= 16) & (j < 28) & (row == 32 + 12 * m + j)
        return up | down

    upc[0:96, :] = dot(pick(96, 128, of_shards), xw[...].reshape(128, D)).astype(BF)
    W[y, z, :, 0:512] = upc[0:96, 0:512]

    def rows_of(q):
        return pl.ds(pl.multiple_of(48 * (q // 2), 16), 48)

    def lanes_of(q, part):
        return pl.ds(pl.multiple_of(256 * part + TILE * lax.rem(q, 2), TILE), TILE)

    a_right, a_left, b_right, b_left, b_y = {}, {}, {}, {}, {}

    def a_send(step, d, right):
        if right:
            ref = W.at[Y(-d), Z(1 - step), :, P0]
            a_right[step, d] = put(ref, ref, to_z[1])
        else:
            ref = W.at[Y(-d), Z(step - 1), :, P0]
            a_left[step, d] = put(ref, ref, to_z[7])

    def b_send(step, right):
        if right:
            ref = W.at[y, Z(1 - step), :, P1]
            b_right[step] = put(ref, ref, to_z[1])
        else:
            ref = W.at[y, Z(step - 1), :, P1]
            b_left[step] = put(ref, ref, to_z[7])

    def b_spread(offset):
        ref = W.at[y, Z(offset), :, P1]
        b_y[offset] = [put(ref, ref, to_y[i]) for i in range(1, NY)]

    def c_ref(yy, zz):
        return W.at[yy, zz, rows_of(x), lanes_of(x, 2)]

    def c_part(k):
        return W.at[:, Z(k), rows_of(x), lanes_of(x, 2)]

    W[y, z, rows_of(x), lanes_of(x, 2)] = upc[rows_of(x), lanes_of(x, 2)]
    own_a = W.at[y, z, :, P0]
    def c_send_y(k):
        ref = c_ref(y, Z(k))
        c_y[k] = [put(ref, ref, to_y[i]) for i in range(1, NY)]

    c_z, c_y = {}, {}
    for i in (1, 7, 6, 2, 5, 3, 4):
        c_z[i] = put(c_ref(y, z), c_ref(y, z), to_z[i])
    b_send(1, True)
    b_send(1, False)
    c_ay = [None] + [put(own_a, own_a, to_y[i]) for i in range(1, NY)]
    c_send_y(0)
    a_send(1, 0, True)
    a_send(1, 0, False)
    b_spread(0)

    rimg[x] = simg[x]
    rcot[x] = scot[x]
    diagonal = pick(TILE, TILE, lambda row, col: row == col).astype(F32)
    brow[...] = bias[...].reshape(1, NB)

    def column(first):
        spread = jnp.broadcast_to(brow[:, first : first + TILE], (TILE, TILE))
        return jnp.sum(spread * diagonal, axis=1, keepdims=True)

    for j in range(3):
        bti[TILE * j : TILE * j + TILE, :] = column(TILE * j)
    for j in range(2):
        bto[TILE * j : TILE * j + TILE, :] = column(DS + TILE * j)
    for d in (1, 3, 2):
        c_ay[d].wait_recv()
        a_send(1, d, True)
        a_send(1, d, False)
    arrived(c_tz)
    c_ty = [put(tk.at[y, :, c], tk.at[y, :, c], to_y[i]) for i in range(1, NY)]
    c_x = {}

    def x_send(k):
        arrived(c_y[k])
        c_x[k] = [put(c_part(k), c_part(k), to_x[i]) for i in range(1, NX)]

    for k in NEAR[1:]:
        c_z[NZ - k].wait_recv()
        c_send_y(k)

    def gather_step(step):
        b_right[step].wait_recv()
        if step < 4:
            b_send(step + 1, True)
        b_spread(-step)
        if step < 4:
            b_left[step].wait_recv()
            if step < 3:
                b_send(step + 1, False)
            b_spread(step)
        if step < 4:
            for d in (0, 1, 3, 2):
                a_right[step, d].wait_recv()
                if step < 3 or d < 2:
                    a_send(step + 1, d, True)
                a_left[step, d].wait_recv()
                if step < 3 or d > 1:
                    a_send(step + 1, d, False)

    gather_step(1)
    for k in FAR:
        c_z[NZ - k].wait_recv()
        c_send_y(k)
    arrived(c_ty)
    c_tc = put(tk.at[:, :, c], tk.at[:, :, c], sibling)
    for k in NEAR:
        x_send(k)
    for zz in range(NZ):
        for cc in range(2):
            first = [DS + S + 48 * ((yy * NZ + zz) * 2 + cc) for yy in range(NY)]
            bup[2 * zz + cc] = jnp.concatenate([brow[:, f : f + 48] for f in first], axis=1)
    bias_down = brow[:, DS + S + DC : NB]

    c_tc.wait_recv()

    def of_group(row, col):
        group, i = col >> 4, col & 15
        first = (i < 6) & (row == 6 * group + i)
        second = (i >= 8) & (i < 14) & (row == 40 + 6 * group + i)
        return first | second

    chooser = pick(96, 128, of_group)
    for g in range(8):
        part = tk[g // 2, 4 * (g % 2) : 4 * (g % 2) + 4].reshape(128, 256)
        part = dot(chooser, part).astype(BF)
        tokin[48 * g : 48 * g + 48, :] = part[0:48]
        tokout[48 * g : 48 * g + 48, :] = part[48:96]

    arrived(c_img)
    arrived(c_cot)
    keep = [jnp.where(2 * x + b < count[0], 1.0, 0.0).astype(F32) for b in range(2)]
    own = c * (2 * ROW)

    def own_rows(b):
        return pl.ds(pl.multiple_of(own + b * ROW, 16), ROW)

    both = pl.ds(pl.multiple_of(own, 16), 2 * ROW)

    def of_images(row, col):
        b = ge(row, IMG)
        i = row - IMG * b
        part = ge(i, 49) + ge(i, 98) + ge(i, 147)
        return (col == 63 * part + 49 * b + i) & (i < S)

    chooser = pick(2 * IMG, NX * PAIR, of_images)
    ximg[...] = dot(chooser, rimg[...].reshape(NX * PAIR, D)).reshape(2, IMG, D)
    back = dot(chooser, rcot[...].reshape(NX * PAIR, D))
    for b in range(2):
        mb[own_rows(b), :] = (back[b * IMG : b * IMG + ROW] * keep[b]).astype(BF)
        xhat, _ = normalise(ximg[b])
        normed[b] = (xhat * norm[0:1, :] + norm[1:2, :]).astype(BF)
    c_mb = put(mb.at[both], mb.at[both], sibling)
    for k in FAR:
        x_send(k)
    gather_step(2)

    @pl.loop(0, 2)
    def _(b):
        pre = dot(tokin[...], normed[b]) + bti[...]
        value, grad = gelu_and_slope(pre)
        slope[b] = grad
        act[b] = value.astype(BF)
        mixed = dot(tokout[...], act[b], 0, 0) + bto[...]
        middle = ximg[b] + mixed.astype(BF).astype(F32)
        mid[b] = middle
        xhat, _ = normalise(middle[0:ROW])
        n2[own_rows(b), :] = (xhat * norm[2:3, :] + norm[3:4, :]).astype(BF)

    c_n2 = put(n2.at[both], n2.at[both], sibling)
    gather_step(3)
    gather_step(4)
    c_mb.wait_recv()
    c_n2.wait_recv()

    def channel_pass(half):
        offsets = FAR_FIRST[4 * half : 4 * half + 4]
        for j, k in enumerate(offsets):
            upc[192 * j : 192 * j + 192, :] = W[:, Z(k), 0:48, :].reshape(192, D)
            dnc[192 * j : 192 * j + 192, :] = W[:, Z(k), 48:96, :].reshape(192, D)
        row = jnp.concatenate([bup[2 * Z(k) + c] for k in offsets], axis=1)
        lanes = slice(half * D, half * D + D)

        @pl.loop(0, 2)
        def _(r):
            rows = pl.ds(pl.multiple_of(r * (2 * ROW), 16), 2 * ROW)
            pre = dot(n2[rows, :], upc[...], 1, 1) + row
            value, grad = gelu_and_slope(pre)
            low = value.astype(BF)
            actb[rows, lanes] = low
            part = dot(low, dnc[...])
            br[rows, :] = part if half == 1 else br[rows, :] + part
            low = (grad * dot(mb[rows, :], dnc[...], 1, 1)).astype(BF)
            dpb[rows, lanes] = low
            part = dot(low, upc[...])
            dn[rows, :] = part if half == 1 else dn[rows, :] + part

    ra, la, xb, yb, yc, xd, rz = {}, {}, {}, {}, {}, {}, {}

    def gradients(pair):
        lanes = slice(2 * 192 * pair, 2 * 192 * pair + 384)
        offsets = FAR_FIRST[2 * pair : 2 * pair + 2]
        for u, (left, right) in enumerate(((dpb, n2), (actb, mb))):
            grad = dot(left[:, lanes], right[...], 0, 0).astype(BF)
            for j, k in enumerate(offsets):
                part = grad[192 * j : 192 * j + 192].reshape(4, 48, D)
                G[:, Z(k), 48 * u : 48 * u + 48, :] = part
        for k in offsets:
            for i in range(1, NX):
                xb[k, i] = put(G.at[X(i), Z(k), :, P1], XB.at[i - 1, Z(k)], to_x[i])
                ref = G.at[:, Z(k), rows_of(Y(i)), lanes_of(Y(i), 2)]
                yb[k, i] = put(ref, YB.at[i - 1, Z(k)], to_y[i])

    def a_reduce(step, ws):
        for w in ws:
            first = 1 if w < 2 else 2
            if step >= first:
                ref = G.at[X(w), Z(5 - step), :, P0]
                if step > first:
                    ra[step - 1, w].wait_recv()
                    ref[...] = total(ref[...], RAr[step - 2, w]).astype(BF)
                ra[step, w] = put(ref, RAr.at[step - 1, w], to_z[1])
            first = 2 if w < 2 else 1
            if step >= first:
                ref = G.at[X(w), Z(step - 5), :, P0]
                if step > first:
                    la[step - 1, w].wait_recv()
                    ref[...] = total(ref[...], RAl[step - 2, w]).astype(BF)
                la[step, w] = put(ref, RAl.at[step - 1, w], to_z[7])

    def second(k):
        arrived([xb[k, i] for i in range(1, NX)])
        ref = G.at[x, Z(k), :, P1]
        ref[...] = total(ref[...], *[XB[i, Z(k)] for i in range(NX - 1)]).astype(BF)
        for i in range(1, NY):
            ref = G.at[x, Z(k), rows_of(Y(i)), lanes_of(Y(i), 1)]
            yc[k, i] = put(ref, YC.at[i - 1, Z(k)], to_y[i])
        arrived([yb[k, i] for i in range(1, NY)])
        ref = G.at[:, Z(k), rows_of(y), lanes_of(y, 2)]
        ref[...] = total(ref[...], *[YB[i, Z(k)] for i in range(NY - 1)]).astype(BF)
        for i in range(1, NX):
            ref = G.at[X(i), Z(k), rows_of(y), lanes_of(y, 2)]
            xd[k, i] = put(ref, XD.at[i - 1, Z(k)], to_x[i])

    def third(k):
        arrived([yc[k, i] for i in range(1, NY)])
        value = G[x, Z(k), rows_of(y), lanes_of(y, 1)]
        PZ[Z(k), :, 0:TILE] = total(value, *[YC[i, Z(k)] for i in range(NY - 1)]).astype(BF)
        arrived([xd[k, i] for i in range(1, NX)])
        value = G[x, Z(k), rows_of(y), lanes_of(y, 2)]
        PZ[Z(k), :, TILE : 2 * TILE] = total(value, *[XD[i, Z(k)] for i in range(NX - 1)]).astype(BF)
        if k > 0:
            rz[k] = put(PZ.at[Z(k)], RZ.at[k - 1], to_z[k])

    for offset in (0, -1, 1, 2):
        arrived(b_y[offset])
    for k in NEAR:
        arrived(c_x[k])
    loads[0].wait()
    loads[1].wait()
    stage[0:12, :] = q_up[...]
    stage[12:16, :] = jnp.zeros((4, DC), F32)
    stage[16:28, :] = p_dn[...]
    stage[28:32, :] = jnp.zeros((4, DC), F32)
    qst[0] = stage[0:16, :].astype(BF)
    qst[1] = stage[16:32, :].astype(BF)
    Qx[:, x] = qst[:, :, pl.ds(pl.multiple_of(x * D, D), D)]
    c_q = [
        put(qst.at[:, :, pl.ds(pl.multiple_of(X(i) * D, D), D)], Qx.at[:, x], to_x[i])
        for i in range(1, NX)
    ]
    channel_pass(1)
    gradients(2)
    gradients(3)
    for offset in (-2, 3, -3, -4):
        arrived(b_y[offset])
    for k in FAR:
        arrived(c_x[k])
    for d in (0, 1, 3, 2):
        (a_right if d < 2 else a_left)[4, d].wait_recv()
    channel_pass(0)

    other = pl.ds(pl.multiple_of((1 - c) * (2 * ROW), 16), 2 * ROW)
    upc[0 : 2 * ROW, :] = dn[other, :].astype(BF)
    c_dn = put(upc.at[0 : 2 * ROW], xbi.at[1], sibling)
    dnc[0 : 2 * ROW, :] = br[other, :].astype(BF)
    c_br = put(dnc.at[0 : 2 * ROW], xbi.at[0], sibling)

    gradients(0)
    a_reduce(1, range(4))
    gradients(1)
    for k in NEAR:
        second(k)

    ones = jnp.ones((8, 4 * ROW), BF)
    up_sums = dot(ones, dpb[...])[0:1]
    down_sums = dot(ones[:, 0 : 2 * ROW], mb[both, :])
    lob, dmx = actb, dpb
    lob[0 : 2 * IMG, 0:D] = jnp.zeros((2 * IMG, D), BF)
    dmx[0 : 2 * IMG, 0:D] = jnp.zeros((2 * IMG, D), BF)
    c_dn.wait_recv()
    c_br.wait_recv()
    gain_two = jnp.zeros((1, D), F32)
    shift_two = jnp.zeros((1, D), F32)
    for b in range(2):
        here = slice(b * ROW, b * ROW + ROW)
        branch = br[own_rows(b), :] + xbi[0, here, :].astype(F32) + bias_down
        lob[b * IMG : b * IMG + ROW, 0:D] = (keep[b] * (mid[b, 0:ROW] + branch)).astype(BF)
        dh = dn[own_rows(b), :] + xbi[1, here, :].astype(F32)
        xhat, r = normalise(mid[b, 0:ROW])
        dv, gain, shift = normalise_back(xhat, r, dh, norm[2:3, :])
        gain_two = gain_two + gain
        shift_two = shift_two + shift
        back = mb[own_rows(b), :].astype(F32) + dv
        mid[b, 0:ROW] = back
        dmx[b * IMG : b * IMG + ROW, 0:D] = back.astype(BF)
        a_reduce(2, (2 * b, 2 * b + 1))

    def of_out(row, col):
        m = ge(row, PAIR) + ge(row, 2 * PAIR) + ge(row, 3 * PAIR)
        i = row - PAIR * m
        second_one = ge(i, PATCHES)
        place = (IMG - PATCHES) * second_one + PATCHES * m + i
        return (col == place) & (i < 2 * PATCHES)

    out_chooser = pick(NX * PAIR, 2 * IMG, of_out)

    def to_patches(buffer, sent):
        settle(sent)
        buffer[...] = dot(out_chooser, lob[0 : 2 * IMG, 0:D]).astype(BF).reshape(NX, PAIR, D)

    a_reduce(3, (0, 1))
    to_patches(simg, c_img)
    own_out = [pltpu.make_async_copy(simg.at[x], rlay.at[x], lsem.at[2])]
    own_out[0].start()
    c_lay = [put(simg.at[X(i)], rlay.at[x], to_x[i]) for i in range(1, NX)]
    a_reduce(3, (2, 3))

    roots = [
        pltpu.make_async_copy(late[2], br.at[0:D], lsem.at[0]),
        pltpu.make_async_copy(late[3], dn.at[0:D], lsem.at[1]),
    ]
    for copy in roots:
        copy.start()
    gti = jnp.zeros((IMG, DS), F32)
    gto = jnp.zeros((IMG, DS), F32)
    sum_ti = jnp.zeros((8, DS), F32)
    sum_to = jnp.zeros((8, IMG), F32)
    gain_one = jnp.zeros((1, D), F32)
    shift_one = jnp.zeros((1, D), F32)
    ones = jnp.ones((8, D), BF)
    for b in range(2):
        dmixed = dmx[b * IMG : b * IMG + IMG, 0:D]
        dpre = (slope[b] * dot(tokout[...], dmixed)).astype(BF)
        gti = gti + dot(normed[b], dpre, 1, 1)
        gto = gto + dot(dmixed, act[b], 1, 1)
        sum_ti = sum_ti + dot(ones, dpre, 1, 1)
        sum_to = sum_to + dot(ones, dmixed, 1, 1)
        dnormed = dot(tokin[...], dpre, 0, 0).astype(BF).astype(F32)
        xhat, r = normalise(ximg[b, 0:ROW])
        dv, gain, shift = normalise_back(xhat, r, dnormed[0:ROW], norm[0:1, :])
        gain_one = gain_one + gain
        shift_one = shift_one + shift
        lob[b * IMG : b * IMG + ROW, 0:D] = (mid[b, 0:ROW] + dv).astype(BF)
        if b == 0:
            a_reduce(4, (0, 1))
            second(4)
            second(5)
            a_reduce(4, (2, 3))

    second(3)
    second(6)
    for w in range(NX):
        ra[4, w].wait_recv()
        la[4, w].wait_recv()
        ref = G.at[X(w), z, :, P0]
        ref[...] = total(ref[...], RAr[3, w], RAl[3, w]).astype(BF)
    c_ya = [
        put(G.at[:, z, rows_of(Y(i)), lanes_of(Y(i), 0)], YA.at[i - 1], to_y[i])
        for i in range(1, NY)
    ]
    for k in NEAR:
        third(k)

    SM[0:IMG, :] = gti
    SM[IMG : IMG + ROW, :] = gto[0:ROW]
    SM[IMG + ROW :, :] = jnp.zeros((IMG - ROW, DS), F32)
    for j, row in enumerate((gain_one, shift_one, gain_two, shift_two)):
        SM[208 + 2 * j : 209 + 2 * j, :] = row[:, 0:HALF]
        SM[209 + 2 * j : 210 + 2 * j, :] = row[:, HALF:D]
    SM[216:224, :] = sum_ti
    SM[224:232, 0:IMG] = sum_to
    SM[224:232, IMG:DS] = jnp.zeros((8, DS - IMG), F32)
    SM[232:240, :] = down_sums[:, 0:HALF]
    SM[240:248, :] = down_sums[:, HALF:D]
    for j, k in enumerate(FAR_FIRST):
        SM[pl.ds(464 + 8 * c + Z(k), 1), 0:192] = up_sums[:, 192 * j : 192 * j + 192]
    SB[...] = SM[...].reshape(NY, NZ, 16, DS).astype(BF)
    c_sy = [put(SB.at[Y(i)], SY.at[i - 1], to_y[i]) for i in range(1, NY)]

    for k in (4, 5):
        third(k)
    arrived(c_ya)
    ref = G.at[:, z, rows_of(y), lanes_of(y, 0)]
    ref[...] = total(ref[...], YA[0], YA[1], YA[2]).astype(BF)
    c_xa = [
        put(G.at[X(i), z, rows_of(y), lanes_of(y, 0)], XA.at[i - 1], to_x[i]) for i in range(1, NX)
    ]
    for k in (3, 6):
        third(k)
    arrived(c_sy)
    SB[y] = total(SB[y], SY[0], SY[1], SY[2]).astype(BF)
    c_sz = [put(SB.at[y, Z(i)], SZ.at[i - 1], to_z[i]) for i in range(1, NZ)]


    hz, hy, hs = {}, {}, {}

    def h_send(lanes):
        ref = HQ.at[c, y, z, :, lanes]
        for i in (1, 7, 2, 6, 3, 5, 4):
            hz[i] = hz.get(i, []) + [put(ref, ref, to_z[i])]

    arrived(c_xa)
    mean = total(G[x, z, rows_of(y), lanes_of(y, 0)], XA[0], XA[1], XA[2]) * PER_IMAGE
    HQ[c, y, z, :, 0:TILE] = mean.astype(BF)
    h_send(slice(0, TILE))
    arrived(rz.values())
    mean = total(PZ[z], *[RZ[i] for i in range(NZ - 1)]) * PER_IMAGE
    HQ[c, y, z, :, TILE:] = mean.astype(BF)
    h_send(slice(TILE, DS))

    def h_spread(offset):
        ref = HQ.at[c, y, Z(offset)]
        hy[offset] = [put(ref, ref, to_y[i]) for i in range(1, NY)]

    def h_share(offset):
        arrived(hy[offset])
        ref = HQ.at[c, :, Z(offset)]
        hs[offset] = put(ref, ref, sibling)

    h_spread(0)
    to_patches(scot, c_cot)
    own_out.append(pltpu.make_async_copy(scot.at[x], rgrad.at[x], lsem.at[3]))
    own_out[1].start()
    c_grad = [put(scot.at[X(i)], rgrad.at[x], to_x[i]) for i in range(1, NX)]
    arrived(c_sz)
    S8[x, c] = total(SB[y, z], *[SZ[i] for i in range(NZ - 1)]).astype(BF)
    c_s8 = [put(S8.at[x, c], S8.at[x, c], device) for device in to_same]
    for i in (1, 7, 2, 6):
        arrived(hz[i])
        h_spread(-i)
    h_share(0)

    first_j = used[0]
    used[0] += 3

    def j_copy(i):
        return pltpu.make_async_remote_copy(
            src_ref=HQ.at[c, :, z], dst_ref=UJQ, send_sem=ssem.at[first_j + i - 1],
            recv_sem=rsem.at[first_j], device_id=to_x[i], device_id_type=MESH,
        )

    @pl.when(x == y)
    def _():
        for i in range(1, NX):
            j_copy(i).start()
        UJQ[...] = HQ[c, :, z]

    for i in (3, 5, 4):
        arrived(hz[i])
        h_spread(-i)
    arrived(c_s8)
    parts = [S8[xx, cc] for xx in range(NX) for cc in range(2)]
    SF[y, z] = (total(*parts) * PER_IMAGE).astype(BF)
    c_fz = [put(SF.at[y, z], SF.at[y, z], to_z[i]) for i in range(1, NZ)]
    for i in (1, 7, 2, 6):
        h_share(-i)
    @pl.when(x != y)
    def _():
        j_copy(1).wait_recv()

    def of_rows(row, col):
        m, i = row >> 4, row & 15
        return (col == 12 * m + i) & (i < 12)

    spread = pick(64, 48, of_rows)
    channels = pick(16, D, lambda row, col: (col == 12 * dp + row) & (row < 12))

    def unfold(dst, read, u):
        for t in range(2):
            value = read(2 * u + t)
            for part in range(3):
                lanes = slice(256 * part + TILE * t, 256 * part + TILE * t + TILE)
                dst[:, lanes] = value[..., TILE * part : TILE * part + TILE].reshape(-1, TILE)

    settle([c_dn, c_mb, c_n2])
    for u, out in enumerate((o_gup, o_gdn)):
        unfold(upc.at[0:48], lambda q: UJQ[q], u)
        UJP[u, 0:64] = dot(spread, upc[0:48, :]).astype(BF)
        UJP[u, 64:80] = channels
        out[...] = UJP[u, pl.ds(pl.multiple_of(16 * x, 16), 16), :][0:12].astype(F32)
    for i in (3, 5, 4):
        h_share(-i)
    arrived(c_fz)
    c_fy = [put(SF.at[y], SF.at[y], to_y[i]) for i in range(1, NY)]

    arrived([hs[offset] for offset in (0, -1, -7, -2, -6, -3, -5, -4)])
    arrived(c_q)
    c_xe = []
    for u in range(2):
        store = (n2, mb)[u]
        for zz in range(NZ):
            for cc in range(2):
                first = (2 * zz + cc) * 48
                unfold(store.at[first : first + 48], lambda q: HQ[cc, q, zz], u)
        quarter = store[0:D, :]
        right = dot(UJP[u], quarter, 1, 1)
        left = jnp.concatenate([Qx[u].reshape(64, D), right[64:80].astype(BF)], axis=0)
        left = dot(left, quarter)
        for m in range(NX):
            XEo[m, u, :, 0:D] = right[16 * m : 16 * m + 16].astype(BF)
            XEo[m, u, :, D : 2 * D] = left[16 * m : 16 * m + 16].astype(BF)
            XEo[m, u, :, 2 * D : 2 * D + 192] = left[64:80, 192 * m : 192 * m + 192].astype(BF)
            XEo[m, u, :, 2 * D + 192 : 2 * D + 256] = jnp.zeros((16, 64), BF)
        XEi[x, u] = XEo[x, u]
        c_xe.append([put(XEo.at[X(i), u], XEi.at[x, u], to_x[i]) for i in range(1, NX)])

    for copy in loads[4:]:
        copy.wait()

    arrived(c_fy)
    small = SF[...].reshape(512, DS)
    o_norm[...] = small[208:216].astype(F32)
    vector = small[208:256].astype(F32)
    ups = small[464:480].astype(F32)
    pieces = [vector[8:9], vector[16:17, 0:S]]
    for yy in range(NY):
        for zz in range(NZ):
            for cc in range(2):
                pieces.append(ups[8 * cc + zz : 8 * cc + zz + 1, 48 * yy : 48 * yy + 48])
    pieces += [vector[24:25], vector[32:33]]
    o_bias[...] = jnp.concatenate(pieces, axis=1)
    real = lax.broadcasted_iota(jnp.int32, (IMG, DS), 0) < S
    g_in = jnp.where(real, small[0:IMG].astype(F32), 0.0).astype(BF)
    g_out = jnp.where(real, small[IMG : 2 * IMG].astype(F32), 0.0).astype(BF)
    o_lti[...] = 0.5 * ol_ti[...] + 0.5 * dot(g_in, g_in, 1, 1)[0:S, 0:S]
    o_rti[...] = 0.5 * or_ti[...] + 0.5 * dot(g_in, g_in, 0, 0)
    o_lto[...] = 0.5 * ol_to[...] + 0.5 * dot(g_out, g_out, 0, 0)
    o_rto[...] = 0.5 * or_to[...] + 0.5 * dot(g_out, g_out, 1, 1)[0:S, 0:S]
    mine = pick(16, DS, lambda row, col: (col == 6 * dp + row) & (row < 6))
    o_gti[...] = dot(mine, g_in, 1, 1)[0:6, 0:S]
    o_gto[...] = dot(mine, g_out, 1, 1)[0:6, 0:S]
    mine = mine.astype(F32)
    step = dot(mine, pr_ti[...], 1, 1, HIGH)
    step = dot(step, g_in.astype(F32), 1, 1, HIGH)[:, 0:S]
    step = dot(step, pl_ti[...], 1, 1, HIGH)
    o_nti[...] = tin[...] - 0.5 * step[0:6]
    step = dot(mine, pl_to[...], 1, 0, HIGH)
    step = dot(step, g_out.astype(F32), 1, 1, HIGH)[:, 0:S]
    step = dot(step, pr_to[...], 1, 0, HIGH)
    o_nto[...] = tout[...] - 0.5 * step[0:6]

    for copy in roots:
        copy.wait()
    settle([c_br])
    upc[...] = br[0:D, :].astype(BF)
    dnc[...] = dn[0:D, :].astype(BF)
    for u, (o_stat, old_stat, o_side, old_side, o_new, weight, root, dim) in enumerate((
        (o_rup, old_r_up, o_lup, old_l_up, o_nup, wup, upc, 1),
        (o_ldn, old_l_dn, o_rdn, old_r_dn, o_ndn, wdn, dnc, 0),
    )):
        arrived(c_xe[u])
        for m in range(NX):
            lanes = slice(D * m, D * m + D)
            fresh = XEi[m, u, :, 0:D][0:12].astype(F32)
            o_stat[:, lanes] = 0.5 * old_stat[:, lanes] + 0.5 * fresh
        side = total(*[XEi[m, u, :, 2 * D : 2 * D + 192] for m in range(NX)])
        o_side[...] = 0.5 * old_side[...] + 0.5 * side[0:12]
        step = total(*[XEi[m, u, :, D : 2 * D] for m in range(NX)])
        high = step.astype(BF)
        step = jnp.concatenate([high, (step - high.astype(F32)).astype(BF)], axis=0)
        step = dot(step, root[...], 1, dim)
        o_new[...] = weight[...] - 0.5 * (step[0:12] + step[16:28])

    arrived(c_lay)
    arrived(c_grad)
    for copy in own_out:
        copy.wait()
    settle(list(started))

    @pl.when(x == y)
    def _():
        for i in range(1, NX):
            j_copy(i).wait_send()


def finish(
    rlay, rgrad, grads, bias_grad, norm, second, bias, bias_second, *refs
):
    handed = (len(refs) - 8) // 2
    sources, outs = refs[:handed], refs[handed:]
    o_layer, o_gimg, o_grad, o_second, o_norm, o_bias_grad, o_bias_second, o_bias = outs[handed:]
    for src, dst in zip(sources, outs):
        dst[...] = src[...]

    def of_patch(row, col):
        image = row & 7
        pair, second_one = image >> 1, image & 1
        return col == PAIR * pair + PATCHES * second_one + (row >> 3)

    chooser = pick(8 * PATCHES, NX * PAIR, of_patch)
    o_layer[...] = dot(chooser, rlay[...].reshape(NX * PAIR, D)).astype(BF)
    o_gimg[...] = dot(chooser, rgrad[...].reshape(NX * PAIR, D))
    for j in range(4):
        row = slice(j, j + 1)
        grad = jnp.concatenate([grads[2 * j : 2 * j + 1, :], grads[2 * j + 1 : 2 * j + 2, :]], axis=1)
        fresh = 0.5 * second[row, :] + 0.5 * grad * grad
        o_grad[row, :] = grad
        o_second[row, :] = fresh
        o_norm[row, :] = norm[row, :] - 0.5 * grad * lax.rsqrt(fresh + 1e-08)
    grad = bias_grad[...].reshape(NB)
    fresh = 0.5 * bias_second[...] + 0.5 * grad * grad
    o_bias_grad[...] = grad
    o_bias_second[...] = fresh
    o_bias[...] = bias[...] - 0.5 * grad * lax.rsqrt(fresh + 1e-08)


def on_device(
    images, cotangent, image_counts, w_tok_in, w_tok_out, w_up, w_down, norm_params, biases,
    left_tok_in, right_tok_in, left_tok_out, right_tok_out, left_up, right_up, left_down, right_down,
    root_left_tok_in, root_right_tok_in, root_left_tok_out, root_right_tok_out,
    root_left_up, root_right_up, root_left_down, root_right_down, norm_second, bias_second,
):
    patch_rows = 8 * PATCHES

    def by_patch(v):
        return v.transpose(1, 0, 2).reshape(patch_rows, D)

    def by_image(v):
        return v.reshape(PATCHES, 8, D).transpose(1, 0, 2)

    args = (
        image_counts, by_patch(images), by_patch(cotangent), w_tok_in.T, w_tok_out, w_up.T, w_down,
        norm_params, biases,
        root_right_up.T, root_left_down, root_left_up, root_right_down,
        right_up.T, left_down, left_up, right_down,
        root_left_tok_in, root_right_tok_in, root_left_tok_out, root_right_tok_out,
        left_tok_in, right_tok_in, left_tok_out, right_tok_out,
    )
    outs = [
        ((NX, PAIR, D), BF), ((NX, PAIR, D), BF), ((12, D), F32), ((12, D), F32), ((12, D), F32),
        ((12, D), F32), ((12, DC), F32), ((12, DC), F32), ((12, 192), F32), ((12, 192), F32),
        ((8, DS), F32), ((1, NB), F32), ((6, S), F32), ((6, S), F32), ((6, S), F32), ((6, S), F32),
        ((S, S), F32), ((DS, DS), F32), ((DS, DS), F32), ((S, S), F32),
    ]

    def shapes(items):
        return [jax.ShapeDtypeStruct(shape, dtype) for shape, dtype in items]

    def vm(dtype, *shape):
        return pltpu.VMEM(shape, dtype)

    copies = 400
    scratch = [
        pltpu.SemaphoreType.DMA((copies,)), pltpu.SemaphoreType.DMA((copies,)), pltpu.SemaphoreType.DMA((4 + NUM_LATE,)),
        vm(F32, 32, DC), vm(BF, 32, D), vm(BF, 16, 256),
        *[vm(BF, NX, PAIR, D) for _ in range(4)],
        vm(BF, NX, 32, D), vm(BF, NY, NZ, 96, D), vm(BF, NY, NZ, 2, 16, 256),
        vm(BF, DS, 256), vm(BF, DS, 256), vm(F32, DS, 1), vm(F32, IMG, 1), vm(F32, 16, 1, 192), vm(F32, 1, NB),
        vm(F32, 2, IMG, D), vm(BF, 2, IMG, D), vm(F32, 2, IMG, D), vm(F32, 2, DS, D), vm(BF, 2, DS, D),
        vm(BF, 4 * ROW, D), vm(BF, 4 * ROW, D), vm(F32, 4 * ROW, D), vm(F32, 4 * ROW, D),
        vm(BF, D, D), vm(BF, D, D), vm(BF, 4 * ROW, 2 * D), vm(BF, 4 * ROW, 2 * D),
        vm(BF, 2, 2 * ROW, D),
        vm(BF, NY, NZ, 96, D),
        vm(BF, 4, NX, 96, 256), vm(BF, 4, NX, 96, 256), vm(BF, 3, 48, TILE), vm(BF, 3, NX, 48, TILE),
        vm(BF, 3, NZ, 96, 256), vm(BF, 3, NZ, NY, 48, TILE), vm(BF, 3, NZ, 48, TILE), vm(BF, 3, NZ, 48, TILE),
        vm(BF, NZ, 48, 256), vm(BF, 7, 48, 256),
        vm(BF, 2, NY, NZ, 48, DS), vm(BF, NY, 48, DS), vm(BF, 2, 80, D),
        vm(BF, 2, 16, DC), vm(BF, 2, NX, 16, D),
        vm(BF, NX, 2, 16, 1792), vm(BF, NX, 2, 16, 1792),
        vm(F32, 512, DS), vm(BF, NY, NZ, 16, DS), vm(BF, 3, NZ, 16, DS), vm(BF, 7, 16, DS),
        vm(BF, NX, 2, 16, DS), vm(BF, NY, NZ, 16, DS),
        vm(BF, patch_rows, D), vm(BF, patch_rows, D), vm(F32, 12, DC), vm(F32, 12, DC), vm(F32, 12, DC), vm(F32, 12, DC),
        vm(F32, 12, 192), vm(F32, 12, 192),
        *[vm(F32, n, n) for n in (S, DS, DS, S, S, DS, DS, S)],
    ]
    in_vmem = pl.BlockSpec(memory_space=pltpu.VMEM)
    anywhere = pl.BlockSpec(memory_space=pl.ANY)
    rlay, rgrad, *rest = pl.pallas_call(
        fused,
        out_shape=shapes(outs),
        in_specs=[pl.BlockSpec(memory_space=pltpu.SMEM)]
        + [anywhere if i < 3 or i > 8 else in_vmem for i in range(1, len(args))],
        out_specs=[anywhere, anywhere] + [in_vmem] * (len(outs) - 2),
        scratch_shapes=scratch,
        compiler_params=pltpu.CompilerParams(
            collective_id=0, has_side_effects=True, vmem_limit_bytes=64 * 2**20
        ),
        name="fused",
    )(*args)
    handed = rest[:8] + rest[10:]
    handed_outs = outs[2:10] + outs[12:]
    own_outs = [((patch_rows, D), BF), ((patch_rows, D), F32)] + [((4, D), F32)] * 3 + [((NB,), F32)] * 3
    (
        gup, gdn, nup, ndn, rup, ldn, lup, rdn, gti, gto, nti, nto, lti, rti, lto, rto,
        layer, gimg, norm_grad, norm_second_new, norm_new, bias_grad, bias_second_new, bias_new,
    ) = pl.pallas_call(
        finish,
        out_shape=shapes(handed_outs + own_outs),
        in_specs=[in_vmem] * (8 + len(handed)),
        out_specs=[in_vmem] * (8 + len(handed)),
        compiler_params=pltpu.CompilerParams(vmem_limit_bytes=64 * 2**20),
        name="finish",
    )(rlay, rgrad, rest[8], rest[9], norm_params, norm_second, biases, bias_second, *handed)

    return (
        by_image(layer), by_image(gimg), gti.T, gto, gup.T, gdn, nti.T, nto, nup.T, ndn,
        lti, rti, lto, rto, lup, rup.T, ldn, rdn,
        norm_grad, norm_second_new, norm_new, bias_grad, bias_second_new, bias_new,
    )


def solution(mesh):
    both, dp, rest = ("dp", "mix"), "dp", P()
    in_specs = (
        P(dp, "mix", None), P(dp, "mix", None), P(dp), P(None, dp), P(dp, None), P(None, both), P(both, None),
        rest, rest, rest, rest, rest, rest,
        P(dp, "mix"), P(None, both), P(both, None), P(dp, "mix"),
        rest, rest, rest, rest, rest, P(None, both), P(both, None), rest, rest, rest,
    )
    out_specs = (
        P(dp, "mix", None), P(dp, "mix", None), P(None, dp), P(dp, None), P(None, both), P(both, None),
        P(None, dp), P(dp, None), P(None, both), P(both, None),
        rest, rest, rest, rest, P(dp, "mix"), P(None, both), P(both, None), P(dp, "mix"),
        rest, rest, rest, rest, rest, rest,
    )
    return jax.shard_map(on_device, mesh=mesh, in_specs=in_specs, out_specs=out_specs, check_vma=False)
```

```python
import jax
import jax.numpy as jnp
from jax import lax
from jax.experimental import pallas as pl
from jax.experimental.pallas import tpu as pltpu
from jax.sharding import PartitionSpec as P

MESH = pl.DeviceIdType.MESH
BF = jnp.bfloat16
F32 = jnp.float32
HIGH = lax.Precision.HIGHEST

D = 768
DC = 3072
DS = 384
S = 196
NX, NY, NZ = 4, 4, 8
EPS = 1e-06
PER_IMAGE = 1.0 / 512.0
PATCHES = 49
NUM_LATE = 16
PAIR = 112
IMG = 256
ROW = 208
HALF = D // 2
NB = 4420
TILE = 128
P0, P1, P2 = slice(0, 256), slice(256, 512), slice(512, 768)
FAR_FIRST = (4, 5, 3, 6, 2, 7, 1, 0)
NEAR, FAR = (0, 7, 1, 2), (6, 3, 5, 4)


def dot(left, right, left_dim=1, right_dim=0, precision=None):
    return lax.dot_general(
        left,
        right,
        (((left_dim,), (right_dim,)), ((), ())),
        preferred_element_type=F32,
        precision=precision,
    )


def pick(rows, cols, rule):
    row = lax.broadcasted_iota(jnp.int32, (rows, cols), 0)
    col = lax.broadcasted_iota(jnp.int32, (rows, cols), 1)
    return jnp.where(rule(row, col), 1.0, 0.0).astype(BF)


def ge(values, bound):
    return (values >= bound).astype(jnp.int32)


def gelu_and_slope(v):
    t = pl.reciprocal(1.0 + 0.23164188 * jnp.abs(v))
    e = jnp.exp(-0.5 * v * v)
    q = 0.5 * t * (
        0.254829592 + t * (-0.284496736 + t * (1.421413741 + t * (-1.453152027 + t * 1.061405429)))
    ) * e
    cdf = jnp.where(v >= 0, 1.0 - q, q)
    return v * cdf, cdf + v * e * 0.3989422804014327


def normalise(v):
    mean = jnp.mean(v, axis=-1, keepdims=True)
    centre = v - mean
    r = lax.rsqrt(jnp.mean(centre * centre, axis=-1, keepdims=True) + EPS)
    return centre * r, r


def normalise_back(xhat, r, dh, gain):
    dxh = dh * gain
    m1 = jnp.mean(dxh, axis=-1, keepdims=True)
    m2 = jnp.mean(dxh * xhat, axis=-1, keepdims=True)
    dv = r * (dxh - m1 - xhat * m2)
    return dv, jnp.sum(dh * xhat, axis=0, keepdims=True), jnp.sum(dh, axis=0, keepdims=True)


def fused(
    count, img_far, cot_far, tin, tout, wup, wdn, norm, bias, *refs
):
    late = refs[:NUM_LATE]
    (
        rlay, rgrad, o_gup, o_gdn, o_nup, o_ndn, o_rup, o_ldn, o_lup, o_rdn,
        o_norm, o_bias, o_gti, o_gto, o_nti, o_nto, o_lti, o_rti, o_lto, o_rto,
        ssem, rsem, lsem, stage, wst, tst, simg, scot, rimg, rcot,
        xw, W, tk, tokin, tokout, bti, bto, bup, brow, ximg, normed, mid, slope, act, n2, mb, br, dn,
        upc, dnc, actb, dpb, xbi, G, RAr, RAl, XA, YA, XB, YB, YC, XD, PZ, RZ,
        HQ, UJQ, UJP, qst, Qx, XEo, XEi, SM, SB, SY, SZ, S8, SF,
        img, cot, q_up, p_dn, old_r_up, old_l_dn, old_l_up, old_r_dn,
        pl_ti, pr_ti, pl_to, pr_to, ol_ti, or_ti, ol_to, or_to,
    ) = refs[NUM_LATE:]
    loaded = (
        q_up, p_dn, None, None, old_r_up, old_l_dn, old_l_up, old_r_dn,
        pl_ti, pr_ti, pl_to, pr_to, ol_ti, or_ti, ol_to, or_to,
    )
    dp = lax.axis_index("dp")
    x = lax.axis_index("mix")
    c = lax.rem(dp, 2)
    y = dp // (2 * NZ)
    z = lax.rem(dp // 2, NZ)

    def X(i):
        return lax.rem(x + i + NX, NX)

    def Y(i):
        return lax.rem(y + i + NY, NY)

    def Z(i):
        return lax.rem(z + i + NZ, NZ)

    def dev(xx, yy, zz, cc):
        return ((yy * NZ + zz) * 2 + cc, xx)

    to_x = [None] + [dev(X(i), y, z, c) for i in range(1, NX)]
    to_y = [None] + [dev(x, Y(i), z, c) for i in range(1, NY)]
    to_z = [None] + [dev(x, y, Z(i), c) for i in range(1, NZ)]
    sibling = dev(x, y, z, 1 - c)
    started = []
    used = [0]

    def put(src, dst, device):
        k = used[0]
        used[0] += 1
        copy = pltpu.make_async_remote_copy(
            src_ref=src, dst_ref=dst, send_sem=ssem.at[k], recv_sem=rsem.at[k],
            device_id=device, device_id_type=MESH,
        )
        copy.start()
        started.append(copy)
        return copy

    def arrived(copies):
        for copy in copies:
            copy.wait_recv()

    def settle(copies):
        for copy in copies:
            copy.wait_send()
        started[:] = [item for item in started if not any(item is copy for copy in copies)]

    def total(*parts):
        value = parts[0].astype(F32)
        for part in parts[1:]:
            value = value + part.astype(F32)
        return value

    barrier = pltpu.get_barrier_semaphore()
    to_same = [dev(X(i), y, z, cc) for i in range(NX) for cc in (c, 1 - c)][1:]
    peers = to_y[1:] + to_z[1:] + to_same
    for peer in peers:
        pl.semaphore_signal(barrier, inc=1, device_id=peer, device_id_type=MESH)

    get_img = pltpu.make_async_copy(img_far, img, lsem.at[1])
    get_img.start()
    get_cot = pltpu.make_async_copy(cot_far, cot, lsem.at[0])
    get_cot.start()
    loads = [None] * NUM_LATE
    for k in (0, 1, *range(4, NUM_LATE)):
        loads[k] = pltpu.make_async_copy(late[k], loaded[k], lsem.at[4 + k])
        loads[k].start()

    stage[:, 0 : 2 * D] = jnp.zeros((32, 2 * D), F32)
    stage[0:12, 0:D] = wup[...]
    stage[16:28, 0:D] = wdn[...]
    stage[0:6, D : D + S] = tin[...]
    stage[8:14, D : D + S] = tout[...]
    wst[...] = stage[:, 0:D].astype(BF)
    tst[...] = stage[0:16, D : D + 256].astype(BF)
    xw[x] = wst[...]
    tk[y, z, c] = tst[...]

    pl.semaphore_wait(barrier, len(peers))
    c_xw = [put(wst, xw.at[x], to_x[i]) for i in range(1, NX)]
    c_tz = [put(tk.at[y, z, c], tk.at[y, z, c], to_z[i]) for i in range(1, NZ)]

    def of_pairs(row, col):
        m = ge(row, PAIR) + ge(row, 2 * PAIR) + ge(row, 3 * PAIR)
        i = row - PAIR * m
        second = ge(i, PATCHES)
        return (col == (i - PATCHES * second) * 8 + 2 * m + second) & (i < 2 * PATCHES)

    chooser = pick(NX * PAIR, 8 * PATCHES, of_pairs)
    get_img.wait()
    simg[...] = dot(chooser, img[...]).astype(BF).reshape(NX, PAIR, D)
    c_img = [put(simg.at[X(i)], rimg.at[x], to_x[i]) for i in range(1, NX)]
    get_cot.wait()
    scot[...] = dot(chooser, cot[...]).astype(BF).reshape(NX, PAIR, D)
    c_cot = [put(scot.at[X(i)], rcot.at[x], to_x[i]) for i in range(1, NX)]

    arrived(c_xw)

    def of_shards(row, col):
        m, j = col >> 5, col & 31
        up = (j < 12) & (row == 12 * m + j)
        down = (j >= 16) & (j < 28) & (row == 32 + 12 * m + j)
        return up | down

    upc[0:96, :] = dot(pick(96, 128, of_shards), xw[...].reshape(128, D)).astype(BF)
    W[y, z, :, 0:512] = upc[0:96, 0:512]

    def rows_of(q):
        return pl.ds(pl.multiple_of(48 * (q // 2), 16), 48)

    def lanes_of(q, part):
        return pl.ds(pl.multiple_of(256 * part + TILE * lax.rem(q, 2), TILE), TILE)

    a_right, a_left, b_right, b_left, b_y = {}, {}, {}, {}, {}

    def a_send(step, d, right):
        if right:
            ref = W.at[Y(-d), Z(1 - step), :, P0]
            a_right[step, d] = put(ref, ref, to_z[1])
        else:
            ref = W.at[Y(-d), Z(step - 1), :, P0]
            a_left[step, d] = put(ref, ref, to_z[7])

    def b_send(step, right):
        if right:
            ref = W.at[y, Z(1 - step), :, P1]
            b_right[step] = put(ref, ref, to_z[1])
        else:
            ref = W.at[y, Z(step - 1), :, P1]
            b_left[step] = put(ref, ref, to_z[7])

    def b_spread(offset):
        ref = W.at[y, Z(offset), :, P1]
        b_y[offset] = [put(ref, ref, to_y[i]) for i in range(1, NY)]

    def c_ref(yy, zz):
        return W.at[yy, zz, rows_of(x), lanes_of(x, 2)]

    def c_part(k):
        return W.at[:, Z(k), rows_of(x), lanes_of(x, 2)]

    W[y, z, rows_of(x), lanes_of(x, 2)] = upc[rows_of(x), lanes_of(x, 2)]
    own_a = W.at[y, z, :, P0]
    def c_send_y(k):
        ref = c_ref(y, Z(k))
        c_y[k] = [put(ref, ref, to_y[i]) for i in range(1, NY)]

    c_z, c_y = {}, {}
    for i in (1, 7, 6, 2, 5, 3, 4):
        c_z[i] = put(c_ref(y, z), c_ref(y, z), to_z[i])
    b_send(1, True)
    b_send(1, False)
    c_ay = [None] + [put(own_a, own_a, to_y[i]) for i in range(1, NY)]
    c_send_y(0)
    a_send(1, 0, True)
    a_send(1, 0, False)
    b_spread(0)

    rimg[x] = simg[x]
    rcot[x] = scot[x]
    diagonal = pick(TILE, TILE, lambda row, col: row == col).astype(F32)
    brow[...] = bias[...].reshape(1, NB)

    def column(first):
        spread = jnp.broadcast_to(brow[:, first : first + TILE], (TILE, TILE))
        return jnp.sum(spread * diagonal, axis=1, keepdims=True)

    for j in range(3):
        bti[TILE * j : TILE * j + TILE, :] = column(TILE * j)
    for j in range(2):
        bto[TILE * j : TILE * j + TILE, :] = column(DS + TILE * j)
    for d in (1, 3, 2):
        c_ay[d].wait_recv()
        a_send(1, d, True)
        a_send(1, d, False)
    arrived(c_tz)
    c_ty = [put(tk.at[y, :, c], tk.at[y, :, c], to_y[i]) for i in range(1, NY)]
    c_x = {}

    def x_send(k):
        arrived(c_y[k])
        c_x[k] = [put(c_part(k), c_part(k), to_x[i]) for i in range(1, NX)]

    for k in NEAR[1:]:
        c_z[NZ - k].wait_recv()
        c_send_y(k)

    def gather_step(step):
        b_right[step].wait_recv()
        if step < 4:
            b_send(step + 1, True)
        b_spread(-step)
        if step < 4:
            b_left[step].wait_recv()
            if step < 3:
                b_send(step + 1, False)
            b_spread(step)
        if step < 4:
            for d in (0, 1, 3, 2):
                a_right[step, d].wait_recv()
                if step < 3 or d < 2:
                    a_send(step + 1, d, True)
                a_left[step, d].wait_recv()
                if step < 3 or d > 1:
                    a_send(step + 1, d, False)

    gather_step(1)
    for k in FAR:
        c_z[NZ - k].wait_recv()
        c_send_y(k)
    arrived(c_ty)
    c_tc = put(tk.at[:, :, c], tk.at[:, :, c], sibling)
    for k in NEAR:
        x_send(k)
    for zz in range(NZ):
        for cc in range(2):
            first = [DS + S + 48 * ((yy * NZ + zz) * 2 + cc) for yy in range(NY)]
            bup[2 * zz + cc] = jnp.concatenate([brow[:, f : f + 48] for f in first], axis=1)
    bias_down = brow[:, DS + S + DC : NB]

    c_tc.wait_recv()

    def of_group(row, col):
        group, i = col >> 4, col & 15
        first = (i < 6) & (row == 6 * group + i)
        second = (i >= 8) & (i < 14) & (row == 40 + 6 * group + i)
        return first | second

    chooser = pick(96, 128, of_group)
    for g in range(8):
        part = tk[g // 2, 4 * (g % 2) : 4 * (g % 2) + 4].reshape(128, 256)
        part = dot(chooser, part).astype(BF)
        tokin[48 * g : 48 * g + 48, :] = part[0:48]
        tokout[48 * g : 48 * g + 48, :] = part[48:96]

    arrived(c_img)
    arrived(c_cot)
    keep = [jnp.where(2 * x + b < count[0], 1.0, 0.0).astype(F32) for b in range(2)]
    own = c * (2 * ROW)

    def own_rows(b):
        return pl.ds(pl.multiple_of(own + b * ROW, 16), ROW)

    both = pl.ds(pl.multiple_of(own, 16), 2 * ROW)

    def of_images(row, col):
        b = ge(row, IMG)
        i = row - IMG * b
        part = ge(i, 49) + ge(i, 98) + ge(i, 147)
        return (col == 63 * part + 49 * b + i) & (i < S)

    chooser = pick(2 * IMG, NX * PAIR, of_images)
    ximg[...] = dot(chooser, rimg[...].reshape(NX * PAIR, D)).reshape(2, IMG, D)
    back = dot(chooser, rcot[...].reshape(NX * PAIR, D))
    for b in range(2):
        mb[own_rows(b), :] = (back[b * IMG : b * IMG + ROW] * keep[b]).astype(BF)
        xhat, _ = normalise(ximg[b])
        normed[b] = (xhat * norm[0:1, :] + norm[1:2, :]).astype(BF)
    c_mb = put(mb.at[both], mb.at[both], sibling)
    for k in FAR:
        x_send(k)
    gather_step(2)

    @pl.loop(0, 2)
    def _(b):
        pre = dot(tokin[...], normed[b]) + bti[...]
        value, grad = gelu_and_slope(pre)
        slope[b] = grad
        act[b] = value.astype(BF)
        mixed = dot(tokout[...], act[b], 0, 0) + bto[...]
        middle = ximg[b] + mixed.astype(BF).astype(F32)
        mid[b] = middle
        xhat, _ = normalise(middle[0:ROW])
        n2[own_rows(b), :] = (xhat * norm[2:3, :] + norm[3:4, :]).astype(BF)

    c_n2 = put(n2.at[both], n2.at[both], sibling)
    gather_step(3)
    gather_step(4)
    c_mb.wait_recv()
    c_n2.wait_recv()

    def channel_pass(half):
        offsets = FAR_FIRST[4 * half : 4 * half + 4]
        for j, k in enumerate(offsets):
            upc[192 * j : 192 * j + 192, :] = W[:, Z(k), 0:48, :].reshape(192, D)
            dnc[192 * j : 192 * j + 192, :] = W[:, Z(k), 48:96, :].reshape(192, D)
        row = jnp.concatenate([bup[2 * Z(k) + c] for k in offsets], axis=1)
        lanes = slice(half * D, half * D + D)

        @pl.loop(0, 2)
        def _(r):
            rows = pl.ds(pl.multiple_of(r * (2 * ROW), 16), 2 * ROW)
            pre = dot(n2[rows, :], upc[...], 1, 1) + row
            value, grad = gelu_and_slope(pre)
            low = value.astype(BF)
            actb[rows, lanes] = low
            part = dot(low, dnc[...])
            br[rows, :] = part if half == 1 else br[rows, :] + part
            low = (grad * dot(mb[rows, :], dnc[...], 1, 1)).astype(BF)
            dpb[rows, lanes] = low
            part = dot(low, upc[...])
            dn[rows, :] = part if half == 1 else dn[rows, :] + part

    ra, la, xb, yb, yc, xd, rz = {}, {}, {}, {}, {}, {}, {}

    def gradients(pair):
        lanes = slice(2 * 192 * pair, 2 * 192 * pair + 384)
        offsets = FAR_FIRST[2 * pair : 2 * pair + 2]
        for u, (left, right) in enumerate(((dpb, n2), (actb, mb))):
            grad = dot(left[:, lanes], right[...], 0, 0).astype(BF)
            for j, k in enumerate(offsets):
                part = grad[192 * j : 192 * j + 192].reshape(4, 48, D)
                G[:, Z(k), 48 * u : 48 * u + 48, :] = part
        for k in offsets:
            for i in range(1, NX):
                xb[k, i] = put(G.at[X(i), Z(k), :, P1], XB.at[i - 1, Z(k)], to_x[i])
                ref = G.at[:, Z(k), rows_of(Y(i)), lanes_of(Y(i), 2)]
                yb[k, i] = put(ref, YB.at[i - 1, Z(k)], to_y[i])

    def a_reduce(step, ws):
        for w in ws:
            first = 1 if w < 2 else 2
            if step >= first:
                ref = G.at[X(w), Z(5 - step), :, P0]
                if step > first:
                    ra[step - 1, w].wait_recv()
                    ref[...] = total(ref[...], RAr[step - 2, w]).astype(BF)
                ra[step, w] = put(ref, RAr.at[step - 1, w], to_z[1])
            first = 2 if w < 2 else 1
            if step >= first:
                ref = G.at[X(w), Z(step - 5), :, P0]
                if step > first:
                    la[step - 1, w].wait_recv()
                    ref[...] = total(ref[...], RAl[step - 2, w]).astype(BF)
                la[step, w] = put(ref, RAl.at[step - 1, w], to_z[7])

    def second(k):
        arrived([xb[k, i] for i in range(1, NX)])
        ref = G.at[x, Z(k), :, P1]
        ref[...] = total(ref[...], *[XB[i, Z(k)] for i in range(NX - 1)]).astype(BF)
        for i in range(1, NY):
            ref = G.at[x, Z(k), rows_of(Y(i)), lanes_of(Y(i), 1)]
            yc[k, i] = put(ref, YC.at[i - 1, Z(k)], to_y[i])
        arrived([yb[k, i] for i in range(1, NY)])
        ref = G.at[:, Z(k), rows_of(y), lanes_of(y, 2)]
        ref[...] = total(ref[...], *[YB[i, Z(k)] for i in range(NY - 1)]).astype(BF)
        for i in range(1, NX):
            ref = G.at[X(i), Z(k), rows_of(y), lanes_of(y, 2)]
            xd[k, i] = put(ref, XD.at[i - 1, Z(k)], to_x[i])

    def third(k):
        arrived([yc[k, i] for i in range(1, NY)])
        value = G[x, Z(k), rows_of(y), lanes_of(y, 1)]
        PZ[Z(k), :, 0:TILE] = total(value, *[YC[i, Z(k)] for i in range(NY - 1)]).astype(BF)
        arrived([xd[k, i] for i in range(1, NX)])
        value = G[x, Z(k), rows_of(y), lanes_of(y, 2)]
        PZ[Z(k), :, TILE : 2 * TILE] = total(value, *[XD[i, Z(k)] for i in range(NX - 1)]).astype(BF)
        if k > 0:
            rz[k] = put(PZ.at[Z(k)], RZ.at[k - 1], to_z[k])

    for offset in (0, -1, 1, 2):
        arrived(b_y[offset])
    for k in NEAR:
        arrived(c_x[k])
    loads[0].wait()
    loads[1].wait()
    stage[0:12, :] = q_up[...]
    stage[12:16, :] = jnp.zeros((4, DC), F32)
    stage[16:28, :] = p_dn[...]
    stage[28:32, :] = jnp.zeros((4, DC), F32)
    qst[0] = stage[0:16, :].astype(BF)
    qst[1] = stage[16:32, :].astype(BF)
    Qx[:, x] = qst[:, :, pl.ds(pl.multiple_of(x * D, D), D)]
    c_q = [
        put(qst.at[:, :, pl.ds(pl.multiple_of(X(i) * D, D), D)], Qx.at[:, x], to_x[i])
        for i in range(1, NX)
    ]
    channel_pass(1)
    gradients(2)
    gradients(3)
    for offset in (-2, 3, -3, -4):
        arrived(b_y[offset])
    for k in FAR:
        arrived(c_x[k])
    for d in (0, 1, 3, 2):
        (a_right if d < 2 else a_left)[4, d].wait_recv()
    channel_pass(0)

    other = pl.ds(pl.multiple_of((1 - c) * (2 * ROW), 16), 2 * ROW)
    upc[0 : 2 * ROW, :] = dn[other, :].astype(BF)
    c_dn = put(upc.at[0 : 2 * ROW], xbi.at[1], sibling)
    dnc[0 : 2 * ROW, :] = br[other, :].astype(BF)
    c_br = put(dnc.at[0 : 2 * ROW], xbi.at[0], sibling)

    gradients(0)
    a_reduce(1, range(4))
    gradients(1)
    for k in NEAR:
        second(k)

    ones = jnp.ones((8, 4 * ROW), BF)
    up_sums = dot(ones, dpb[...])[0:1]
    down_sums = dot(ones[:, 0 : 2 * ROW], mb[both, :])
    lob, dmx = actb, dpb
    lob[0 : 2 * IMG, 0:D] = jnp.zeros((2 * IMG, D), BF)
    dmx[0 : 2 * IMG, 0:D] = jnp.zeros((2 * IMG, D), BF)
    c_dn.wait_recv()
    c_br.wait_recv()
    gain_two = jnp.zeros((1, D), F32)
    shift_two = jnp.zeros((1, D), F32)
    for b in range(2):
        here = slice(b * ROW, b * ROW + ROW)
        branch = br[own_rows(b), :] + xbi[0, here, :].astype(F32) + bias_down
        lob[b * IMG : b * IMG + ROW, 0:D] = (keep[b] * (mid[b, 0:ROW] + branch)).astype(BF)
        dh = dn[own_rows(b), :] + xbi[1, here, :].astype(F32)
        xhat, r = normalise(mid[b, 0:ROW])
        dv, gain, shift = normalise_back(xhat, r, dh, norm[2:3, :])
        gain_two = gain_two + gain
        shift_two = shift_two + shift
        back = mb[own_rows(b), :].astype(F32) + dv
        mid[b, 0:ROW] = back
        dmx[b * IMG : b * IMG + ROW, 0:D] = back.astype(BF)
        a_reduce(2, (2 * b, 2 * b + 1))

    def of_out(row, col):
        m = ge(row, PAIR) + ge(row, 2 * PAIR) + ge(row, 3 * PAIR)
        i = row - PAIR * m
        second_one = ge(i, PATCHES)
        place = (IMG - PATCHES) * second_one + PATCHES * m + i
        return (col == place) & (i < 2 * PATCHES)

    out_chooser = pick(NX * PAIR, 2 * IMG, of_out)

    def to_patches(buffer, sent):
        settle(sent)
        buffer[...] = dot(out_chooser, lob[0 : 2 * IMG, 0:D]).astype(BF).reshape(NX, PAIR, D)

    a_reduce(3, (0, 1))
    to_patches(simg, c_img)
    own_out = [pltpu.make_async_copy(simg.at[x], rlay.at[x], lsem.at[2])]
    own_out[0].start()
    c_lay = [put(simg.at[X(i)], rlay.at[x], to_x[i]) for i in range(1, NX)]
    a_reduce(3, (2, 3))

    roots = [
        pltpu.make_async_copy(late[2], br.at[0:D], lsem.at[0]),
        pltpu.make_async_copy(late[3], dn.at[0:D], lsem.at[1]),
    ]
    for copy in roots:
        copy.start()
    gti = jnp.zeros((IMG, DS), F32)
    gto = jnp.zeros((IMG, DS), F32)
    sum_ti = jnp.zeros((8, DS), F32)
    sum_to = jnp.zeros((8, IMG), F32)
    gain_one = jnp.zeros((1, D), F32)
    shift_one = jnp.zeros((1, D), F32)
    ones = jnp.ones((8, D), BF)
    for b in range(2):
        dmixed = dmx[b * IMG : b * IMG + IMG, 0:D]
        dpre = (slope[b] * dot(tokout[...], dmixed)).astype(BF)
        gti = gti + dot(normed[b], dpre, 1, 1)
        gto = gto + dot(dmixed, act[b], 1, 1)
        sum_ti = sum_ti + dot(ones, dpre, 1, 1)
        sum_to = sum_to + dot(ones, dmixed, 1, 1)
        dnormed = dot(tokin[...], dpre, 0, 0).astype(BF).astype(F32)
        xhat, r = normalise(ximg[b, 0:ROW])
        dv, gain, shift = normalise_back(xhat, r, dnormed[0:ROW], norm[0:1, :])
        gain_one = gain_one + gain
        shift_one = shift_one + shift
        lob[b * IMG : b * IMG + ROW, 0:D] = (mid[b, 0:ROW] + dv).astype(BF)
        if b == 0:
            a_reduce(4, (0, 1))
            second(4)
            second(5)
            a_reduce(4, (2, 3))

    second(3)
    second(6)
    for w in range(NX):
        ra[4, w].wait_recv()
        la[4, w].wait_recv()
        ref = G.at[X(w), z, :, P0]
        ref[...] = total(ref[...], RAr[3, w], RAl[3, w]).astype(BF)
    c_ya = [
        put(G.at[:, z, rows_of(Y(i)), lanes_of(Y(i), 0)], YA.at[i - 1], to_y[i])
        for i in range(1, NY)
    ]
    for k in NEAR:
        third(k)

    SM[0:IMG, :] = gti
    SM[IMG : IMG + ROW, :] = gto[0:ROW]
    SM[IMG + ROW :, :] = jnp.zeros((IMG - ROW, DS), F32)
    for j, row in enumerate((gain_one, shift_one, gain_two, shift_two)):
        SM[208 + 2 * j : 209 + 2 * j, :] = row[:, 0:HALF]
        SM[209 + 2 * j : 210 + 2 * j, :] = row[:, HALF:D]
    SM[216:224, :] = sum_ti
    SM[224:232, 0:IMG] = sum_to
    SM[224:232, IMG:DS] = jnp.zeros((8, DS - IMG), F32)
    SM[232:240, :] = down_sums[:, 0:HALF]
    SM[240:248, :] = down_sums[:, HALF:D]
    for j, k in enumerate(FAR_FIRST):
        SM[pl.ds(464 + 8 * c + Z(k), 1), 0:192] = up_sums[:, 192 * j : 192 * j + 192]
    SB[...] = SM[...].reshape(NY, NZ, 16, DS).astype(BF)
    c_sy = [put(SB.at[Y(i)], SY.at[i - 1], to_y[i]) for i in range(1, NY)]

    for k in (4, 5):
        third(k)
    arrived(c_ya)
    ref = G.at[:, z, rows_of(y), lanes_of(y, 0)]
    ref[...] = total(ref[...], YA[0], YA[1], YA[2]).astype(BF)
    c_xa = [
        put(G.at[X(i), z, rows_of(y), lanes_of(y, 0)], XA.at[i - 1], to_x[i]) for i in range(1, NX)
    ]
    for k in (3, 6):
        third(k)
    arrived(c_sy)
    SB[y] = total(SB[y], SY[0], SY[1], SY[2]).astype(BF)
    c_sz = [put(SB.at[y, Z(i)], SZ.at[i - 1], to_z[i]) for i in range(1, NZ)]


    hz, hy, hs = {}, {}, {}

    def h_send(lanes):
        ref = HQ.at[c, y, z, :, lanes]
        for i in (1, 7, 2, 6, 3, 5, 4):
            hz[i] = hz.get(i, []) + [put(ref, ref, to_z[i])]

    arrived(c_xa)
    mean = total(G[x, z, rows_of(y), lanes_of(y, 0)], XA[0], XA[1], XA[2]) * PER_IMAGE
    HQ[c, y, z, :, 0:TILE] = mean.astype(BF)
    arrived(rz.values())
    mean = total(PZ[z], *[RZ[i] for i in range(NZ - 1)]) * PER_IMAGE
    HQ[c, y, z, :, TILE:] = mean.astype(BF)
    h_send(slice(0, DS))

    def h_spread(offset):
        ref = HQ.at[c, y, Z(offset)]
        hy[offset] = [put(ref, ref, to_y[i]) for i in range(1, NY)]

    def h_share(offset):
        arrived(hy[offset])
        ref = HQ.at[c, :, Z(offset)]
        hs[offset] = put(ref, ref, sibling)

    h_spread(0)
    to_patches(scot, c_cot)
    own_out.append(pltpu.make_async_copy(scot.at[x], rgrad.at[x], lsem.at[3]))
    own_out[1].start()
    c_grad = [put(scot.at[X(i)], rgrad.at[x], to_x[i]) for i in range(1, NX)]
    arrived(c_sz)
    S8[x, c] = total(SB[y, z], *[SZ[i] for i in range(NZ - 1)]).astype(BF)
    c_s8 = [put(S8.at[x, c], S8.at[x, c], device) for device in to_same]
    for i in (1, 7, 2, 6):
        arrived(hz[i])
        h_spread(-i)
    h_share(0)

    first_j = used[0]
    used[0] += 3

    def j_copy(i):
        return pltpu.make_async_remote_copy(
            src_ref=HQ.at[c, :, z], dst_ref=UJQ, send_sem=ssem.at[first_j + i - 1],
            recv_sem=rsem.at[first_j], device_id=to_x[i], device_id_type=MESH,
        )

    @pl.when(x == y)
    def _():
        for i in range(1, NX):
            j_copy(i).start()
        UJQ[...] = HQ[c, :, z]

    for i in (3, 5, 4):
        arrived(hz[i])
        h_spread(-i)
    arrived(c_s8)
    parts = [S8[xx, cc] for xx in range(NX) for cc in range(2)]
    SF[y, z] = (total(*parts) * PER_IMAGE).astype(BF)
    c_fz = [put(SF.at[y, z], SF.at[y, z], to_z[i]) for i in range(1, NZ)]
    for i in (1, 7, 2, 6):
        h_share(-i)
    @pl.when(x != y)
    def _():
        j_copy(1).wait_recv()

    def of_rows(row, col):
        m, i = row >> 4, row & 15
        return (col == 12 * m + i) & (i < 12)

    spread = pick(64, 48, of_rows)
    channels = pick(16, D, lambda row, col: (col == 12 * dp + row) & (row < 12))

    def unfold(dst, read, u):
        for t in range(2):
            value = read(2 * u + t)
            for part in range(3):
                lanes = slice(256 * part + TILE * t, 256 * part + TILE * t + TILE)
                dst[:, lanes] = value[..., TILE * part : TILE * part + TILE].reshape(-1, TILE)

    settle([c_dn, c_mb, c_n2])
    for u, out in enumerate((o_gup, o_gdn)):
        unfold(upc.at[0:48], lambda q: UJQ[q], u)
        UJP[u, 0:64] = dot(spread, upc[0:48, :]).astype(BF)
        UJP[u, 64:80] = channels
        out[...] = UJP[u, pl.ds(pl.multiple_of(16 * x, 16), 16), :][0:12].astype(F32)
    for i in (3, 5, 4):
        h_share(-i)
    arrived(c_fz)
    c_fy = [put(SF.at[y], SF.at[y], to_y[i]) for i in range(1, NY)]

    arrived([hs[offset] for offset in (0, -1, -7, -2, -6, -3, -5, -4)])
    arrived(c_q)
    c_xe = []
    for u in range(2):
        store = (n2, mb)[u]
        for zz in range(NZ):
            for cc in range(2):
                first = (2 * zz + cc) * 48
                unfold(store.at[first : first + 48], lambda q: HQ[cc, q, zz], u)
        quarter = store[0:D, :]
        right = dot(UJP[u], quarter, 1, 1)
        left = jnp.concatenate([Qx[u].reshape(64, D), right[64:80].astype(BF)], axis=0)
        left = dot(left, quarter)
        for m in range(NX):
            XEo[m, u, :, 0:D] = right[16 * m : 16 * m + 16].astype(BF)
            XEo[m, u, :, D : 2 * D] = left[16 * m : 16 * m + 16].astype(BF)
            XEo[m, u, :, 2 * D : 2 * D + 192] = left[64:80, 192 * m : 192 * m + 192].astype(BF)
            XEo[m, u, :, 2 * D + 192 : 2 * D + 256] = jnp.zeros((16, 64), BF)
        XEi[x, u] = XEo[x, u]
        c_xe.append([put(XEo.at[X(i), u], XEi.at[x, u], to_x[i]) for i in range(1, NX)])

    for copy in loads[4:]:
        copy.wait()

    arrived(c_fy)
    small = SF[...].reshape(512, DS)
    o_norm[...] = small[208:216].astype(F32)
    vector = small[208:256].astype(F32)
    ups = small[464:480].astype(F32)
    pieces = [vector[8:9], vector[16:17, 0:S]]
    for yy in range(NY):
        for zz in range(NZ):
            for cc in range(2):
                pieces.append(ups[8 * cc + zz : 8 * cc + zz + 1, 48 * yy : 48 * yy + 48])
    pieces += [vector[24:25], vector[32:33]]
    o_bias[...] = jnp.concatenate(pieces, axis=1)
    real = lax.broadcasted_iota(jnp.int32, (IMG, DS), 0) < S
    g_in = jnp.where(real, small[0:IMG].astype(F32), 0.0).astype(BF)
    g_out = jnp.where(real, small[IMG : 2 * IMG].astype(F32), 0.0).astype(BF)
    o_lti[...] = 0.5 * ol_ti[...] + 0.5 * dot(g_in, g_in, 1, 1)[0:S, 0:S]
    o_rti[...] = 0.5 * or_ti[...] + 0.5 * dot(g_in, g_in, 0, 0)
    o_lto[...] = 0.5 * ol_to[...] + 0.5 * dot(g_out, g_out, 0, 0)
    o_rto[...] = 0.5 * or_to[...] + 0.5 * dot(g_out, g_out, 1, 1)[0:S, 0:S]
    mine = pick(16, DS, lambda row, col: (col == 6 * dp + row) & (row < 6))
    o_gti[...] = dot(mine, g_in, 1, 1)[0:6, 0:S]
    o_gto[...] = dot(mine, g_out, 1, 1)[0:6, 0:S]
    mine = mine.astype(F32)
    step = dot(mine, pr_ti[...], 1, 1, HIGH)
    step = dot(step, g_in.astype(F32), 1, 1, HIGH)[:, 0:S]
    step = dot(step, pl_ti[...], 1, 1, HIGH)
    o_nti[...] = tin[...] - 0.5 * step[0:6]
    step = dot(mine, pl_to[...], 1, 0, HIGH)
    step = dot(step, g_out.astype(F32), 1, 1, HIGH)[:, 0:S]
    step = dot(step, pr_to[...], 1, 0, HIGH)
    o_nto[...] = tout[...] - 0.5 * step[0:6]

    for copy in roots:
        copy.wait()
    settle([c_br])
    upc[...] = br[0:D, :].astype(BF)
    dnc[...] = dn[0:D, :].astype(BF)
    for u, (o_stat, old_stat, o_side, old_side, o_new, weight, root, dim) in enumerate((
        (o_rup, old_r_up, o_lup, old_l_up, o_nup, wup, upc, 1),
        (o_ldn, old_l_dn, o_rdn, old_r_dn, o_ndn, wdn, dnc, 0),
    )):
        arrived(c_xe[u])
        for m in range(NX):
            lanes = slice(D * m, D * m + D)
            fresh = XEi[m, u, :, 0:D][0:12].astype(F32)
            o_stat[:, lanes] = 0.5 * old_stat[:, lanes] + 0.5 * fresh
        side = total(*[XEi[m, u, :, 2 * D : 2 * D + 192] for m in range(NX)])
        o_side[...] = 0.5 * old_side[...] + 0.5 * side[0:12]
        step = total(*[XEi[m, u, :, D : 2 * D] for m in range(NX)])
        high = step.astype(BF)
        step = jnp.concatenate([high, (step - high.astype(F32)).astype(BF)], axis=0)
        step = dot(step, root[...], 1, dim)
        o_new[...] = weight[...] - 0.5 * (step[0:12] + step[16:28])

    arrived(c_lay)
    arrived(c_grad)
    for copy in own_out:
        copy.wait()
    settle(list(started))

    @pl.when(x == y)
    def _():
        for i in range(1, NX):
            j_copy(i).wait_send()


def finish(
    rlay, rgrad, grads, bias_grad, norm, second, bias, bias_second, *refs
):
    handed = (len(refs) - 8) // 2
    sources, outs = refs[:handed], refs[handed:]
    o_layer, o_gimg, o_grad, o_second, o_norm, o_bias_grad, o_bias_second, o_bias = outs[handed:]
    for src, dst in zip(sources, outs):
        dst[...] = src[...]

    def of_patch(row, col):
        image = row & 7
        pair, second_one = image >> 1, image & 1
        return col == PAIR * pair + PATCHES * second_one + (row >> 3)

    chooser = pick(8 * PATCHES, NX * PAIR, of_patch)
    o_layer[...] = dot(chooser, rlay[...].reshape(NX * PAIR, D)).astype(BF)
    o_gimg[...] = dot(chooser, rgrad[...].reshape(NX * PAIR, D))
    for j in range(4):
        row = slice(j, j + 1)
        grad = jnp.concatenate([grads[2 * j : 2 * j + 1, :], grads[2 * j + 1 : 2 * j + 2, :]], axis=1)
        fresh = 0.5 * second[row, :] + 0.5 * grad * grad
        o_grad[row, :] = grad
        o_second[row, :] = fresh
        o_norm[row, :] = norm[row, :] - 0.5 * grad * lax.rsqrt(fresh + 1e-08)
    grad = bias_grad[...].reshape(NB)
    fresh = 0.5 * bias_second[...] + 0.5 * grad * grad
    o_bias_grad[...] = grad
    o_bias_second[...] = fresh
    o_bias[...] = bias[...] - 0.5 * grad * lax.rsqrt(fresh + 1e-08)


def on_device(
    images, cotangent, image_counts, w_tok_in, w_tok_out, w_up, w_down, norm_params, biases,
    left_tok_in, right_tok_in, left_tok_out, right_tok_out, left_up, right_up, left_down, right_down,
    root_left_tok_in, root_right_tok_in, root_left_tok_out, root_right_tok_out,
    root_left_up, root_right_up, root_left_down, root_right_down, norm_second, bias_second,
):
    patch_rows = 8 * PATCHES

    def by_patch(v):
        return v.transpose(1, 0, 2).reshape(patch_rows, D)

    def by_image(v):
        return v.reshape(PATCHES, 8, D).transpose(1, 0, 2)

    args = (
        image_counts, by_patch(images), by_patch(cotangent), w_tok_in.T, w_tok_out, w_up.T, w_down,
        norm_params, biases,
        root_right_up.T, root_left_down, root_left_up, root_right_down,
        right_up.T, left_down, left_up, right_down,
        root_left_tok_in, root_right_tok_in, root_left_tok_out, root_right_tok_out,
        left_tok_in, right_tok_in, left_tok_out, right_tok_out,
    )
    outs = [
        ((NX, PAIR, D), BF), ((NX, PAIR, D), BF), ((12, D), F32), ((12, D), F32), ((12, D), F32),
        ((12, D), F32), ((12, DC), F32), ((12, DC), F32), ((12, 192), F32), ((12, 192), F32),
        ((8, DS), F32), ((1, NB), F32), ((6, S), F32), ((6, S), F32), ((6, S), F32), ((6, S), F32),
        ((S, S), F32), ((DS, DS), F32), ((DS, DS), F32), ((S, S), F32),
    ]

    def shapes(items):
        return [jax.ShapeDtypeStruct(shape, dtype) for shape, dtype in items]

    def vm(dtype, *shape):
        return pltpu.VMEM(shape, dtype)

    copies = 400
    scratch = [
        pltpu.SemaphoreType.DMA((copies,)), pltpu.SemaphoreType.DMA((copies,)), pltpu.SemaphoreType.DMA((4 + NUM_LATE,)),
        vm(F32, 32, DC), vm(BF, 32, D), vm(BF, 16, 256),
        *[vm(BF, NX, PAIR, D) for _ in range(4)],
        vm(BF, NX, 32, D), vm(BF, NY, NZ, 96, D), vm(BF, NY, NZ, 2, 16, 256),
        vm(BF, DS, 256), vm(BF, DS, 256), vm(F32, DS, 1), vm(F32, IMG, 1), vm(F32, 16, 1, 192), vm(F32, 1, NB),
        vm(F32, 2, IMG, D), vm(BF, 2, IMG, D), vm(F32, 2, IMG, D), vm(F32, 2, DS, D), vm(BF, 2, DS, D),
        vm(BF, 4 * ROW, D), vm(BF, 4 * ROW, D), vm(F32, 4 * ROW, D), vm(F32, 4 * ROW, D),
        vm(BF, D, D), vm(BF, D, D), vm(BF, 4 * ROW, 2 * D), vm(BF, 4 * ROW, 2 * D),
        vm(BF, 2, 2 * ROW, D),
        vm(BF, NY, NZ, 96, D),
        vm(BF, 4, NX, 96, 256), vm(BF, 4, NX, 96, 256), vm(BF, 3, 48, TILE), vm(BF, 3, NX, 48, TILE),
        vm(BF, 3, NZ, 96, 256), vm(BF, 3, NZ, NY, 48, TILE), vm(BF, 3, NZ, 48, TILE), vm(BF, 3, NZ, 48, TILE),
        vm(BF, NZ, 48, 256), vm(BF, 7, 48, 256),
        vm(BF, 2, NY, NZ, 48, DS), vm(BF, NY, 48, DS), vm(BF, 2, 80, D),
        vm(BF, 2, 16, DC), vm(BF, 2, NX, 16, D),
        vm(BF, NX, 2, 16, 1792), vm(BF, NX, 2, 16, 1792),
        vm(F32, 512, DS), vm(BF, NY, NZ, 16, DS), vm(BF, 3, NZ, 16, DS), vm(BF, 7, 16, DS),
        vm(BF, NX, 2, 16, DS), vm(BF, NY, NZ, 16, DS),
        vm(BF, patch_rows, D), vm(BF, patch_rows, D), vm(F32, 12, DC), vm(F32, 12, DC), vm(F32, 12, DC), vm(F32, 12, DC),
        vm(F32, 12, 192), vm(F32, 12, 192),
        *[vm(F32, n, n) for n in (S, DS, DS, S, S, DS, DS, S)],
    ]
    in_vmem = pl.BlockSpec(memory_space=pltpu.VMEM)
    anywhere = pl.BlockSpec(memory_space=pl.ANY)
    rlay, rgrad, *rest = pl.pallas_call(
        fused,
        out_shape=shapes(outs),
        in_specs=[pl.BlockSpec(memory_space=pltpu.SMEM)]
        + [anywhere if i < 3 or i > 8 else in_vmem for i in range(1, len(args))],
        out_specs=[anywhere, anywhere] + [in_vmem] * (len(outs) - 2),
        scratch_shapes=scratch,
        compiler_params=pltpu.CompilerParams(
            collective_id=0, has_side_effects=True, vmem_limit_bytes=64 * 2**20
        ),
        name="fused",
    )(*args)
    handed = rest[:8] + rest[10:]
    handed_outs = outs[2:10] + outs[12:]
    own_outs = [((patch_rows, D), BF), ((patch_rows, D), F32)] + [((4, D), F32)] * 3 + [((NB,), F32)] * 3
    (
        gup, gdn, nup, ndn, rup, ldn, lup, rdn, gti, gto, nti, nto, lti, rti, lto, rto,
        layer, gimg, norm_grad, norm_second_new, norm_new, bias_grad, bias_second_new, bias_new,
    ) = pl.pallas_call(
        finish,
        out_shape=shapes(handed_outs + own_outs),
        in_specs=[in_vmem] * (8 + len(handed)),
        out_specs=[in_vmem] * (8 + len(handed)),
        compiler_params=pltpu.CompilerParams(vmem_limit_bytes=64 * 2**20),
        name="finish",
    )(rlay, rgrad, rest[8], rest[9], norm_params, norm_second, biases, bias_second, *handed)

    return (
        by_image(layer), by_image(gimg), gti.T, gto, gup.T, gdn, nti.T, nto, nup.T, ndn,
        lti, rti, lto, rto, lup, rup.T, ldn, rdn,
        norm_grad, norm_second_new, norm_new, bias_grad, bias_second_new, bias_new,
    )


def solution(mesh):
    both, dp, rest = ("dp", "mix"), "dp", P()
    in_specs = (
        P(dp, "mix", None), P(dp, "mix", None), P(dp), P(None, dp), P(dp, None), P(None, both), P(both, None),
        rest, rest, rest, rest, rest, rest,
        P(dp, "mix"), P(None, both), P(both, None), P(dp, "mix"),
        rest, rest, rest, rest, rest, P(None, both), P(both, None), rest, rest, rest,
    )
    out_specs = (
        P(dp, "mix", None), P(dp, "mix", None), P(None, dp), P(dp, None), P(None, both), P(both, None),
        P(None, dp), P(dp, None), P(None, both), P(both, None),
        rest, rest, rest, rest, P(dp, "mix"), P(None, both), P(both, None), P(dp, "mix"),
        rest, rest, rest, rest, rest, rest,
    )
    return jax.shard_map(on_device, mesh=mesh, in_specs=in_specs, out_specs=out_specs, check_vma=False)
```
